32 devices in a mesh: clip: 4 (over z), frame: 8 (over y, x, core).
Axes of the slice: x: 2, y: 2, z: 4, core: 2. Of those that a mesh axis runs over, the one named last changes fastest.
Arguments:
- tokens: bfloat16 [4, 8, 196, 1024], P('clip', 'frame'), may hold values from -6 to 6
- counts: int32 [4], P('clip'), may hold values from 1 to 8, 16 in all
- norm_gain: float32 [1024], replicated, may hold values from 0.1 to 1.9
- input_weights: bfloat16 [1024, 3072], P('frame', 'clip'), may hold values from -5 to 5
- output_weights: bfloat16 [1024, 1024], P('frame', 'clip'), may hold values from -0.1875 to 0.1875
- cotangent: bfloat16 [4, 8, 196, 1024], P('clip', 'frame'), may hold values from -6 to 6
Outputs:
- result: bfloat16 [4, 8, 196, 1024], P('clip', 'frame')
- grad_tokens: bfloat16 [4, 8, 196, 1024], P('clip', 'frame')
The draws below stay inside these ranges and needn't reach their ends.
Inputs may be any that keep to these rules, and one draw needn't show every extreme that they name: The 4 counts sum to 16.
All inputs are finite; a program needn't handle non-finite values. No bound on the sum of `counts` on one device may be relied on, other than what follows from the above.
Results may differ from the reference program's by a relative error of at most 0.006.
Values may be sent and summed in bfloat16 or wider, within the bound.
No kernel may reach another device: no remote copies, remote signals or barrier semaphores. Data moves between devices by JAX's collectives and lax.ppermute only.
A program may use at most 64 MiB of HBM per device.

```python
import math
import jax
import jax.numpy as jnp
import numpy as np
from jax import lax

D = 1024
P_SIZE = 196
DH = 64
FRAMES = 8
CLIPS = 4
TOTAL = 16


def draw_input_weights(key, part):
    normal_key = jax.random.fold_in(key, 0)
    weights = jax.random.truncated_normal(normal_key, -4.0, 4.0, (D, 3 * D), jnp.float32) * D ** (-0.5)
    return weights.astype(jnp.bfloat16)


def block_levels(own_key, dims, cuts, least, largest):
    loudness = 1.0
    for dim, parts in cuts:
        draws = jax.random.uniform(jax.random.fold_in(jax.random.fold_in(own_key, 6), dim), (parts,), jnp.float32, least / len(cuts), largest / len(cuts))
        loudness = loudness * jnp.repeat(jnp.exp(draws), dims[dim] // parts).reshape((-1,) + (1,) * (len(dims) - 1 - dim))
    return loudness


def split_up(count, total, reach, lean):
    loads = [(1 << 20) // math.isqrt(standing ** lean) + 1 for standing in range(2, count + 1)]
    surplus, holding = total - reach - (count - 1), [1] * (count - 1)
    while surplus > 0:
        movable = [i for i in range(count - 1) if holding[i] < reach]
        mass, remaining = sum([loads[i] for i in movable]), surplus
        for i in movable:
            extra = min(reach - holding[i], max(1, remaining * loads[i] // mass), surplus)
            holding[i] = holding[i] + extra
            surplus = surplus - extra
    return np.array([reach] + holding)


def uneven_parts(stream_key, number_of, total, most, lean):
    if number_of == 2:
        one = jax.random.randint(stream_key, (), max(1, total - most), min(most, total - 1) + 1)
        return jnp.stack([one, total - one])
    sizes = jnp.asarray(split_up(number_of, total, most, lean), jnp.int32)
    twos = (number_of - 1) // 2
    donor, sink = sizes[1:1 + 2 * twos:2], sizes[2:2 + 2 * twos:2]
    room = jnp.minimum(donor - 1, most - sink)
    shifted = jax.random.randint(jax.random.fold_in(stream_key, 1), (twos,), 0, 1 << 20) % (room + 1)
    sizes = sizes.at[1:1 + 2 * twos:2].set(donor - shifted).at[2:2 + 2 * twos:2].set(sink + shifted)
    return sizes[jax.random.permutation(jax.random.fold_in(stream_key, 2), number_of)]


def bell_draw(key, dims, spread, reach, shards=(), held_as=jnp.bfloat16):
    entries = jax.random.normal(key, dims, jnp.float32) * spread
    if len(shards) > 0:
        entries = block_levels(key, dims, shards, -0.22, 0.18) * entries
    return jnp.clip(entries, min=-reach, max=reach).astype(held_as)


def setup_inputs(seed: int = 0) -> dict:
    seeds = jax.random.split(jax.random.key(seed), 7)
    tokens = bell_draw(seeds[0], (CLIPS, FRAMES, P_SIZE, D), 1.0, 6.0, ((0, 4), (1, 8)))
    counts = uneven_parts(seeds[1], CLIPS, TOTAL, FRAMES, 2).astype(jnp.int32)
    norm_gain = jnp.clip(1.0 + 0.18 * jax.random.normal(seeds[2], (D,), jnp.float32), 0.1, 1.9)
    input_weights = draw_input_weights(jax.random.fold_in(seeds[6], 71), 0)
    output_weights = bell_draw(seeds[4], (D, D), D ** -0.5, 0.1875, ((0, 8), (1, 4)))
    cotangent = bell_draw(seeds[5], (CLIPS, FRAMES, P_SIZE, D), 1.0, 6.0, ((0, 4), (1, 8)))
    return {"tokens": tokens, "counts": counts, "norm_gain": norm_gain, "input_weights": input_weights, "output_weights": output_weights, "cotangent": cotangent}


EPSILON = 1e-06
NEGATIVE = -1e+30

def layer_norm(wide_precision_rows, norm_gain):
    average = lax.optimization_barrier(jnp.mean(wide_precision_rows, axis=-1, keepdims=True))
    centred = wide_precision_rows - average
    variance = lax.optimization_barrier(jnp.mean(centred * centred, axis=-1, keepdims=True))
    return centred * lax.rsqrt(variance + EPSILON) * norm_gain

def clip_pass(tokens, cotangent, length, norm_gain, input_weights, output_weights):
    frames_total, patches, embedding_width = tokens.shape
    heads = embedding_width // DH
    score_scale = DH ** (-0.5)
    position = jnp.arange(frames_total)
    occupied_frame_slots = position < length
    frame_presence_mask = occupied_frame_slots.astype(jnp.float32)[:, None, None]
    wide_precision_rows = tokens.astype(jnp.float32)
    normed = layer_norm(wide_precision_rows, norm_gain).astype(jnp.bfloat16).reshape(-1, embedding_width)
    projected = jnp.dot(normed, input_weights, preferred_element_type=jnp.float32).astype(jnp.bfloat16)
    projected = projected.reshape(frames_total, patches, 3, heads, DH)
    query = projected[:, :, 0].astype(jnp.float32)
    keys_all = projected[:, :, 1].astype(jnp.float32)
    values = projected[:, :, 2].astype(jnp.float32)
    scores = jnp.einsum('tphd,uphd->phtu', query, keys_all) * score_scale
    scores = jnp.where(occupied_frame_slots[None, None, None, :], scores, NEGATIVE)
    highest = lax.optimization_barrier(jnp.max(scores, axis=-1, keepdims=True))
    expanded = jnp.exp(scores - highest)
    probabilities = expanded / lax.optimization_barrier(jnp.sum(expanded, axis=-1, keepdims=True))
    probs_low = lax.optimization_barrier(probabilities.astype(jnp.bfloat16)).astype(jnp.float32)
    attended = jnp.einsum('phtu,uphd->tphd', probs_low, values).astype(jnp.bfloat16)
    temporal_mixed_rows = jnp.dot(attended.reshape(-1, embedding_width), output_weights, preferred_element_type=jnp.float32)
    temporal_mixed_rows = temporal_mixed_rows.reshape(wide_precision_rows.shape)
    result = (wide_precision_rows + frame_presence_mask * temporal_mixed_rows).astype(jnp.bfloat16)
    output_gradient = (cotangent.astype(jnp.float32) * frame_presence_mask).astype(jnp.bfloat16).reshape(-1, embedding_width)
    grad_attended = jnp.dot(output_gradient, output_weights.T, preferred_element_type=jnp.float32).astype(jnp.bfloat16)
    grad_attended = grad_attended.reshape(frames_total, patches, heads, DH).astype(jnp.float32)
    attended_float = attended.astype(jnp.float32)
    grad_probs = jnp.einsum('tphd,uphd->phtu', grad_attended, values)
    row_delta = jnp.einsum('tphd,tphd->pht', grad_attended, attended_float)
    grad_scores = (probabilities * (grad_probs - row_delta[..., None])).astype(jnp.bfloat16)
    grad_scores = lax.optimization_barrier(grad_scores).astype(jnp.float32)
    grad_query = (jnp.einsum('phtu,uphd->tphd', grad_scores, keys_all) * score_scale).astype(jnp.bfloat16)
    grad_keys = (jnp.einsum('phtu,tphd->uphd', grad_scores, query) * score_scale).astype(jnp.bfloat16)
    grad_values = jnp.einsum('phtu,tphd->uphd', probs_low, grad_attended).astype(jnp.bfloat16)
    stacked = jnp.stack([grad_query, grad_keys, grad_values], axis=2).reshape(-1, 3 * embedding_width)
    grad_normed = jnp.dot(stacked, input_weights.T, preferred_element_type=jnp.float32).reshape(wide_precision_rows.shape)
    pullback = jax.vjp(lambda source: layer_norm(source, norm_gain), wide_precision_rows)[1]
    grad_rows = pullback(grad_normed)[0]
    grad_tokens = (cotangent.astype(jnp.float32) + grad_rows).astype(jnp.bfloat16)
    return (result, grad_tokens)

def reference(tokens, counts, norm_gain, input_weights, output_weights, cotangent):

    def one_clip(operands):
        return clip_pass(operands[0], operands[2], operands[1], norm_gain, input_weights, output_weights)
    result, grad_tokens = lax.map(one_clip, (tokens, counts, cotangent))
    return (result, grad_tokens)
```

```python
import functools

import jax
import jax.numpy as jnp
from jax import lax
from jax.experimental import pallas as pl
from jax.experimental.pallas import tpu as pltpu
from jax.sharding import PartitionSpec as P

DH = 64
PAIR = 2 * DH
SUB = 16
EPSILON = 1e-06
NEGATIVE = -1e30
NN = (((1,), (0,)), ((), ()))
NT = (((1,), (1,)), ((), ()))
TN = (((0,), (0,)), ((), ()))


def dot(a, b, dims):
    return lax.dot_general(a, b, dims, preferred_element_type=jnp.float32)


def attention_pair(q, k, v, ga, mask, low_lanes):
    zero = jnp.zeros_like(q)

    def apart(block):
        return jnp.concatenate(
            [jnp.where(low_lanes, block, zero), jnp.where(low_lanes, zero, block)], axis=0
        )

    rows = q.shape[0]
    q_two, k_two, v_two, ga_two = apart(q), apart(k), apart(v), apart(ga)
    scores = dot(q_two, k, NT) * DH ** (-0.5)
    grad_probs = dot(ga_two, v, NT)
    scores = jnp.where(mask, scores, NEGATIVE)
    highest = jnp.max(scores, axis=-1, keepdims=True)
    expanded = jnp.exp(scores - highest)
    probs = expanded * (1.0 / jnp.sum(expanded, axis=-1, keepdims=True))
    probs_low = probs.astype(jnp.bfloat16)
    beside = jnp.concatenate([probs_low[:rows], probs_low[rows:]], axis=1)
    attended = dot(beside, v_two, NN).astype(jnp.bfloat16)
    grad_values = dot(probs_low, ga_two, TN).astype(jnp.bfloat16)
    both = attended.astype(jnp.float32)
    delta = jnp.sum(
        ga_two.astype(jnp.float32) * jnp.concatenate([both, both], axis=0), axis=-1, keepdims=True
    )
    grad_scores = (probs * (grad_probs - delta)).astype(jnp.bfloat16)
    beside = jnp.concatenate([grad_scores[:rows], grad_scores[rows:]], axis=1)
    grad_query = (dot(beside, k_two, NN) * DH ** (-0.5)).astype(jnp.bfloat16)
    grad_keys = (dot(grad_scores, q_two, TN) * DH ** (-0.5)).astype(jnp.bfloat16)
    return attended, grad_query, grad_keys, grad_values


def block_kernel(
    pieces, frames, patches, width,
    counts_ref, gain_ref, tokens_ref, cot_ref, *rest,
):
    weight_refs = rest[: len(rest) - 11]
    result_ref, grad_ref, w_in, w_out, normed, proj, ga, att, gproj, stats, sems = rest[-11:]
    groups = patches // SUB
    rows = frames * SUB
    total = groups * rows
    count = counts_ref[0]

    copies = []
    for which, (target, found) in enumerate(zip((w_in, w_out), pieces)):
        mine = []
        for ref, index, lanes, row, column in found:
            source = weight_refs[ref].at[index] if index is not None else weight_refs[ref]
            depth = source.shape[0]
            mine.append(
                pltpu.make_async_copy(
                    source.at[:, pl.ds(*lanes)],
                    target.at[pl.ds(row, depth), pl.ds(column, lanes[1])],
                    sems.at[which],
                )
            )
        copies.append(mine)
    for mine in copies:
        for copy in mine:
            copy.start()

    live = (lax.broadcasted_iota(jnp.int32, (rows, 1), 0) // SUB < count).astype(jnp.float32)
    gain = gain_ref[...]

    def load(ref, group):
        start = pl.multiple_of(group * SUB, SUB)
        return ref[:, pl.ds(start, SUB), :].reshape(rows, width)

    def store(ref, group, value):
        start = pl.multiple_of(group * SUB, SUB)
        ref[:, pl.ds(start, SUB), :] = value.reshape(frames, SUB, width)

    for group in range(groups):
        here = pl.ds(group * rows, rows)
        wide = load(tokens_ref, group).astype(jnp.float32)
        average = jnp.mean(wide, axis=-1, keepdims=True)
        centred = wide - average
        variance = jnp.mean(centred * centred, axis=-1, keepdims=True)
        scale = lax.rsqrt(variance + EPSILON)
        normed[here, :] = (centred * scale * gain).astype(jnp.bfloat16)
        stats[here, 0:1] = average
        stats[here, 1:2] = scale

    for copy in copies[0]:
        copy.wait()

    step = 512

    @pl.loop(0, 3 * width // step)
    def _(j):
        columns = pl.ds(pl.multiple_of(j * step, step), step)
        proj[:, columns] = dot(normed[...], w_in[:, columns], NN).astype(jnp.bfloat16)

    for copy in copies[1]:
        copy.wait()

    for group in range(groups):
        here = pl.ds(group * rows, rows)
        normed[here, :] = (load(cot_ref, group).astype(jnp.float32) * live).astype(jnp.bfloat16)

    @pl.loop(0, width // step)
    def _(j):
        columns = pl.ds(pl.multiple_of(j * step, step), step)
        ga[:, columns] = dot(normed[...], w_out[columns, :], NT).astype(jnp.bfloat16)

    row = lax.broadcasted_iota(jnp.int32, (2 * rows, rows), 0)
    key = lax.broadcasted_iota(jnp.int32, (2 * rows, rows), 1)
    mask = (row % SUB == key % SUB) & (key // SUB < count)
    low_lanes = lax.broadcasted_iota(jnp.int32, (rows, PAIR), 1) < DH
    unroll = 4 if rows <= 128 else 1

    for group in range(groups):
        here = pl.ds(group * rows, rows)

        @pl.loop(0, width // (PAIR * unroll))
        def _(step_index):
            for inner in range(unroll):
                pair = step_index * unroll + inner

                def lanes(part):
                    return pl.ds(pl.multiple_of(part * width + pair * PAIR, PAIR), PAIR)

                attended, grad_query, grad_keys, grad_values = attention_pair(
                    proj[here, lanes(0)],
                    proj[here, lanes(1)],
                    proj[here, lanes(2)],
                    ga[here, lanes(0)],
                    mask,
                    low_lanes,
                )
                att[here, lanes(0)] = attended
                gproj[here, lanes(0)] = grad_query
                gproj[here, lanes(1)] = grad_keys
                gproj[here, lanes(2)] = grad_values

    for group in range(groups):
        here = pl.ds(group * rows, rows)
        mixed = dot(att[here, :], w_out[...], NN)
        store(
            result_ref,
            group,
            (load(tokens_ref, group).astype(jnp.float32) + live * mixed).astype(jnp.bfloat16),
        )

    for group in range(groups):
        here = pl.ds(group * rows, rows)
        grad = dot(gproj[here, :], w_in[...], NT) * gain
        scale = stats[here, 1:2]
        hat = (load(tokens_ref, group).astype(jnp.float32) - stats[here, 0:1]) * scale
        grad_rows = scale * (
            grad
            - jnp.mean(grad, axis=-1, keepdims=True)
            - hat * jnp.mean(grad * hat, axis=-1, keepdims=True)
        )
        store(
            grad_ref,
            group,
            (load(cot_ref, group).astype(jnp.float32) + grad_rows).astype(jnp.bfloat16),
        )


def run_block(counts, gain, tokens, cot, weights, pieces):
    frames, patches, width = tokens.shape
    total = frames * patches
    vmem = pl.BlockSpec(memory_space=pltpu.VMEM)
    anywhere = pl.BlockSpec(memory_space=pl.ANY)
    out = jax.ShapeDtypeStruct(tokens.shape, jnp.bfloat16)
    return pl.pallas_call(
        functools.partial(block_kernel, pieces, frames, patches, width),
        out_shape=(out, out),
        in_specs=[pl.BlockSpec(memory_space=pltpu.SMEM), vmem, vmem, vmem]
        + [anywhere] * len(weights),
        out_specs=(vmem, vmem),
        scratch_shapes=[
            pltpu.VMEM((width, 3 * width), jnp.bfloat16),
            pltpu.VMEM((width, width), jnp.bfloat16),
            pltpu.VMEM((total, width), jnp.bfloat16),
            pltpu.VMEM((total, 3 * width), jnp.bfloat16),
            pltpu.VMEM((total, width), jnp.bfloat16),
            pltpu.VMEM((total, width), jnp.bfloat16),
            pltpu.VMEM((total, 3 * width), jnp.bfloat16),
            pltpu.VMEM((total, 128), jnp.float32),
            pltpu.SemaphoreType.DMA((2,)),
        ],
        compiler_params=pltpu.CompilerParams(vmem_limit_bytes=48 * 1024 * 1024),
        cost_estimate=pl.CostEstimate(
            flops=16 * total * width * width,
            bytes_accessed=8 * width * width + 8 * total * width,
            transcendentals=total * 2048,
        ),
        name="block",
    )(counts, gain, tokens, cot, *weights)


def gather_weights(input_weights, output_weights, clips, devices):
    depth, in_columns = input_weights.shape
    out_columns = output_weights.shape[1]
    if in_columns % 128 == 0 and out_columns % 128 == 0 and depth % 16 == 0:
        joined = jnp.concatenate([input_weights, output_weights], axis=1)
        whole = lax.all_gather(joined, ("clip", "frame"), axis=0)
        whole = whole.reshape(clips * devices, depth, in_columns + out_columns)
        pieces = ([], [])
        for c in range(clips):
            for f in range(devices):
                index = c * devices + f
                pieces[0].append((0, index, (0, in_columns), f * depth, c * in_columns))
                pieces[1].append((0, index, (in_columns, out_columns), f * depth, c * out_columns))
        return [whole], pieces
    both = []
    for weights in (input_weights, output_weights):
        columns = lax.all_gather(weights, "clip", axis=1, tiled=True)
        both.append(lax.all_gather(columns, "frame", axis=0, tiled=True))
    pieces = tuple([(i, None, (0, w.shape[1]), 0, 0)] for i, w in enumerate(both))
    return both, pieces


def per_device(clips, devices, tokens, counts, norm_gain, input_weights, output_weights, cotangent):
    _, slots, patches, width = tokens.shape
    weights, pieces = gather_weights(input_weights, output_weights, clips, devices)
    share = -(-patches // devices)
    share = -(-share // SUB) * SUB
    extra = devices * share - patches
    both = jnp.concatenate([tokens, cotangent], axis=0)
    both = jnp.pad(both, ((0, 0), (0, 0), (0, extra), (0, 0)))
    both = both.reshape(2, slots, devices, share, width)
    both = lax.all_to_all(both, "frame", split_axis=2, concat_axis=1, tiled=True)
    both = both.reshape(2, devices * slots, share, width)
    outs = run_block(counts, norm_gain.reshape(1, width), both[0], both[1], weights, pieces)
    back = jnp.stack(outs).reshape(2, devices * slots, 1, share, width)
    back = lax.all_to_all(back, "frame", split_axis=1, concat_axis=2, tiled=True)
    back = back.reshape(2, slots, devices * share, width)[:, :, :patches]
    return back[0][None], back[1][None]


def solution(mesh):
    in_specs = (
        P("clip", "frame", None, None),
        P("clip"),
        P(),
        P("frame", "clip"),
        P("frame", "clip"),
        P("clip", "frame", None, None),
    )
    out_specs = (P("clip", "frame", None, None), P("clip", "frame", None, None))
    body = functools.partial(per_device, mesh.shape["clip"], mesh.shape["frame"])
    return jax.shard_map(body, mesh=mesh, in_specs=in_specs, out_specs=out_specs, check_vma=False)
```

```python
import functools

import jax
import jax.numpy as jnp
from jax import lax
from jax.experimental import pallas as pl
from jax.experimental.pallas import tpu as pltpu
from jax.sharding import PartitionSpec as P

DH = 64
PAIR = 2 * DH
SUB = 16
EPSILON = 1e-06
NEGATIVE = -1e30
NN = (((1,), (0,)), ((), ()))
NT = (((1,), (1,)), ((), ()))
TN = (((0,), (0,)), ((), ()))


def dot(a, b, dims):
    return lax.dot_general(a, b, dims, preferred_element_type=jnp.float32)


def attention_pair(q, k, v, ga, mask, low_lanes):
    zero = jnp.zeros_like(q)

    def apart(block):
        return jnp.concatenate(
            [jnp.where(low_lanes, block, zero), jnp.where(low_lanes, zero, block)], axis=0
        )

    rows = q.shape[0]
    q_two, k_two, v_two, ga_two = apart(q), apart(k), apart(v), apart(ga)
    scores = dot(q_two, k, NT) * DH ** (-0.5)
    grad_probs = dot(ga_two, v, NT)
    scores = jnp.where(mask, scores, NEGATIVE)
    highest = jnp.max(scores, axis=-1, keepdims=True)
    expanded = jnp.exp(scores - highest)
    probs = expanded * (1.0 / jnp.sum(expanded, axis=-1, keepdims=True))
    probs_low = probs.astype(jnp.bfloat16)
    beside = jnp.concatenate([probs_low[:rows], probs_low[rows:]], axis=1)
    attended = dot(beside, v_two, NN).astype(jnp.bfloat16)
    grad_values = dot(probs_low, ga_two, TN).astype(jnp.bfloat16)
    both = attended.astype(jnp.float32)
    delta = jnp.sum(
        ga_two.astype(jnp.float32) * jnp.concatenate([both, both], axis=0), axis=-1, keepdims=True
    )
    grad_scores = (probs * (grad_probs - delta)).astype(jnp.bfloat16)
    beside = jnp.concatenate([grad_scores[:rows], grad_scores[rows:]], axis=1)
    grad_query = (dot(beside, k_two, NN) * DH ** (-0.5)).astype(jnp.bfloat16)
    grad_keys = (dot(grad_scores, q_two, TN) * DH ** (-0.5)).astype(jnp.bfloat16)
    return attended, grad_query, grad_keys, grad_values


def block_kernel(
    pieces, frames, patches, width,
    counts_ref, gain_ref, tokens_ref, cot_ref, *rest,
):
    weight_refs = rest[: len(rest) - 11]
    result_ref, grad_ref, w_in, w_out, normed, proj, ga, att, gproj, stats, sems = rest[-11:]
    groups = patches // SUB
    rows = frames * SUB
    total = groups * rows
    count = counts_ref[0]

    copies = []
    for which, (target, found) in enumerate(zip((w_in, w_out), pieces())):
        mine = []
        for ref, index, lanes, row, column in found:
            source = weight_refs[ref].at[index] if index is not None else weight_refs[ref]
            depth = source.shape[0]
            mine.append(
                pltpu.make_async_copy(
                    source.at[:, pl.ds(*lanes)],
                    target.at[
                        pl.ds(pl.multiple_of(row, 16), depth),
                        pl.ds(pl.multiple_of(column, 128), lanes[1]),
                    ],
                    sems.at[which],
                )
            )
        copies.append(mine)
    for mine in copies:
        for copy in mine:
            copy.start()

    live = (lax.broadcasted_iota(jnp.int32, (rows, 1), 0) // SUB < count).astype(jnp.float32)
    gain = gain_ref[...]

    def load(ref, group):
        start = pl.multiple_of(group * SUB, SUB)
        return ref[:, pl.ds(start, SUB), :].reshape(rows, width)

    def store(ref, group, value):
        start = pl.multiple_of(group * SUB, SUB)
        ref[:, pl.ds(start, SUB), :] = value.reshape(frames, SUB, width)

    for group in range(groups):
        here = pl.ds(group * rows, rows)
        wide = load(tokens_ref, group).astype(jnp.float32)
        average = jnp.mean(wide, axis=-1, keepdims=True)
        centred = wide - average
        variance = jnp.mean(centred * centred, axis=-1, keepdims=True)
        scale = lax.rsqrt(variance + EPSILON)
        normed[here, :] = (centred * scale * gain).astype(jnp.bfloat16)
        stats[here, 0:1] = average
        stats[here, 1:2] = scale

    for copy in copies[0]:
        copy.wait()

    step = 512

    @pl.loop(0, 3 * width // step)
    def _(j):
        columns = pl.ds(pl.multiple_of(j * step, step), step)
        proj[:, columns] = dot(normed[...], w_in[:, columns], NN).astype(jnp.bfloat16)

    for copy in copies[1]:
        copy.wait()

    for group in range(groups):
        here = pl.ds(group * rows, rows)
        normed[here, :] = (load(cot_ref, group).astype(jnp.float32) * live).astype(jnp.bfloat16)

    @pl.loop(0, width // step)
    def _(j):
        columns = pl.ds(pl.multiple_of(j * step, step), step)
        ga[:, columns] = dot(normed[...], w_out[columns, :], NT).astype(jnp.bfloat16)

    row = lax.broadcasted_iota(jnp.int32, (2 * rows, rows), 0)
    key = lax.broadcasted_iota(jnp.int32, (2 * rows, rows), 1)
    mask = (row % SUB == key % SUB) & (key // SUB < count)
    low_lanes = lax.broadcasted_iota(jnp.int32, (rows, PAIR), 1) < DH
    unroll = 4 if rows <= 128 else 1

    for group in range(groups):
        here = pl.ds(group * rows, rows)

        @pl.loop(0, width // (PAIR * unroll))
        def _(step_index):
            for inner in range(unroll):
                pair = step_index * unroll + inner

                def lanes(part):
                    return pl.ds(pl.multiple_of(part * width + pair * PAIR, PAIR), PAIR)

                attended, grad_query, grad_keys, grad_values = attention_pair(
                    proj[here, lanes(0)],
                    proj[here, lanes(1)],
                    proj[here, lanes(2)],
                    ga[here, lanes(0)],
                    mask,
                    low_lanes,
                )
                att[here, lanes(0)] = attended
                gproj[here, lanes(0)] = grad_query
                gproj[here, lanes(1)] = grad_keys
                gproj[here, lanes(2)] = grad_values

    for group in range(groups):
        here = pl.ds(group * rows, rows)
        mixed = dot(att[here, :], w_out[...], NN)
        store(
            result_ref,
            group,
            (load(tokens_ref, group).astype(jnp.float32) + live * mixed).astype(jnp.bfloat16),
        )

    for group in range(groups):
        here = pl.ds(group * rows, rows)
        grad = dot(gproj[here, :], w_in[...], NT) * gain
        scale = stats[here, 1:2]
        hat = (load(tokens_ref, group).astype(jnp.float32) - stats[here, 0:1]) * scale
        grad_rows = scale * (
            grad
            - jnp.mean(grad, axis=-1, keepdims=True)
            - hat * jnp.mean(grad * hat, axis=-1, keepdims=True)
        )
        store(
            grad_ref,
            group,
            (load(cot_ref, group).astype(jnp.float32) + grad_rows).astype(jnp.bfloat16),
        )


def run_block(counts, gain, tokens, cot, weights, pieces):
    frames, patches, width = tokens.shape
    total = frames * patches
    vmem = pl.BlockSpec(memory_space=pltpu.VMEM)
    anywhere = pl.BlockSpec(memory_space=pl.ANY)
    out = jax.ShapeDtypeStruct(tokens.shape, jnp.bfloat16)
    return pl.pallas_call(
        functools.partial(block_kernel, pieces, frames, patches, width),
        out_shape=(out, out),
        in_specs=[pl.BlockSpec(memory_space=pltpu.SMEM), vmem, vmem, vmem]
        + [anywhere] * len(weights),
        out_specs=(vmem, vmem),
        scratch_shapes=[
            pltpu.VMEM((width, 3 * width), jnp.bfloat16),
            pltpu.VMEM((width, width), jnp.bfloat16),
            pltpu.VMEM((total, width), jnp.bfloat16),
            pltpu.VMEM((total, 3 * width), jnp.bfloat16),
            pltpu.VMEM((total, width), jnp.bfloat16),
            pltpu.VMEM((total, width), jnp.bfloat16),
            pltpu.VMEM((total, 3 * width), jnp.bfloat16),
            pltpu.VMEM((total, 128), jnp.float32),
            pltpu.SemaphoreType.DMA((2,)),
        ],
        compiler_params=pltpu.CompilerParams(vmem_limit_bytes=48 * 1024 * 1024),
        cost_estimate=pl.CostEstimate(
            flops=16 * total * width * width,
            bytes_accessed=8 * width * width + 8 * total * width,
            transcendentals=total * 2048,
        ),
        name="block",
    )(counts, gain, tokens, cot, *weights)


def swap(array, distance, devices):
    return lax.ppermute(array, "frame", [(f, f ^ distance) for f in range(devices)])


def gather_weights(input_weights, output_weights, clips, devices):
    depth, in_columns = input_weights.shape
    out_columns = output_weights.shape[1]
    if devices == 8 and in_columns % 128 == 0 and out_columns % 128 == 0 and depth % 32 == 0:
        joined = jnp.concatenate([input_weights, output_weights], axis=1)
        half = depth // 2
        found = []
        for offset in range(clips):
            own = joined
            if offset > 0:
                own = lax.ppermute(
                    joined, "clip", [(c, (c + offset) % clips) for c in range(clips)]
                )
            by_x, by_y = swap(own, 2, devices), swap(own, 4, devices)
            top = swap(by_y[:half], 2, devices)
            bottom = swap(by_x[half:], 4, devices)
            for array, distance, row in (
                (own, 0, 0),
                (by_x, 2, 0),
                (by_y, 4, 0),
                (top, 6, 0),
                (bottom, 6, half),
            ):
                found.append((array, offset, distance, row))
                found.append((swap(array, 1, devices), offset, distance ^ 1, row))
        arrays = [entry[0] for entry in found]
        places = [entry[1:] for entry in found]

        def pieces():
            clip, frame = lax.axis_index("clip"), lax.axis_index("frame")
            both = ([], [])
            for ref, (offset, distance, row) in enumerate(places):
                column = lax.rem(clip + (clips - offset), clips)
                start = (frame ^ distance) * depth + row
                both[0].append((ref, None, (0, in_columns), start, column * in_columns))
                both[1].append((ref, None, (in_columns, out_columns), start, column * out_columns))
            return both

        return arrays, pieces
    both = []
    for weights in (input_weights, output_weights):
        columns = lax.all_gather(weights, "clip", axis=1, tiled=True)
        both.append(lax.all_gather(columns, "frame", axis=0, tiled=True))
    pieces = tuple([(i, None, (0, w.shape[1]), 0, 0)] for i, w in enumerate(both))
    return both, lambda: pieces


def per_device(clips, devices, tokens, counts, norm_gain, input_weights, output_weights, cotangent):
    _, slots, patches, width = tokens.shape
    weights, pieces = gather_weights(input_weights, output_weights, clips, devices)
    share = -(-patches // devices)
    share = -(-share // SUB) * SUB
    extra = devices * share - patches
    both = jnp.concatenate([tokens, cotangent], axis=0)
    both = jnp.pad(both, ((0, 0), (0, 0), (0, extra), (0, 0)))
    both = both.reshape(2, slots, devices, share, width)
    both = lax.all_to_all(both, "frame", split_axis=2, concat_axis=1, tiled=True)
    both = both.reshape(2, devices * slots, share, width)
    outs = run_block(counts, norm_gain.reshape(1, width), both[0], both[1], weights, pieces)
    back = jnp.stack(outs).reshape(2, devices * slots, 1, share, width)
    back = lax.all_to_all(back, "frame", split_axis=1, concat_axis=2, tiled=True)
    back = back.reshape(2, slots, devices * share, width)[:, :, :patches]
    return back[0][None], back[1][None]


def solution(mesh):
    in_specs = (
        P("clip", "frame", None, None),
        P("clip"),
        P(),
        P("frame", "clip"),
        P("frame", "clip"),
        P("clip", "frame", None, None),
    )
    out_specs = (P("clip", "frame", None, None), P("clip", "frame", None, None))
    body = functools.partial(per_device, mesh.shape["clip"], mesh.shape["frame"])
    return jax.shard_map(body, mesh=mesh, in_specs=in_specs, out_specs=out_specs, check_vma=False)
```

```python
import functools

import jax
import jax.numpy as jnp
from jax import lax
from jax.experimental import pallas as pl
from jax.experimental.pallas import tpu as pltpu
from jax.sharding import PartitionSpec as P

DH = 64
PAIR = 2 * DH
SUB = 16
EPSILON = 1e-06
NEGATIVE = -1e30
NN = (((1,), (0,)), ((), ()))
NT = (((1,), (1,)), ((), ()))
TN = (((0,), (0,)), ((), ()))


def dot(a, b, dims):
    return lax.dot_general(a, b, dims, preferred_element_type=jnp.float32)


def attention_pair(q, k, v, ga, mask, low_lanes):
    zero = jnp.zeros_like(q)

    def apart(block):
        return jnp.concatenate(
            [jnp.where(low_lanes, block, zero), jnp.where(low_lanes, zero, block)], axis=0
        )

    def stacked(block):
        return jnp.concatenate([block[:, :rows], block[:, rows:]], axis=0)

    rows = q.shape[0]
    q_two, k_two, v_two, ga_two = apart(q), apart(k), apart(v), apart(ga)
    scores = dot(k, q_two, NT) * DH ** (-0.5)
    grad_probs = dot(v, ga_two, NT)
    scores = jnp.where(mask, scores, NEGATIVE)
    highest = jnp.max(scores, axis=0, keepdims=True)
    expanded = jnp.exp(scores - highest)
    probs = expanded * (1.0 / jnp.sum(expanded, axis=0, keepdims=True))
    probs_low = probs.astype(jnp.bfloat16)
    weighted = probs * grad_probs
    delta = jnp.sum(weighted, axis=0, keepdims=True)
    grad_scores = (weighted - probs * delta).astype(jnp.bfloat16)
    attended = dot(stacked(probs_low), v_two, TN).astype(jnp.bfloat16)
    grad_values = dot(probs_low, ga_two, NN).astype(jnp.bfloat16)
    grad_query = (dot(stacked(grad_scores), k_two, TN) * DH ** (-0.5)).astype(jnp.bfloat16)
    grad_keys = (dot(grad_scores, q_two, NN) * DH ** (-0.5)).astype(jnp.bfloat16)
    return attended, grad_query, grad_keys, grad_values


def block_kernel(
    pieces, frames, patches, width,
    counts_ref, gain_ref, both_ref, *rest,
):
    weight_refs = rest[: len(rest) - 10]
    out_ref, w_in, w_out, normed, proj, ga, att, gproj, stats, sems = rest[-10:]
    groups = patches // SUB
    rows = frames * SUB
    total = groups * rows
    count = counts_ref[0]

    copies = []
    for which, (target, found) in enumerate(zip((w_in, w_out), pieces())):
        mine = []
        for ref, first, depth, lanes, row, column in found:
            source = weight_refs[ref].at[pl.ds(first, depth)]
            mine.append(
                pltpu.make_async_copy(
                    source.at[:, pl.ds(*lanes)],
                    target.at[
                        pl.ds(pl.multiple_of(row, 16), depth),
                        pl.ds(pl.multiple_of(column, 128), lanes[1]),
                    ],
                    sems.at[which],
                )
            )
        copies.append(mine)
    for mine in copies:
        for copy in mine:
            copy.start()

    live = (lax.broadcasted_iota(jnp.int32, (rows, 1), 0) // SUB < count).astype(jnp.float32)
    gain = gain_ref[...]

    def load(which, group):
        return both_ref[:, which, group * SUB : (group + 1) * SUB, :].reshape(rows, width)

    def store(which, group, value):
        out_ref[:, which, group * SUB : (group + 1) * SUB, :] = value.reshape(frames, SUB, width)

    for group in range(groups):
        here = pl.ds(group * rows, rows)
        wide = load(0, group).astype(jnp.float32)
        average = jnp.mean(wide, axis=-1, keepdims=True)
        centred = wide - average
        variance = jnp.mean(centred * centred, axis=-1, keepdims=True)
        scale = lax.rsqrt(variance + EPSILON)
        normed[here, :] = (centred * scale * gain).astype(jnp.bfloat16)
        stats[here, 0:1] = average
        stats[here, 1:2] = scale

    for copy in copies[0]:
        copy.wait()

    step = 512

    @pl.loop(0, 3 * width // step)
    def _(j):
        columns = pl.ds(pl.multiple_of(j * step, step), step)
        proj[:, columns] = dot(normed[...], w_in[:, columns], NN).astype(jnp.bfloat16)

    for copy in copies[1]:
        copy.wait()

    for group in range(groups):
        here = pl.ds(group * rows, rows)
        normed[here, :] = (load(1, group).astype(jnp.float32) * live).astype(jnp.bfloat16)

    @pl.loop(0, width // step)
    def _(j):
        columns = pl.ds(pl.multiple_of(j * step, step), step)
        ga[:, columns] = dot(normed[...], w_out[columns, :], NT).astype(jnp.bfloat16)

    key = lax.broadcasted_iota(jnp.int32, (rows, 2 * rows), 0)
    query = lax.broadcasted_iota(jnp.int32, (rows, 2 * rows), 1)
    mask = (query % SUB == key % SUB) & (key // SUB < count)
    low_lanes = lax.broadcasted_iota(jnp.int32, (rows, PAIR), 1) < DH
    unroll = 4 if rows <= 128 else 1

    for group in range(groups):
        here = pl.ds(group * rows, rows)

        @pl.loop(0, width // (PAIR * unroll))
        def _(step_index):
            for inner in range(unroll):
                pair = step_index * unroll + inner

                def lanes(part):
                    return pl.ds(pl.multiple_of(part * width + pair * PAIR, PAIR), PAIR)

                attended, grad_query, grad_keys, grad_values = attention_pair(
                    proj[here, lanes(0)],
                    proj[here, lanes(1)],
                    proj[here, lanes(2)],
                    ga[here, lanes(0)],
                    mask,
                    low_lanes,
                )
                att[here, lanes(0)] = attended
                gproj[here, lanes(0)] = grad_query
                gproj[here, lanes(1)] = grad_keys
                gproj[here, lanes(2)] = grad_values

    for group in range(groups):
        here = pl.ds(group * rows, rows)
        mixed = dot(att[here, :], w_out[...], NN)
        store(
            0,
            group,
            (load(0, group).astype(jnp.float32) + live * mixed).astype(jnp.bfloat16),
        )

    for group in range(groups):
        here = pl.ds(group * rows, rows)
        grad = dot(gproj[here, :], w_in[...], NT) * gain
        scale = stats[here, 1:2]
        hat = (load(0, group).astype(jnp.float32) - stats[here, 0:1]) * scale
        grad_rows = scale * (
            grad
            - jnp.mean(grad, axis=-1, keepdims=True)
            - hat * jnp.mean(grad * hat, axis=-1, keepdims=True)
        )
        store(
            1,
            group,
            (load(1, group).astype(jnp.float32) + grad_rows).astype(jnp.bfloat16),
        )


def run_block(counts, gain, both, weights, pieces):
    frames, _, patches, width = both.shape
    total = frames * patches
    vmem = pl.BlockSpec(memory_space=pltpu.VMEM)
    anywhere = pl.BlockSpec(memory_space=pl.ANY)
    return pl.pallas_call(
        functools.partial(block_kernel, pieces, frames, patches, width),
        out_shape=jax.ShapeDtypeStruct(both.shape, jnp.bfloat16),
        in_specs=[pl.BlockSpec(memory_space=pltpu.SMEM), vmem, vmem]
        + [anywhere] * len(weights),
        out_specs=vmem,
        scratch_shapes=[
            pltpu.VMEM((width, 3 * width), jnp.bfloat16),
            pltpu.VMEM((width, width), jnp.bfloat16),
            pltpu.VMEM((total, width), jnp.bfloat16),
            pltpu.VMEM((total, 3 * width), jnp.bfloat16),
            pltpu.VMEM((total, width), jnp.bfloat16),
            pltpu.VMEM((total, width), jnp.bfloat16),
            pltpu.VMEM((total, 3 * width), jnp.bfloat16),
            pltpu.VMEM((total, 128), jnp.float32),
            pltpu.SemaphoreType.DMA((2,)),
        ],
        compiler_params=pltpu.CompilerParams(vmem_limit_bytes=48 * 1024 * 1024),
        cost_estimate=pl.CostEstimate(
            flops=16 * total * width * width,
            bytes_accessed=8 * width * width + 8 * total * width,
            transcendentals=total * 2048,
        ),
        name="block",
    )(counts, gain, both, *weights)


def swap(array, distance, devices):
    return lax.ppermute(array, "frame", [(f, f ^ distance) for f in range(devices)])


def finish(held, half, devices):
    _, by_x, by_y = held
    top, bottom = swap(by_y[:half], 2, devices), swap(by_x[half:], 4, devices)
    return [array for mine in (*held, top, bottom) for array in (mine, swap(mine, 1, devices))]


def join_kernel(left_ref, right_ref, out_ref, sems):
    width = left_ref.shape[1]
    copies = [
        pltpu.make_async_copy(left_ref, out_ref.at[:, pl.ds(0, width)], sems.at[0]),
        pltpu.make_async_copy(right_ref, out_ref.at[:, pl.ds(width, right_ref.shape[1])], sems.at[1]),
    ]
    for copy in copies:
        copy.start()
    for copy in copies:
        copy.wait()


def join(left, right):
    anywhere = pl.BlockSpec(memory_space=pl.ANY)
    return pl.pallas_call(
        join_kernel,
        out_shape=jax.ShapeDtypeStruct((left.shape[0], left.shape[1] + right.shape[1]), left.dtype),
        in_specs=[anywhere, anywhere],
        out_specs=pl.BlockSpec(memory_space=pltpu.VMEM),
        scratch_shapes=[pltpu.SemaphoreType.DMA((2,))],
        name="join",
    )(left, right)


def gather_weights(input_weights, output_weights, both, clips, devices):
    depth, in_columns = input_weights.shape
    out_columns = output_weights.shape[1]
    fits = in_columns % 128 == 0 and out_columns % 128 == 0 and depth % 32 == 0
    if clips == 4 and devices == 8 and fits:
        joined = join(input_weights, output_weights)
        half = depth // 2
        order = (0, 1, 3, 2)
        held, source = [joined], joined
        for offset in order[1:]:
            held.append(lax.ppermute(source, "clip", [(c, c ^ offset) for c in range(clips)]))
            source, held[-1] = lax.optimization_barrier((source, held[-1]))
        arrays, places, before, earlier = [], [], [], []
        for step, own in enumerate(held):
            if step > 0:
                gate = before + earlier + ([both] if step == 2 else [])
                own, *gate = lax.optimization_barrier((own, *gate))
                if step == 2:
                    both = gate.pop()
                earlier = gate[len(before):]
                arrays += earlier
                before = gate[: len(before)]
            by_x, by_y = swap(own, 2, devices), swap(own, 4, devices)
            if step > 0:
                earlier = finish(before, half, devices)
            before = [own, by_x, by_y]
        arrays += earlier + finish(before, half, devices)

        def pieces():
            clip, frame = lax.axis_index("clip"), lax.axis_index("frame")
            found = ([], [])
            ref = 0
            for offset in order:
                column = clip ^ offset
                for distance, row in ((0, 0), (2, 0), (4, 0), (6, 0), (6, half)):
                    for core in (0, 1):
                        start = (frame ^ (distance + core)) * depth + row
                        part = (ref, 0, half if distance == 6 else depth)
                        found[0].append((*part, (0, in_columns), start, column * in_columns))
                        found[1].append(
                            (*part, (in_columns, out_columns), start, column * out_columns)
                        )
                        ref += 1
            return found

        return arrays, pieces, both
    arrays = []
    for weights in (input_weights, output_weights):
        columns = lax.all_gather(weights, "clip", axis=1, tiled=True)
        arrays.append(lax.all_gather(columns, "frame", axis=0, tiled=True))
    found = tuple([(i, 0, w.shape[0], (0, w.shape[1]), 0, 0)] for i, w in enumerate(arrays))
    return arrays, lambda: found, both


def per_device(clips, devices, tokens, counts, norm_gain, input_weights, output_weights, cotangent):
    _, slots, patches, width = tokens.shape
    share = -(-patches // devices)
    share = -(-share // SUB) * SUB
    extra = devices * share - patches

    def by_destination(source):
        padded = jnp.pad(source[0], ((0, 0), (0, extra), (0, 0)))
        return padded.reshape(slots, devices, share, width).transpose(1, 0, 2, 3)

    both = jnp.stack([by_destination(tokens), by_destination(cotangent)], axis=2)
    both = lax.all_to_all(both, "frame", split_axis=0, concat_axis=0, tiled=True)
    weights, pieces, both = gather_weights(input_weights, output_weights, both, clips, devices)
    both = both.reshape(devices * slots, 2, share, width)
    back = run_block(counts, norm_gain.reshape(1, width), both, weights, pieces)
    back = back.reshape(devices, slots, 2, share, width)
    back = lax.all_to_all(back, "frame", split_axis=0, concat_axis=0, tiled=True)

    def in_order(which):
        rows = back[:, :, which].transpose(1, 0, 2, 3).reshape(slots, devices * share, width)
        return rows[None, :, :patches]

    return in_order(0), in_order(1)


def solution(mesh):
    in_specs = (
        P("clip", "frame", None, None),
        P("clip"),
        P(),
        P("frame", "clip"),
        P("frame", "clip"),
        P("clip", "frame", None, None),
    )
    out_specs = (P("clip", "frame", None, None), P("clip", "frame", None, None))
    body = functools.partial(per_device, mesh.shape["clip"], mesh.shape["frame"])
    return jax.shard_map(body, mesh=mesh, in_specs=in_specs, out_specs=out_specs, check_vma=False)
```

```python
import functools
import math

import jax
import jax.numpy as jnp
from jax import lax
from jax.experimental import pallas as pl
from jax.experimental.pallas import tpu as pltpu
from jax.sharding import PartitionSpec as P

DH = 64
PAIR = 2 * DH
SUB = 16
EPSILON = 1e-06
NEGATIVE = -1e30
NN = (((1,), (0,)), ((), ()))
NT = (((1,), (1,)), ((), ()))
TN = (((0,), (0,)), ((), ()))


def dot(a, b, dims):
    return lax.dot_general(a, b, dims, preferred_element_type=jnp.float32)


def attention_pair(q, k, v, ga, mask, low, high):
    def apart(block):
        return jnp.concatenate([block * low, block * high], axis=0)

    def stacked(block):
        return jnp.concatenate([block[:, :rows], block[:, rows:]], axis=0)

    rows = q.shape[0]
    q_two, k_two, v_two, ga_two = apart(q * DH ** (-0.5)), apart(k), apart(v), apart(ga)
    scores = dot(k, q_two, NT)
    grad_probs = dot(v, ga_two, NT)
    scores = jnp.where(mask, scores, NEGATIVE)
    highest = jnp.max(scores, axis=0, keepdims=True)
    expanded = jnp.exp(scores - highest)
    probs = expanded * (1.0 / jnp.sum(expanded, axis=0, keepdims=True))
    probs_low = probs.astype(jnp.bfloat16)
    weighted = probs * grad_probs
    delta = jnp.sum(weighted, axis=0, keepdims=True)
    grad_scores = (weighted - probs * delta).astype(jnp.bfloat16)
    attended = dot(stacked(probs_low), v_two, TN).astype(jnp.bfloat16)
    grad_values = dot(probs_low, ga_two, NN).astype(jnp.bfloat16)
    grad_query = (dot(stacked(grad_scores), k_two, TN) * DH ** (-0.5)).astype(jnp.bfloat16)
    grad_keys = dot(grad_scores, q_two, NN).astype(jnp.bfloat16)
    return attended, grad_query, grad_keys, grad_values


def block_kernel(
    pieces, xor_order, frames, patches, width,
    counts_ref, gain_ref, both_ref, *rest,
):
    weight_refs = rest[: len(rest) - 11]
    out_ref, w_in, w_out, normed, proj, ga, att, gproj, gnorm, stats, sems = rest[-11:]
    groups = patches // SUB
    rows = frames * SUB
    total = groups * rows
    count = counts_ref[0]
    device = lax.axis_index("frame")

    found = pieces()
    copies = []
    for block, parts in enumerate(found):
        mine = []
        for ref, first, depth, lanes, target, row, column in parts:
            mine.append(
                pltpu.make_async_copy(
                    weight_refs[ref].at[pl.ds(first, depth), pl.ds(*lanes)],
                    (w_in, w_out)[target].at[
                        pl.ds(pl.multiple_of(row, 16), depth),
                        pl.ds(pl.multiple_of(column, 128), lanes[1]),
                    ],
                    sems.at[block],
                )
            )
        copies.append(mine)
    for mine in copies:
        for copy in mine:
            copy.start()

    live = (lax.broadcasted_iota(jnp.int32, (rows, 1), 0) // SUB < count).astype(jnp.float32)
    gain = gain_ref[...]

    def load(which, group):
        return both_ref[:, which, group * SUB : (group + 1) * SUB, :].reshape(rows, width)

    def store(which, group, value):
        for frame in range(frames):
            place = frame ^ device if xor_order else frame
            out_ref[pl.ds(place, 1), which, group * SUB : (group + 1) * SUB, :] = value[
                frame * SUB : (frame + 1) * SUB
            ].reshape(1, SUB, width)

    for group in range(groups):
        here = pl.ds(group * rows, rows)
        wide = load(0, group).astype(jnp.float32)
        average = jnp.mean(wide, axis=-1, keepdims=True)
        centred = wide - average
        variance = jnp.mean(centred * centred, axis=-1, keepdims=True)
        scale = lax.rsqrt(variance + EPSILON)
        normed[here, :] = (centred * scale * gain).astype(jnp.bfloat16)
        stats[here, 0:1] = average
        stats[here, 1:2] = scale

    for parts, mine in zip(found[:-1], copies[:-1]):
        for copy in mine:
            copy.wait()
        column, columns = parts[0][-1], parts[0][3][1]
        step = math.gcd(columns, 768)

        @pl.loop(0, columns // step)
        def _(j):
            here = pl.ds(pl.multiple_of(column + j * step, 128), step)
            proj[:, here] = dot(normed[...], w_in[:, here], NN).astype(jnp.bfloat16)

    for copy in copies[-1]:
        copy.wait()

    for group in range(groups):
        here = pl.ds(group * rows, rows)
        normed[here, :] = (load(1, group).astype(jnp.float32) * live).astype(jnp.bfloat16)

    step = min(width, 256)

    @pl.loop(0, width // step)
    def _(j):
        columns = pl.ds(pl.multiple_of(j * step, step), step)
        ga[:, columns] = dot(w_out[columns, :], normed[...], NT).astype(jnp.bfloat16).T

    key = lax.broadcasted_iota(jnp.int32, (rows, 2 * rows), 0)
    query = lax.broadcasted_iota(jnp.int32, (rows, 2 * rows), 1)
    mask = (query % SUB == key % SUB) & (key // SUB < count)
    lane = lax.broadcasted_iota(jnp.int32, (1, PAIR), 1)
    low, high = (lane < DH).astype(jnp.bfloat16), (lane >= DH).astype(jnp.bfloat16)
    unroll = 4 if rows <= 128 else 1

    for group in range(groups):
        here = pl.ds(group * rows, rows)

        @pl.loop(0, width // (PAIR * unroll))
        def _(step_index):
            for inner in range(unroll):
                pair = step_index * unroll + inner

                def lanes(part):
                    return pl.ds(pl.multiple_of(part * width + pair * PAIR, PAIR), PAIR)

                attended, grad_query, grad_keys, grad_values = attention_pair(
                    proj[here, lanes(0)],
                    proj[here, lanes(1)],
                    proj[here, lanes(2)],
                    ga[here, lanes(0)],
                    mask,
                    low,
                    high,
                )
                att[here, lanes(0)] = attended
                gproj[here, lanes(0)] = grad_query
                gproj[here, lanes(1)] = grad_keys
                gproj[here, lanes(2)] = grad_values

    for group in range(groups):
        here = pl.ds(group * rows, rows)
        mixed = dot(att[here, :], w_out[...], NN)
        store(
            0,
            group,
            (load(0, group).astype(jnp.float32) + live * mixed).astype(jnp.bfloat16),
        )

    @pl.loop(0, width // step)
    def _(j):
        columns = pl.ds(pl.multiple_of(j * step, step), step)
        gnorm[:, columns] = dot(w_in[columns, :], gproj[...], NT).T

    for group in range(groups):
        here = pl.ds(group * rows, rows)
        grad = gnorm[here, :] * gain
        scale = stats[here, 1:2]
        hat = (load(0, group).astype(jnp.float32) - stats[here, 0:1]) * scale
        grad_rows = scale * (
            grad
            - jnp.mean(grad, axis=-1, keepdims=True)
            - hat * jnp.mean(grad * hat, axis=-1, keepdims=True)
        )
        store(
            1,
            group,
            (load(1, group).astype(jnp.float32) + grad_rows).astype(jnp.bfloat16),
        )


def run_block(counts, gain, both, weights, pieces, xor_order):
    frames, _, patches, width = both.shape
    total = frames * patches
    vmem = pl.BlockSpec(memory_space=pltpu.VMEM)
    anywhere = pl.BlockSpec(memory_space=pl.ANY)
    return pl.pallas_call(
        functools.partial(block_kernel, pieces, xor_order, frames, patches, width),
        out_shape=jax.ShapeDtypeStruct(both.shape, jnp.bfloat16),
        in_specs=[pl.BlockSpec(memory_space=pltpu.SMEM), vmem, vmem]
        + [anywhere] * len(weights),
        out_specs=vmem,
        scratch_shapes=[
            pltpu.VMEM((width, 3 * width), jnp.bfloat16),
            pltpu.VMEM((width, width), jnp.bfloat16),
            pltpu.VMEM((total, width), jnp.bfloat16),
            pltpu.VMEM((total, 3 * width), jnp.bfloat16),
            pltpu.VMEM((total, width), jnp.bfloat16),
            pltpu.VMEM((total, width), jnp.bfloat16),
            pltpu.VMEM((total, 3 * width), jnp.bfloat16),
            pltpu.VMEM((total, width), jnp.float32),
            pltpu.VMEM((total, 128), jnp.float32),
            pltpu.SemaphoreType.DMA((8,)),
        ],
        compiler_params=pltpu.CompilerParams(vmem_limit_bytes=48 * 1024 * 1024),
        cost_estimate=pl.CostEstimate(
            flops=16 * total * width * width,
            bytes_accessed=8 * width * width + 8 * total * width,
            transcendentals=total * 2048,
        ),
        name="block",
    )(counts, gain, both, *weights)


def swap(array, distance, devices):
    return lax.ppermute(array, "frame", [(f, f ^ distance) for f in range(devices)])


def join_kernel(axis, *refs):
    *sources, target = refs
    start = 0
    for source in sources:
        end = start + source.shape[axis]
        if axis == 0:
            target[start:end, :] = source[...]
        else:
            target[:, start:end] = source[...]
        start = end


def join(axis, *arrays):
    shape = list(arrays[0].shape)
    shape[axis] = sum(array.shape[axis] for array in arrays)
    vmem = pl.BlockSpec(memory_space=pltpu.VMEM)
    return pl.pallas_call(
        functools.partial(join_kernel, axis),
        out_shape=jax.ShapeDtypeStruct(shape, arrays[0].dtype),
        in_specs=[vmem] * len(arrays),
        out_specs=vmem,
        name="join",
    )(*arrays)


def gather_rounds(input_weights, output_weights, both, devices):
    depth, in_columns = input_weights.shape
    out_columns = output_weights.shape[1]
    joined = join(1, input_weights, output_weights)
    half = depth // 2
    one, three, two = (
        lax.ppermute(joined, "clip", [(c, c ^ offset) for c in range(4)]) for offset in (1, 3, 2)
    )

    def across(own):
        return swap(own, 2, devices), swap(own, 4, devices)

    def diagonal(by_x, by_y):
        middle = by_x.shape[0] // 2
        return swap(by_y[:middle], 2, devices), swap(by_x[middle:], 4, devices)

    def other_core(arrays):
        return [swap(array, 1, devices) for array in arrays]

    first = [joined, *across(joined)]
    first += diagonal(*first[1:])
    both, *gate = lax.optimization_barrier((both, *first[1:3]))
    first[1:3] = gate
    both = lax.all_to_all(both, "frame", split_axis=0, concat_axis=0, tiled=True)
    second = [one, *across(one)]
    second += diagonal(*second[1:])
    first_other = other_core(first)
    three, second[1], second[2] = lax.optimization_barrier((three, second[1], second[2]))
    third, both, *first_other = lax.optimization_barrier((join(0, three, two), both, *first_other))
    third = [third, *across(third)]
    second_other = other_core(second)
    third[1], *second_other = lax.optimization_barrier((third[1], *second_other))
    third += diagonal(*third[1:])
    third_other = other_core(third)
    arrays = first + first_other + second + second_other + third + third_other

    def pieces():
        clip, frame = lax.axis_index("clip"), lax.axis_index("frame")
        found = {offset: [] for offset in (0, 1, 3, 2)}
        outer = []
        ref = 0
        for offsets in ((0,), (1,), (3, 2)):
            for core in (0, 1):
                for distance, part in ((0, None), (2, None), (4, None), (6, 0), (6, 1)):
                    rows = depth * len(offsets)
                    held = (0, rows) if part is None else (part * (rows // 2), rows // 2)
                    for place, offset in enumerate(offsets):
                        start = max(held[0], place * depth)
                        end = min(sum(held), (place + 1) * depth)
                        if end <= start:
                            continue
                        row = (frame ^ (distance + core)) * depth + (start - place * depth)
                        block = clip ^ offset
                        where = (ref, start - held[0], end - start)
                        found[offset].append(
                            (*where, (0, in_columns), 0, row, block * in_columns)
                        )
                        outer.append(
                            (*where, (in_columns, out_columns), 1, row, block * out_columns)
                        )
                    ref += 1
        return [*found.values(), outer]

    return arrays, pieces, both


def gather_plainly(input_weights, output_weights, both):
    arrays = []
    for weights in (input_weights, output_weights):
        columns = lax.all_gather(weights, "clip", axis=1, tiled=True)
        arrays.append(lax.all_gather(columns, "frame", axis=0, tiled=True))
    both = lax.all_to_all(both, "frame", split_axis=0, concat_axis=0, tiled=True)
    found = [[(i, 0, w.shape[0], (0, w.shape[1]), i, 0, 0)] for i, w in enumerate(arrays)]
    return arrays, lambda: found, both


def order_kernel(devices, patches, *refs):
    *sources, result_ref, grad_ref, held = refs
    me = lax.axis_index("frame")
    share = sources[0].shape[1]
    for distance, source in enumerate(sources):
        rows = pl.ds(pl.multiple_of((me ^ distance) * share, share), share)
        held[0, rows, :] = source[0]
        held[1, rows, :] = source[1]
    result_ref[0, 0] = held[0, :patches]
    grad_ref[0, 0] = held[1, :patches]


def bring_back(blocks, devices, patches):
    _, _, share, width = blocks.shape
    vmem = pl.BlockSpec(memory_space=pltpu.VMEM)
    got = [blocks[0]] + [None] * (devices - 1)
    for distance in sorted(range(1, devices), reverse=True):
        pairs = [(f, f ^ distance) for f in range(devices) if f * share < patches]
        got[distance] = lax.ppermute(blocks[distance], "frame", pairs)
    out = jax.ShapeDtypeStruct((1, 1, patches, width), blocks.dtype)
    return pl.pallas_call(
        functools.partial(order_kernel, devices, patches),
        out_shape=(out, out),
        in_specs=[vmem] * devices,
        out_specs=(vmem, vmem),
        scratch_shapes=[pltpu.VMEM((2, devices * share, width), blocks.dtype)],
        name="order",
    )(*got)


def per_device(clips, devices, tokens, counts, norm_gain, input_weights, output_weights, cotangent):
    _, slots, patches, width = tokens.shape
    share = -(-patches // devices)
    share = -(-share // SUB) * SUB
    extra = devices * share - patches

    def by_destination(source):
        padded = jnp.pad(source[0], ((0, 0), (0, extra), (0, 0)))
        return padded.reshape(slots, devices, share, width).transpose(1, 0, 2, 3)

    both = jnp.stack([by_destination(tokens), by_destination(cotangent)], axis=2)
    depth, in_columns = input_weights.shape
    fits = in_columns % 128 == 0 and output_weights.shape[1] % 128 == 0 and depth % 32 == 0
    small = clips == 4 and devices == 8 and slots == 1 and fits
    if small:
        weights, pieces, both = gather_rounds(input_weights, output_weights, both, devices)
    else:
        weights, pieces, both = gather_plainly(input_weights, output_weights, both)
    both = both.reshape(devices * slots, 2, share, width)
    back = run_block(counts, norm_gain.reshape(1, width), both, weights, pieces, small)
    if small:
        return bring_back(back, devices, patches)
    back = back.reshape(devices, slots, 2, share, width)
    back = lax.all_to_all(back, "frame", split_axis=0, concat_axis=0, tiled=True)

    def in_order(which):
        rows = back[:, :, which].transpose(1, 0, 2, 3).reshape(slots, devices * share, width)
        return rows[None, :, :patches]

    return in_order(0), in_order(1)


def solution(mesh):
    in_specs = (
        P("clip", "frame", None, None),
        P("clip"),
        P(),
        P("frame", "clip"),
        P("frame", "clip"),
        P("clip", "frame", None, None),
    )
    out_specs = (P("clip", "frame", None, None), P("clip", "frame", None, None))
    body = functools.partial(per_device, mesh.shape["clip"], mesh.shape["frame"])
    return jax.shard_map(body, mesh=mesh, in_specs=in_specs, out_specs=out_specs, check_vma=False)
```

```python
import functools
import math

import jax
import jax.numpy as jnp
from jax import lax
from jax.experimental import pallas as pl
from jax.experimental.pallas import tpu as pltpu
from jax.sharding import PartitionSpec as P

DH = 64
PAIR = 2 * DH
SUB = 16
EPSILON = 1e-06
NEGATIVE = -1e30
NN = (((1,), (0,)), ((), ()))
NT = (((1,), (1,)), ((), ()))
TN = (((0,), (0,)), ((), ()))
VMEM_LIMIT = 48 * 1024 * 1024


def dot(a, b, dims):
    return lax.dot_general(a, b, dims, preferred_element_type=jnp.float32)


def fetch(parts, refs, target, sem):
    copies = []
    for ref, index, first, depth, lanes, row, column in parts:
        source = refs[ref] if index is None else refs[ref].at[index]
        copies.append(
            pltpu.make_async_copy(
                source.at[pl.ds(first, depth), pl.ds(*lanes)],
                target.at[
                    pl.ds(pl.multiple_of(row, 16), depth),
                    pl.ds(pl.multiple_of(column, 128), lanes[1]),
                ],
                sem,
            )
        )
    for copy in copies:
        copy.start()
    return copies


def wait(copies):
    for copy in copies:
        copy.wait()


def load_rows(ref, which, group):
    frames, _, _, width = ref.shape
    return ref[:, which, group * SUB : (group + 1) * SUB, :].reshape(frames * SUB, width)


def front_kernel(plan, both_ref, gain_ref, *rest):
    weight_refs = rest[:-5]
    normed_ref, stats_ref, proj_ref, w_front, sems = rest[-5:]
    copies = fetch(plan["front"](), weight_refs, w_front, sems.at[0])
    frames, _, patches, _ = both_ref.shape
    rows = frames * SUB
    for group in range(patches // SUB):
        here = pl.ds(group * rows, rows)
        wide = load_rows(both_ref, 0, group).astype(jnp.float32)
        average = jnp.mean(wide, axis=-1, keepdims=True)
        centred = wide - average
        variance = jnp.mean(centred * centred, axis=-1, keepdims=True)
        scale = lax.rsqrt(variance + EPSILON)
        normed_ref[here, :] = (centred * scale * gain_ref[...]).astype(jnp.bfloat16)
        stats_ref[here, 0:1] = average
        stats_ref[here, 1:2] = scale
    wait(copies)
    columns = w_front.shape[1]
    step = math.gcd(columns, 512)

    @pl.loop(0, columns // step)
    def _(j):
        here = pl.ds(pl.multiple_of(j * step, step), step)
        proj_ref[:, here] = dot(normed_ref[...], w_front[:, here], NN).astype(jnp.bfloat16)


def main_kernel(plan, counts_ref, gain_ref, both_ref, normed_ref, stats_ref, front_ref, *rest):
    weight_refs = rest[:-14]
    out_ref, w_in, w_out, grads, proj, ga, att, gproj, gnorm, bias, scores, gprobs, low, sems = rest[-14:]
    frames, _, patches, width = both_ref.shape
    groups = patches // SUB
    rows = frames * SUB
    count = counts_ref[0]

    place = [
        pltpu.make_async_copy(
            front_ref.at[:, pl.ds(start, size)], proj.at[:, pl.ds(target, size)], sems.at[3]
        )
        for start, target, size in plan["placed"]
    ]
    for copy in place:
        copy.start()
    late = fetch(plan["late"](), weight_refs, w_in, sems.at[0])
    outer = fetch(plan["outer"](), weight_refs, w_out, sems.at[1])
    again = fetch(plan["again"](), weight_refs, w_in, sems.at[2])

    live = (lax.broadcasted_iota(jnp.int32, (rows, 1), 0) // SUB < count).astype(jnp.float32)
    for group in range(groups):
        here = pl.ds(group * rows, rows)
        grads[here, :] = (load_rows(both_ref, 1, group).astype(jnp.float32) * live).astype(
            jnp.bfloat16
        )
    key = lax.broadcasted_iota(jnp.int32, (rows, 2 * rows), 0)
    query = lax.broadcasted_iota(jnp.int32, (rows, 2 * rows), 1)
    bias[...] = jnp.where((query % SUB == key % SUB) & (key // SUB < count), 0.0, NEGATIVE)
    lane = lax.broadcasted_iota(jnp.int32, (1, PAIR), 1)
    low_lanes = (lane < DH).astype(jnp.bfloat16)
    high_lanes = (lane >= DH).astype(jnp.bfloat16)

    wait(late)
    for start, size in plan["missing"]:
        proj[:, start : start + size] = dot(
            normed_ref[...], w_in[:, start : start + size], NN
        ).astype(jnp.bfloat16)

    wait(outer)
    step = min(width, 256)

    @pl.loop(0, width // step)
    def _(j):
        columns = pl.ds(pl.multiple_of(j * step, step), step)
        ga[:, columns] = dot(grads[...], w_out[columns, :], NT).astype(jnp.bfloat16)

    wait(place)

    def apart(block):
        return jnp.concatenate([block * low_lanes, block * high_lanes], axis=0)

    def stacked(block):
        return jnp.concatenate([block[:, :rows], block[:, rows:]], axis=0)

    def lanes(part, pair):
        return pl.ds(pl.multiple_of(part * width + pair * PAIR, PAIR), PAIR)

    chunk = scores.shape[0]
    unroll = min(chunk, 4)

    def each(body):
        @pl.loop(0, chunk // unroll)
        def _(i):
            for inner in range(unroll):
                body(i * unroll + inner)

    for group in range(groups):
        here = pl.ds(group * rows, rows)

        @pl.loop(0, width // (PAIR * chunk))
        def _(part):
            def products(item):
                pair = part * chunk + item
                q_two = apart(proj[here, lanes(0, pair)] * DH ** (-0.5))
                scores[item] = dot(proj[here, lanes(1, pair)], q_two, NT)
                ga_two = apart(ga[here, lanes(0, pair)])
                gprobs[item] = dot(proj[here, lanes(2, pair)], ga_two, NT)

            def softmax(item):
                masked = scores[item] + bias[...]
                expanded = jnp.exp(masked - jnp.max(masked, axis=0, keepdims=True))
                probs = expanded * (1.0 / jnp.sum(expanded, axis=0, keepdims=True))
                low[item, 0] = probs.astype(jnp.bfloat16)
                weighted = probs * gprobs[item]
                delta = jnp.sum(weighted, axis=0, keepdims=True)
                low[item, 1] = (weighted - probs * delta).astype(jnp.bfloat16)

            def results(item):
                pair = part * chunk + item
                probs_low, grad_scores = low[item, 0], low[item, 1]
                q_two = apart(proj[here, lanes(0, pair)] * DH ** (-0.5))
                k_two = apart(proj[here, lanes(1, pair)])
                v_two = apart(proj[here, lanes(2, pair)])
                ga_two = apart(ga[here, lanes(0, pair)])
                att[here, lanes(0, pair)] = dot(stacked(probs_low), v_two, TN).astype(jnp.bfloat16)
                gproj[here, lanes(0, pair)] = (
                    dot(stacked(grad_scores), k_two, TN) * DH ** (-0.5)
                ).astype(jnp.bfloat16)
                gproj[here, lanes(1, pair)] = dot(grad_scores, q_two, NN).astype(jnp.bfloat16)
                gproj[here, lanes(2, pair)] = dot(probs_low, ga_two, NN).astype(jnp.bfloat16)

            each(products)
            each(softmax)
            each(results)

    def store(which, group, value):
        out_ref[:, which, group * SUB : (group + 1) * SUB, :] = value.reshape(frames, SUB, width)

    for group in range(groups):
        here = pl.ds(group * rows, rows)
        mixed = dot(att[here, :], w_out[...], NN)
        wide = load_rows(both_ref, 0, group).astype(jnp.float32)
        store(0, group, (wide + live * mixed).astype(jnp.bfloat16))

    wait(again)

    @pl.loop(0, width // step)
    def _(j):
        columns = pl.ds(pl.multiple_of(j * step, step), step)
        gnorm[:, columns] = dot(gproj[...], w_in[columns, :], NT)

    for group in range(groups):
        here = pl.ds(group * rows, rows)
        grad = gnorm[here, :] * gain_ref[...]
        scale = stats_ref[here, 1:2]
        hat = (load_rows(both_ref, 0, group).astype(jnp.float32) - stats_ref[here, 0:1]) * scale
        grad_rows = scale * (
            grad
            - jnp.mean(grad, axis=-1, keepdims=True)
            - hat * jnp.mean(grad * hat, axis=-1, keepdims=True)
        )
        cot = load_rows(both_ref, 1, group).astype(jnp.float32)
        store(1, group, (cot + grad_rows).astype(jnp.bfloat16))


def run_block(counts, gain, both, front_weights, late_weights, plan):
    frames, _, patches, width = both.shape
    total, rows = frames * patches, frames * SUB
    vmem = pl.BlockSpec(memory_space=pltpu.VMEM)
    smem = pl.BlockSpec(memory_space=pltpu.SMEM)
    anywhere = pl.BlockSpec(memory_space=pl.ANY)
    shape = jax.ShapeDtypeStruct
    params = pltpu.CompilerParams(vmem_limit_bytes=VMEM_LIMIT)
    front_columns = sum(size for _, _, size in plan["placed"])
    normed, stats, front = pl.pallas_call(
        functools.partial(front_kernel, plan),
        out_shape=(
            shape((total, width), jnp.bfloat16),
            shape((total, 128), jnp.float32),
            shape((total, front_columns), jnp.bfloat16),
        ),
        in_specs=[vmem, vmem] + [anywhere] * len(front_weights),
        out_specs=(vmem, vmem, vmem),
        scratch_shapes=[
            pltpu.VMEM((width, front_columns), jnp.bfloat16),
            pltpu.SemaphoreType.DMA((1,)),
        ],
        compiler_params=params,
        cost_estimate=pl.CostEstimate(
            flops=2 * total * width * front_columns,
            bytes_accessed=2 * width * front_columns + 8 * total * width,
            transcendentals=total,
        ),
        name="front",
    )(both, gain, *front_weights)
    chunk = 8 if rows <= 128 else 1
    return pl.pallas_call(
        functools.partial(main_kernel, plan),
        out_shape=shape(both.shape, jnp.bfloat16),
        in_specs=[smem, vmem, vmem, vmem, vmem, anywhere]
        + [anywhere] * (len(front_weights) + len(late_weights)),
        out_specs=vmem,
        scratch_shapes=[
            pltpu.VMEM((width, 3 * width), jnp.bfloat16),
            pltpu.VMEM((width, width), jnp.bfloat16),
            pltpu.VMEM((total, width), jnp.bfloat16),
            pltpu.VMEM((total, 3 * width), jnp.bfloat16),
            pltpu.VMEM((total, width), jnp.bfloat16),
            pltpu.VMEM((total, width), jnp.bfloat16),
            pltpu.VMEM((total, 3 * width), jnp.bfloat16),
            pltpu.VMEM((total, width), jnp.float32),
            pltpu.VMEM((rows, 2 * rows), jnp.float32),
            pltpu.VMEM((chunk, rows, 2 * rows), jnp.float32),
            pltpu.VMEM((chunk, rows, 2 * rows), jnp.float32),
            pltpu.VMEM((chunk, 2, rows, 2 * rows), jnp.bfloat16),
            pltpu.SemaphoreType.DMA((4,)),
        ],
        compiler_params=params,
        cost_estimate=pl.CostEstimate(
            flops=12 * total * width * width,
            bytes_accessed=8 * width * width + 8 * total * width,
            transcendentals=total * 2048,
        ),
        name="main",
    )(counts, gain, both, normed, stats, front, *front_weights, *late_weights)


def swap(array, distance, devices):
    return lax.ppermute(array, "frame", [(f, f ^ distance) for f in range(devices)])


def join_kernel(axis, *refs):
    *sources, target = refs
    start = 0
    for source in sources:
        end = start + source.shape[axis]
        if axis == 0:
            target[start:end, :] = source[...]
        else:
            target[:, start:end] = source[...]
        start = end


def join(axis, *arrays):
    shape = list(arrays[0].shape)
    shape[axis] = sum(array.shape[axis] for array in arrays)
    vmem = pl.BlockSpec(memory_space=pltpu.VMEM)
    return pl.pallas_call(
        functools.partial(join_kernel, axis),
        out_shape=jax.ShapeDtypeStruct(shape, arrays[0].dtype),
        in_specs=[vmem] * len(arrays),
        out_specs=vmem,
        name="join",
    )(*arrays)


def gather_two_ways(input_weights, output_weights, both, devices):
    depth, in_columns = input_weights.shape
    out_columns = output_weights.shape[1]
    early = in_columns * 2 // 3 // 128 * 128
    late = in_columns - early
    late_shard = join(1, output_weights, input_weights[:, early:])
    late_whole = lax.all_gather(late_shard, ("clip", "frame"), axis=0)
    late_whole = late_whole.reshape(4 * devices, depth, out_columns + late)

    shard = input_weights[:, :early]
    offsets = (0, 1, 3, 2)
    held = [shard] + [
        lax.ppermute(shard, "clip", [(c, c ^ offset) for c in range(4)]) for offset in offsets[1:]
    ]
    both, held[1] = lax.optimization_barrier((both, held[1]))
    both = lax.all_to_all(both, "frame", split_axis=0, concat_axis=0, tiled=True)
    own = join(0, *held)
    by_x, by_y = swap(own, 2, devices), swap(own, 4, devices)
    by_x, both = lax.optimization_barrier((by_x, both))
    middle = 2 * depth
    arrays = [own, by_x, by_y, swap(by_y[:middle], 2, devices), swap(by_x[middle:], 4, devices)]
    arrays += [swap(array, 1, devices) for array in arrays]

    def front(stride=early):
        clip, frame = lax.axis_index("clip"), lax.axis_index("frame")
        found = []
        for ref in range(10):
            distance = (0, 2, 4, 6, 6)[ref % 5] ^ (ref // 5)
            places = {3: (0, 1), 4: (2, 3)}.get(ref % 5, range(4))
            for order, place in enumerate(places):
                row = (frame ^ distance) * depth
                column = (clip ^ offsets[place]) * stride
                found.append((ref, None, order * depth, depth, (0, early), row, column))
        return found

    def pieces(first, size, stride, offset):
        return [
            (10, c * devices + f, 0, depth, (first, size), f * depth, c * stride + offset)
            for c in range(4)
            for f in range(devices)
        ]

    plan = {
        "front": front,
        "again": lambda: front(in_columns),
        "late": lambda: pieces(out_columns, late, in_columns, early),
        "outer": lambda: pieces(0, out_columns, out_columns, 0),
        "placed": [(c * early, c * in_columns, early) for c in range(4)],
        "missing": [(c * in_columns + early, late) for c in range(4)],
    }
    return arrays, [late_whole], plan, both


def gather_plainly(input_weights, output_weights, both):
    whole = []
    for weights in (input_weights, output_weights):
        columns = lax.all_gather(weights, "clip", axis=1, tiled=True)
        whole.append(lax.all_gather(columns, "frame", axis=0, tiled=True))
    both = lax.all_to_all(both, "frame", split_axis=0, concat_axis=0, tiled=True)
    inner, outer = [[(i, None, 0, w.shape[0], (0, w.shape[1]), 0, 0)] for i, w in enumerate(whole)]
    plan = {
        "front": lambda: inner,
        "again": lambda: inner,
        "late": lambda: [],
        "outer": lambda: outer,
        "placed": [(0, 0, whole[0].shape[1])],
        "missing": [],
    }
    return whole[:1], whole[1:], plan, both


def per_device(clips, devices, tokens, counts, norm_gain, input_weights, output_weights, cotangent):
    _, slots, patches, width = tokens.shape
    share = -(-patches // devices)
    share = -(-share // SUB) * SUB
    extra = devices * share - patches

    def by_destination(source):
        padded = jnp.pad(source[0], ((0, 0), (0, extra), (0, 0)))
        return padded.reshape(slots, devices, share, width).transpose(1, 0, 2, 3)

    both = jnp.stack([by_destination(tokens), by_destination(cotangent)], axis=2)
    depth, in_columns = input_weights.shape
    fits = in_columns % 384 == 0 and output_weights.shape[1] % 128 == 0 and depth % 16 == 0
    if clips == 4 and devices == 8 and fits:
        front, late, plan, both = gather_two_ways(input_weights, output_weights, both, devices)
    else:
        front, late, plan, both = gather_plainly(input_weights, output_weights, both)
    both = both.reshape(devices * slots, 2, share, width)
    back = run_block(counts, norm_gain.reshape(1, width), both, front, late, plan)
    back = back.reshape(devices, slots, 2, share, width)
    back = lax.all_to_all(back, "frame", split_axis=0, concat_axis=0, tiled=True)

    def in_order(which):
        rows = back[:, :, which].transpose(1, 0, 2, 3).reshape(slots, devices * share, width)
        return rows[None, :, :patches]

    return in_order(0), in_order(1)


def solution(mesh):
    in_specs = (
        P("clip", "frame", None, None),
        P("clip"),
        P(),
        P("frame", "clip"),
        P("frame", "clip"),
        P("clip", "frame", None, None),
    )
    out_specs = (P("clip", "frame", None, None), P("clip", "frame", None, None))
    body = functools.partial(per_device, mesh.shape["clip"], mesh.shape["frame"])
    return jax.shard_map(body, mesh=mesh, in_specs=in_specs, out_specs=out_specs, check_vma=False)
```

```python
import functools
import math

import jax
import jax.numpy as jnp
from jax import lax
from jax.experimental import pallas as pl
from jax.experimental.pallas import tpu as pltpu
from jax.sharding import PartitionSpec as P

DH = 64
PAIR = 2 * DH
SUB = 16
EPSILON = 1e-06
NEGATIVE = -1e30
NN = (((1,), (0,)), ((), ()))
NT = (((1,), (1,)), ((), ()))
TN = (((0,), (0,)), ((), ()))
VMEM_LIMIT = 27 * 1024 * 1024


def dot(a, b, dims):
    return lax.dot_general(a, b, dims, preferred_element_type=jnp.float32)


def fetch(parts, refs, target, sem):
    copies = []
    for ref, index, first, depth, lanes, row, column in parts:
        source = refs[ref] if index is None else refs[ref].at[index]
        copies.append(
            pltpu.make_async_copy(
                source.at[pl.ds(first, depth), pl.ds(*lanes)],
                target.at[
                    pl.ds(pl.multiple_of(row, 16), depth),
                    pl.ds(pl.multiple_of(column, 128), lanes[1]),
                ],
                sem,
            )
        )
    for copy in copies:
        copy.start()
    return copies


def wait(copies):
    for copy in copies:
        copy.wait()


def load_rows(ref, which, group):
    frames, _, _, width = ref.shape
    return ref[:, which, group * SUB : (group + 1) * SUB, :].reshape(frames * SUB, width)


def front_kernel(plan, *refs):
    gain_ref, *sources = refs[:-6]
    both_ref, normed_ref, stats_ref, proj_ref, w_front, sems = refs[-6:]
    copies = fetch(plan["front"](), sources, w_front, sems.at[0])
    plan["tokens"](sources, both_ref)
    frames, _, patches, _ = both_ref.shape
    rows = frames * SUB
    for group in range(patches // SUB):
        here = pl.ds(group * rows, rows)
        wide = load_rows(both_ref, 0, group).astype(jnp.float32)
        average = jnp.mean(wide, axis=-1, keepdims=True)
        centred = wide - average
        variance = jnp.mean(centred * centred, axis=-1, keepdims=True)
        scale = lax.rsqrt(variance + EPSILON)
        normed_ref[here, :] = (centred * scale * gain_ref[...]).astype(jnp.bfloat16)
        stats_ref[here, 0:1] = average
        stats_ref[here, 1:2] = scale
    wait(copies)
    columns = w_front.shape[1]
    step = math.gcd(columns, 512)

    @pl.loop(0, columns // step)
    def _(j):
        here = pl.ds(pl.multiple_of(j * step, step), step)
        proj_ref[:, here] = dot(normed_ref[...], w_front[:, here], NN).astype(jnp.bfloat16)


def main_kernel(plan, counts_ref, gain_ref, both_ref, normed_ref, stats_ref, front_ref, *rest):
    weight_refs = rest[:-14]
    out_ref, w_in, w_out, grads, proj, ga, att, gproj, gnorm, bias, scores, gprobs, low, sems = rest[-14:]
    frames, _, patches, width = both_ref.shape
    groups = patches // SUB
    rows = frames * SUB
    count = counts_ref[0]

    device = plan["device"]()
    place = [
        pltpu.make_async_copy(
            front_ref.at[:, pl.ds(start, size)],
            proj.at[:, pl.ds(pl.multiple_of(target, 128), size)],
            sems.at[3],
        )
        for start, target, size in plan["placed"]()
    ]
    for copy in place:
        copy.start()
    late = fetch(plan["late"](), weight_refs, w_in, sems.at[0])
    outer = fetch(plan["outer"](), weight_refs, w_out, sems.at[1])
    again = fetch(plan["again"](), weight_refs, w_in, sems.at[2])

    def real(index):
        return ((index // SUB) ^ device) < count

    live = real(lax.broadcasted_iota(jnp.int32, (rows, 1), 0)).astype(jnp.float32)
    for group in range(groups):
        here = pl.ds(group * rows, rows)
        grads[here, :] = (load_rows(both_ref, 1, group).astype(jnp.float32) * live).astype(
            jnp.bfloat16
        )
    key = lax.broadcasted_iota(jnp.int32, (rows, 2 * rows), 0)
    query = lax.broadcasted_iota(jnp.int32, (rows, 2 * rows), 1)
    bias[...] = jnp.where((query % SUB == key % SUB) & real(key), 0.0, NEGATIVE)
    lane = lax.broadcasted_iota(jnp.int32, (1, PAIR), 1)
    low_lanes = (lane < DH).astype(jnp.bfloat16)
    high_lanes = (lane >= DH).astype(jnp.bfloat16)

    wait(late)
    for start, size in plan["missing"]():
        columns = pl.ds(pl.multiple_of(start, 128), size)
        proj[:, columns] = dot(normed_ref[...], w_in[:, columns], NN).astype(jnp.bfloat16)

    wait(outer)
    step = min(width, 256)

    @pl.loop(0, width // step)
    def _(j):
        columns = pl.ds(pl.multiple_of(j * step, step), step)
        ga[:, columns] = dot(grads[...], w_out[columns, :], NT).astype(jnp.bfloat16)

    wait(place)

    def apart(block):
        return jnp.concatenate([block * low_lanes, block * high_lanes], axis=0)

    def stacked(block):
        return jnp.concatenate([block[:, :rows], block[:, rows:]], axis=0)

    def lanes(part, pair):
        return pl.ds(pl.multiple_of(part * width + pair * PAIR, PAIR), PAIR)

    chunk = scores.shape[0]
    unroll = min(chunk, 4)

    def each(body):
        @pl.loop(0, chunk // unroll)
        def _(i):
            for inner in range(unroll):
                body(i * unroll + inner)

    for group in range(groups):
        here = pl.ds(group * rows, rows)

        @pl.loop(0, width // (PAIR * chunk))
        def _(part):
            def products(item):
                pair = part * chunk + item
                q_two = apart(proj[here, lanes(0, pair)] * DH ** (-0.5))
                scores[item] = dot(proj[here, lanes(1, pair)], q_two, NT)
                ga_two = apart(ga[here, lanes(0, pair)])
                gprobs[item] = dot(proj[here, lanes(2, pair)], ga_two, NT)

            def softmax(item):
                masked = scores[item] + bias[...]
                expanded = jnp.exp(masked - jnp.max(masked, axis=0, keepdims=True))
                probs = expanded * (1.0 / jnp.sum(expanded, axis=0, keepdims=True))
                low[item, 0] = probs.astype(jnp.bfloat16)
                weighted = probs * gprobs[item]
                delta = jnp.sum(weighted, axis=0, keepdims=True)
                low[item, 1] = (weighted - probs * delta).astype(jnp.bfloat16)

            def results(item):
                pair = part * chunk + item
                probs_low, grad_scores = low[item, 0], low[item, 1]
                q_two = apart(proj[here, lanes(0, pair)] * DH ** (-0.5))
                k_two = apart(proj[here, lanes(1, pair)])
                v_two = apart(proj[here, lanes(2, pair)])
                ga_two = apart(ga[here, lanes(0, pair)])
                att[here, lanes(0, pair)] = dot(stacked(probs_low), v_two, TN).astype(jnp.bfloat16)
                gproj[here, lanes(0, pair)] = (
                    dot(stacked(grad_scores), k_two, TN) * DH ** (-0.5)
                ).astype(jnp.bfloat16)
                gproj[here, lanes(1, pair)] = dot(grad_scores, q_two, NN).astype(jnp.bfloat16)
                gproj[here, lanes(2, pair)] = dot(probs_low, ga_two, NN).astype(jnp.bfloat16)

            each(products)
            each(softmax)
            each(results)

    def store(which, group, value):
        for frame in range(frames):
            out_ref[pl.ds(frame ^ device, 1), which, group * SUB : (group + 1) * SUB, :] = value[
                frame * SUB : (frame + 1) * SUB
            ].reshape(1, SUB, width)

    for group in range(groups):
        here = pl.ds(group * rows, rows)
        mixed = dot(att[here, :], w_out[...], NN)
        wide = load_rows(both_ref, 0, group).astype(jnp.float32)
        store(0, group, (wide + live * mixed).astype(jnp.bfloat16))

    wait(again)

    @pl.loop(0, width // step)
    def _(j):
        columns = pl.ds(pl.multiple_of(j * step, step), step)
        gnorm[:, columns] = dot(gproj[...], w_in[columns, :], NT)

    for group in range(groups):
        here = pl.ds(group * rows, rows)
        grad = gnorm[here, :] * gain_ref[...]
        scale = stats_ref[here, 1:2]
        hat = (load_rows(both_ref, 0, group).astype(jnp.float32) - stats_ref[here, 0:1]) * scale
        grad_rows = scale * (
            grad
            - jnp.mean(grad, axis=-1, keepdims=True)
            - hat * jnp.mean(grad * hat, axis=-1, keepdims=True)
        )
        cot = load_rows(both_ref, 1, group).astype(jnp.float32)
        store(1, group, (cot + grad_rows).astype(jnp.bfloat16))


def run_front(gain, shape, sources, plan):
    frames, _, patches, width = shape
    total = frames * patches
    vmem = pl.BlockSpec(memory_space=pltpu.VMEM)
    anywhere = pl.BlockSpec(memory_space=pl.ANY)
    columns = plan["columns"]
    return pl.pallas_call(
        functools.partial(front_kernel, plan),
        out_shape=(
            jax.ShapeDtypeStruct(shape, jnp.bfloat16),
            jax.ShapeDtypeStruct((total, width), jnp.bfloat16),
            jax.ShapeDtypeStruct((total, 128), jnp.float32),
            jax.ShapeDtypeStruct((total, columns), jnp.bfloat16),
        ),
        in_specs=[vmem] + [anywhere if wide else vmem for wide in plan["spread"]],
        out_specs=(vmem, vmem, vmem, vmem),
        scratch_shapes=[
            pltpu.VMEM((width, columns), jnp.bfloat16),
            pltpu.SemaphoreType.DMA((1,)),
        ],
        compiler_params=pltpu.CompilerParams(vmem_limit_bytes=VMEM_LIMIT),
        cost_estimate=pl.CostEstimate(
            flops=2 * total * width * columns,
            bytes_accessed=2 * width * columns + 8 * total * width,
            transcendentals=total,
        ),
        name="front",
    )(gain, *sources)


def run_main(counts, gain, fronted, weights, plan):
    both, normed, stats, front = fronted
    frames, _, patches, width = both.shape
    total, rows = frames * patches, frames * SUB
    vmem = pl.BlockSpec(memory_space=pltpu.VMEM)
    smem = pl.BlockSpec(memory_space=pltpu.SMEM)
    anywhere = pl.BlockSpec(memory_space=pl.ANY)
    params = pltpu.CompilerParams(vmem_limit_bytes=VMEM_LIMIT if rows <= 128 else 2 * VMEM_LIMIT)
    chunk = 8 if rows <= 128 else 1
    return pl.pallas_call(
        functools.partial(main_kernel, plan),
        out_shape=jax.ShapeDtypeStruct(both.shape, jnp.bfloat16),
        in_specs=[smem, vmem, vmem, vmem, vmem, anywhere]
        + [anywhere] * len(weights),
        out_specs=vmem,
        scratch_shapes=[
            pltpu.VMEM((width, 3 * width), jnp.bfloat16),
            pltpu.VMEM((width, width), jnp.bfloat16),
            pltpu.VMEM((total, width), jnp.bfloat16),
            pltpu.VMEM((total, 3 * width), jnp.bfloat16),
            pltpu.VMEM((total, width), jnp.bfloat16),
            pltpu.VMEM((total, width), jnp.bfloat16),
            pltpu.VMEM((total, 3 * width), jnp.bfloat16),
            pltpu.VMEM((total, width), jnp.float32),
            pltpu.VMEM((rows, 2 * rows), jnp.float32),
            pltpu.VMEM((chunk, rows, 2 * rows), jnp.float32),
            pltpu.VMEM((chunk, rows, 2 * rows), jnp.float32),
            pltpu.VMEM((chunk, 2, rows, 2 * rows), jnp.bfloat16),
            pltpu.SemaphoreType.DMA((4,)),
        ],
        compiler_params=params,
        cost_estimate=pl.CostEstimate(
            flops=12 * total * width * width,
            bytes_accessed=8 * width * width + 8 * total * width,
            transcendentals=total * 2048,
        ),
        name="main",
    )(counts, gain, both, normed, stats, front, *weights)


def swap(array, distance, devices):
    return lax.ppermute(array, "frame", [(f, f ^ distance) for f in range(devices)])


def join_kernel(axis, *refs):
    *sources, target = refs
    start = 0
    for source in sources:
        end = start + source.shape[axis]
        if axis == 0:
            target[start:end, :] = source[...]
        else:
            target[:, start:end] = source[...]
        start = end


def join(axis, *arrays):
    shape = list(arrays[0].shape)
    shape[axis] = sum(array.shape[axis] for array in arrays)
    vmem = pl.BlockSpec(memory_space=pltpu.VMEM)
    return pl.pallas_call(
        functools.partial(join_kernel, axis),
        out_shape=jax.ShapeDtypeStruct(shape, arrays[0].dtype),
        in_specs=[vmem] * len(arrays),
        out_specs=vmem,
        name="join",
    )(*arrays)


def pack_kernel(patches, share, w_in, w_out, tokens, cot, joined, own, mine, to_x, to_y, held):
    depth = w_in.shape[0]
    half, block = depth // 2, 2 * share
    device = lax.axis_index("frame")
    chip, core = device // 2, device % 2
    joined[:, : w_in.shape[1]] = w_in[...]
    joined[:, w_in.shape[1] :] = w_out[...]
    held[...] = jnp.zeros_like(held)
    held[0, :patches] = tokens[0, 0]
    held[1, :patches] = cot[0, 0]

    def put(target, row, owner):
        rows = pl.ds(pl.multiple_of(owner * share, share), share)
        target[row : row + share, :] = held[0, rows, :]
        target[row + share : row + block, :] = held[1, rows, :]

    put(mine, 0, device)
    own[:depth, :] = joined[...]
    put(own, depth, device ^ 1)
    for target, first, last, away, core_by in ((to_x, 0, half, 1, 0), (to_y, half, 0, 2, 1)):
        target[:half, :] = joined[first : first + half, :]
        put(target, half, (chip ^ away) * 2)
        put(target, half + block, (chip ^ away) * 2 + 1)
        target[half + 2 * block : depth + 2 * block, :] = joined[last : last + half, :]
        put(target, depth + 2 * block, (chip ^ 3) * 2 + core_by)


def turn_kernel(half, by_x, by_y, pair_x, pair_y, to_dx, to_dy):
    to_dx[:half, :] = by_y[:half, :]
    to_dx[half:, :] = pair_y[: 2 * half, :]
    to_dy[:half, :] = by_x[half:, :]
    to_dy[half:, :] = pair_x[2 * half :, :]


def gather_in_rounds(input_weights, output_weights, tokens, cotangent, gain, share, devices):
    depth, in_columns = input_weights.shape
    out_columns = output_weights.shape[1]
    _, _, patches, width = tokens.shape
    half, block = depth // 2, 2 * share
    vmem = pl.BlockSpec(memory_space=pltpu.VMEM)

    def rows_of(count):
        return jax.ShapeDtypeStruct((count, width), jnp.bfloat16)

    joined, own, mine, to_x, to_y = pl.pallas_call(
        functools.partial(pack_kernel, patches, share),
        out_shape=tuple(
            map(rows_of, (depth, depth + block, block, depth + 3 * block, depth + 3 * block))
        ),
        in_specs=[vmem] * 4,
        out_specs=(vmem,) * 5,
        scratch_shapes=[pltpu.VMEM((2, devices * share, width), jnp.bfloat16)],
        name="pack",
    )(input_weights, output_weights, tokens, cotangent)

    def by_clip(array, offset):
        return lax.ppermute(array, "clip", [(c, c ^ offset) for c in range(4)])

    def across(array):
        return [swap(array, 2, devices), swap(array, 4, devices)]

    def other_core(arrays):
        return [swap(array, 1, devices) for array in arrays]

    one = by_clip(joined, 1)
    first = [swap(to_x, 2, devices), swap(to_y, 4, devices)]
    tail = half + 2 * block
    first += [swap(first[1][tail:], 2, devices), swap(first[0][tail:], 4, devices)]
    third = [by_clip(join(0, joined, one), 2)]
    second = [one, *across(one)]
    third[0], second[1], second[2] = lax.optimization_barrier((third[0], second[1], second[2]))
    first_other = other_core([own, *first])
    second_other = other_core(second)
    third[0], first[2], first[3] = lax.optimization_barrier((third[0], first[2], first[3]))
    ready = [joined, *first, *first_other, *second, *second_other]
    third += across(third[0])

    def tokens_in(sources, both_ref):
        core = lax.axis_index("frame") % 2
        mine_ref, _, x_ref, y_ref, dx_ref, dy_ref, own2, x2, y2, dx2, dy2 = sources[:11]
        rows = pl.ds(pl.multiple_of(half + core * block, block), block)
        behind = slice(half, half + block)

        def diagonal(by_x, by_y):
            return jnp.where(core == 0, by_y[behind, :], by_x[behind, :])

        found = (
            mine_ref[...], own2[depth : depth + block, :],
            x_ref[rows, :], x2[rows, :], y_ref[rows, :], y2[rows, :],
            diagonal(dx_ref, dy_ref), diagonal(dx2, dy2),
        )
        for distance, value in enumerate(found):
            both_ref[distance] = value.reshape(2, share, width)

    table = [
        [(0, 0, 0, depth, 0)],
        [(0, 2, 0, half, 0), (0, 2, tail, half, half)],
        [(0, 4, 0, half, half), (0, 4, tail, half, 0)],
        [(0, 6, 0, half, 0)],
        [(0, 6, 0, half, half)],
    ]
    others = [[(1, d, 0, depth, 0)] for d in (0, 2, 4)]
    pairs = [[(2, d, 0, depth, 0), (3, d, depth, depth, 0)] for d in (0, 2, 4)]
    pairs += [
        [(1, 6, 0, half, 0), (2, 6, half, depth, 0)],
        [(1, 6, 0, half, half), (3, 6, half, depth, 0)],
    ]
    arrays = []
    for group in (table, others, pairs):
        arrays += [(core, parts) for core in (0, 1) for parts in group]

    def pieces(offsets, lanes, base):
        clip, frame = lax.axis_index("clip"), lax.axis_index("frame")
        found = []
        for ref, (core, parts) in enumerate(arrays):
            for offset, distance, first, rows, inside in parts:
                if offset in offsets:
                    row = (frame ^ distance ^ core) * depth + inside
                    found.append((base + ref, None, first, rows, lanes, row, clip ^ offset))
        return found

    def placed(parts, stride):
        return [(*part[:-1], part[-1] * stride) for part in parts]

    def compact():
        return [(*part[:-1], 0) for part in pieces((0,), (0, in_columns), 1)]

    inner, outer = (0, in_columns), (in_columns, out_columns)

    def columns_of(offsets):
        clip = lax.axis_index("clip")
        return [(clip ^ offset) * in_columns for offset in offsets]

    plan = {
        "front": compact,
        "tokens": tokens_in,
        "columns": in_columns,
        "spread": [False] * 11,
        "device": lambda: lax.axis_index("frame"),
        "late": lambda: placed(pieces((1, 2, 3), inner, 0), in_columns),
        "again": lambda: placed(pieces((0,), inner, 0), in_columns),
        "outer": lambda: placed(pieces((0, 1, 2, 3), outer, 0), out_columns),
        "placed": lambda: [
            (0, start, in_columns) for start in columns_of((0,))
        ],
        "missing": lambda: [(start, in_columns) for start in columns_of((1, 2, 3))],
    }
    fronted = run_front(gain, (devices, 2, share, width), [mine, *ready[:10]], plan)
    third[1], *fronted = lax.optimization_barrier((third[1], *fronted))
    to_dx, to_dy = pl.pallas_call(
        functools.partial(turn_kernel, half),
        out_shape=(rows_of(depth + half), rows_of(depth + half)),
        in_specs=[vmem] * 4,
        out_specs=(vmem, vmem),
        name="turn",
    )(second[1], second[2], third[1], third[2])
    third += [swap(to_dx, 2, devices), swap(to_dy, 4, devices)]
    third += other_core(third)
    return fronted, [*ready, *third], plan


def gather_plainly(input_weights, output_weights, tokens, cotangent, gain, share, devices):
    _, slots, patches, width = tokens.shape
    whole = []
    for weights in (input_weights, output_weights):
        columns = lax.all_gather(weights, "clip", axis=1, tiled=True)
        whole.append(lax.all_gather(columns, "frame", axis=0, tiled=True))

    def by_destination(source):
        padded = jnp.pad(source[0], ((0, 0), (0, devices * share - patches), (0, 0)))
        return padded.reshape(slots, devices, share, width).transpose(1, 0, 2, 3)

    both = jnp.stack([by_destination(tokens), by_destination(cotangent)], axis=2)
    both = lax.all_to_all(both, "frame", split_axis=0, concat_axis=0, tiled=True)
    both = both.reshape(devices * slots, 2, share, width)

    def tokens_in(sources, both_ref):
        both_ref[...] = sources[1][...]

    inner, outer = [[(i, None, 0, w.shape[0], (0, w.shape[1]), 0, 0)] for i, w in enumerate(whole)]
    plan = {
        "front": lambda: inner,
        "tokens": tokens_in,
        "columns": whole[0].shape[1],
        "spread": [True, False],
        "device": lambda: 0,
        "late": lambda: [],
        "again": lambda: inner,
        "outer": lambda: outer,
        "placed": lambda: [(0, 0, whole[0].shape[1])],
        "missing": lambda: [],
    }
    return run_front(gain, both.shape, [whole[0], both], plan), whole, plan


def per_device(clips, devices, tokens, counts, norm_gain, input_weights, output_weights, cotangent):
    _, slots, patches, width = tokens.shape
    share = -(-patches // devices)
    share = -(-share // SUB) * SUB
    depth, in_columns = input_weights.shape
    fits = in_columns % 128 == 0 and output_weights.shape[1] % 128 == 0 and depth % 32 == 0
    small = clips == 4 and devices == 8 and slots == 1 and fits
    gather = gather_in_rounds if small else gather_plainly
    gain = norm_gain.reshape(1, width)
    fronted, weights, plan = gather(
        input_weights, output_weights, tokens, cotangent, gain, share, devices
    )
    back = run_main(counts, gain, fronted, weights, plan)
    back = back.reshape(devices, slots, 2, share, width)
    back = lax.all_to_all(back, "frame", split_axis=0, concat_axis=0, tiled=True)

    def in_order(which):
        rows = back[:, :, which].transpose(1, 0, 2, 3).reshape(slots, devices * share, width)
        return rows[None, :, :patches]

    return in_order(0), in_order(1)


def solution(mesh):
    in_specs = (
        P("clip", "frame", None, None),
        P("clip"),
        P(),
        P("frame", "clip"),
        P("frame", "clip"),
        P("clip", "frame", None, None),
    )
    out_specs = (P("clip", "frame", None, None), P("clip", "frame", None, None))
    body = functools.partial(per_device, mesh.shape["clip"], mesh.shape["frame"])
    return jax.shard_map(body, mesh=mesh, in_specs=in_specs, out_specs=out_specs, check_vma=False)
```

```python
import functools
import math

import jax
import jax.numpy as jnp
from jax import lax
from jax.experimental import pallas as pl
from jax.experimental.pallas import tpu as pltpu
from jax.sharding import PartitionSpec as P

DH = 64
PAIR = 2 * DH
SUB = 16
EPSILON = 1e-06
NEGATIVE = -1e30
NN = (((1,), (0,)), ((), ()))
NT = (((1,), (1,)), ((), ()))
TN = (((0,), (0,)), ((), ()))
VMEM_LIMIT = 27 * 1024 * 1024
SMALL = pltpu.CompilerParams(vmem_limit_bytes=6 * 1024 * 1024)


def dot(a, b, dims):
    return lax.dot_general(a, b, dims, preferred_element_type=jnp.float32)


def fetch(parts, refs, target, sem):
    copies = []
    for ref, index, first, depth, lanes, row, column in parts:
        source = refs[ref] if index is None else refs[ref].at[index]
        copies.append(
            pltpu.make_async_copy(
                source.at[pl.ds(first, depth), pl.ds(*lanes)],
                target.at[
                    pl.ds(pl.multiple_of(row, 16), depth),
                    pl.ds(pl.multiple_of(column, 128), lanes[1]),
                ],
                sem,
            )
        )
    for copy in copies:
        copy.start()
    return copies


def wait(copies):
    for copy in copies:
        copy.wait()


def load_rows(ref, which, group):
    frames, _, _, width = ref.shape
    return ref[:, which, group * SUB : (group + 1) * SUB, :].reshape(frames * SUB, width)


def front_kernel(plan, *refs):
    gain_ref, *sources = refs[:-6]
    both_ref, normed_ref, stats_ref, proj_ref, w_front, sems = refs[-6:]
    copies = fetch(plan["front"](), sources, w_front, sems.at[0])
    plan["tokens"](sources, both_ref)
    frames, _, patches, _ = both_ref.shape
    rows = frames * SUB
    for group in range(patches // SUB):
        here = pl.ds(group * rows, rows)
        wide = load_rows(both_ref, 0, group).astype(jnp.float32)
        average = jnp.mean(wide, axis=-1, keepdims=True)
        centred = wide - average
        variance = jnp.mean(centred * centred, axis=-1, keepdims=True)
        scale = lax.rsqrt(variance + EPSILON)
        normed_ref[here, :] = (centred * scale * gain_ref[...]).astype(jnp.bfloat16)
        stats_ref[here, 0:1] = average
        stats_ref[here, 1:2] = scale
    wait(copies)
    columns = w_front.shape[1]
    step = math.gcd(columns, 512)

    @pl.loop(0, columns // step)
    def _(j):
        here = pl.ds(pl.multiple_of(j * step, step), step)
        proj_ref[:, here] = dot(normed_ref[...], w_front[:, here], NN).astype(jnp.bfloat16)


def main_kernel(plan, counts_ref, gain_ref, both_ref, normed_ref, stats_ref, front_ref, *rest):
    weight_refs = rest[:-14]
    out_ref, w_in, w_out, grads, proj, ga, att, gproj, gnorm, bias, scores, gprobs, low, sems = rest[-14:]
    frames, _, patches, width = both_ref.shape
    groups = patches // SUB
    rows = frames * SUB
    count = counts_ref[0]

    device = plan["device"]()
    place = [
        pltpu.make_async_copy(
            front_ref.at[:, pl.ds(start, size)],
            proj.at[:, pl.ds(pl.multiple_of(target, 128), size)],
            sems.at[3],
        )
        for start, target, size in plan["placed"]()
    ]
    for copy in place:
        copy.start()
    late = fetch(plan["late"](), weight_refs, w_in, sems.at[0])
    outer = fetch(plan["outer"](), weight_refs, w_out, sems.at[1])
    again = fetch(plan["again"](), weight_refs, w_in, sems.at[2])

    def real(index):
        return ((index // SUB) ^ device) < count

    live = real(lax.broadcasted_iota(jnp.int32, (rows, 1), 0)).astype(jnp.float32)
    for group in range(groups):
        here = pl.ds(group * rows, rows)
        grads[here, :] = (load_rows(both_ref, 1, group).astype(jnp.float32) * live).astype(
            jnp.bfloat16
        )
    key = lax.broadcasted_iota(jnp.int32, (rows, 2 * rows), 0)
    query = lax.broadcasted_iota(jnp.int32, (rows, 2 * rows), 1)
    bias[...] = jnp.where((query % SUB == key % SUB) & real(key), 0.0, NEGATIVE)
    lane = lax.broadcasted_iota(jnp.int32, (1, PAIR), 1)
    low_lanes = (lane < DH).astype(jnp.bfloat16)
    high_lanes = (lane >= DH).astype(jnp.bfloat16)

    wait(late)
    for start, size in plan["missing"]():
        columns = pl.ds(pl.multiple_of(start, 128), size)
        proj[:, columns] = dot(normed_ref[...], w_in[:, columns], NN).astype(jnp.bfloat16)

    wait(outer)
    step = min(width, 256)

    @pl.loop(0, width // step)
    def _(j):
        columns = pl.ds(pl.multiple_of(j * step, step), step)
        ga[:, columns] = dot(grads[...], w_out[columns, :], NT).astype(jnp.bfloat16)

    wait(place)

    def apart(block):
        return jnp.concatenate([block * low_lanes, block * high_lanes], axis=0)

    def stacked(block):
        return jnp.concatenate([block[:, :rows], block[:, rows:]], axis=0)

    def lanes(part, pair):
        return pl.ds(pl.multiple_of(part * width + pair * PAIR, PAIR), PAIR)

    chunk = scores.shape[0]
    unroll = min(chunk, 4)

    def each(body):
        @pl.loop(0, chunk // unroll)
        def _(i):
            for inner in range(unroll):
                body(i * unroll + inner)

    for group in range(groups):
        here = pl.ds(group * rows, rows)

        @pl.loop(0, width // (PAIR * chunk))
        def _(part):
            def products(item):
                pair = part * chunk + item
                q_two = apart(proj[here, lanes(0, pair)] * DH ** (-0.5))
                scores[item] = dot(proj[here, lanes(1, pair)], q_two, NT)
                ga_two = apart(ga[here, lanes(0, pair)])
                gprobs[item] = dot(proj[here, lanes(2, pair)], ga_two, NT)

            def softmax(item):
                masked = scores[item] + bias[...]
                expanded = jnp.exp(masked - jnp.max(masked, axis=0, keepdims=True))
                probs = expanded * (1.0 / jnp.sum(expanded, axis=0, keepdims=True))
                low[item, 0] = probs.astype(jnp.bfloat16)
                weighted = probs * gprobs[item]
                delta = jnp.sum(weighted, axis=0, keepdims=True)
                low[item, 1] = (weighted - probs * delta).astype(jnp.bfloat16)

            def results(item):
                pair = part * chunk + item
                probs_low, grad_scores = low[item, 0], low[item, 1]
                q_two = apart(proj[here, lanes(0, pair)] * DH ** (-0.5))
                k_two = apart(proj[here, lanes(1, pair)])
                v_two = apart(proj[here, lanes(2, pair)])
                ga_two = apart(ga[here, lanes(0, pair)])
                att[here, lanes(0, pair)] = dot(stacked(probs_low), v_two, TN).astype(jnp.bfloat16)
                gproj[here, lanes(0, pair)] = (
                    dot(stacked(grad_scores), k_two, TN) * DH ** (-0.5)
                ).astype(jnp.bfloat16)
                gproj[here, lanes(1, pair)] = dot(grad_scores, q_two, NN).astype(jnp.bfloat16)
                gproj[here, lanes(2, pair)] = dot(probs_low, ga_two, NN).astype(jnp.bfloat16)

            each(products)
            each(softmax)
            each(results)

    def store(which, group, value):
        for frame in range(frames):
            out_ref[pl.ds(frame ^ device, 1), which, group * SUB : (group + 1) * SUB, :] = value[
                frame * SUB : (frame + 1) * SUB
            ].reshape(1, SUB, width)

    for group in range(groups):
        here = pl.ds(group * rows, rows)
        mixed = dot(att[here, :], w_out[...], NN)
        wide = load_rows(both_ref, 0, group).astype(jnp.float32)
        store(0, group, (wide + live * mixed).astype(jnp.bfloat16))

    wait(again)

    @pl.loop(0, width // step)
    def _(j):
        columns = pl.ds(pl.multiple_of(j * step, step), step)
        gnorm[:, columns] = dot(gproj[...], w_in[columns, :], NT)

    for group in range(groups):
        here = pl.ds(group * rows, rows)
        grad = gnorm[here, :] * gain_ref[...]
        scale = stats_ref[here, 1:2]
        hat = (load_rows(both_ref, 0, group).astype(jnp.float32) - stats_ref[here, 0:1]) * scale
        grad_rows = scale * (
            grad
            - jnp.mean(grad, axis=-1, keepdims=True)
            - hat * jnp.mean(grad * hat, axis=-1, keepdims=True)
        )
        cot = load_rows(both_ref, 1, group).astype(jnp.float32)
        store(1, group, (cot + grad_rows).astype(jnp.bfloat16))


def run_front(gain, shape, sources, plan):
    frames, _, patches, width = shape
    total = frames * patches
    vmem = pl.BlockSpec(memory_space=pltpu.VMEM)
    anywhere = pl.BlockSpec(memory_space=pl.ANY)
    columns = plan["columns"]
    return pl.pallas_call(
        functools.partial(front_kernel, plan),
        out_shape=(
            jax.ShapeDtypeStruct(shape, jnp.bfloat16),
            jax.ShapeDtypeStruct((total, width), jnp.bfloat16),
            jax.ShapeDtypeStruct((total, 128), jnp.float32),
            jax.ShapeDtypeStruct((total, columns), jnp.bfloat16),
        ),
        in_specs=[vmem] + [anywhere if wide else vmem for wide in plan["spread"]],
        out_specs=(vmem, vmem, vmem, vmem),
        scratch_shapes=[
            pltpu.VMEM((width, columns), jnp.bfloat16),
            pltpu.SemaphoreType.DMA((1,)),
        ],
        compiler_params=pltpu.CompilerParams(vmem_limit_bytes=VMEM_LIMIT),
        cost_estimate=pl.CostEstimate(
            flops=2 * total * width * columns,
            bytes_accessed=2 * width * columns + 8 * total * width,
            transcendentals=total,
        ),
        name="front",
    )(gain, *sources)


def run_main(counts, gain, fronted, weights, plan):
    both, normed, stats, front = fronted
    frames, _, patches, width = both.shape
    total, rows = frames * patches, frames * SUB
    vmem = pl.BlockSpec(memory_space=pltpu.VMEM)
    smem = pl.BlockSpec(memory_space=pltpu.SMEM)
    anywhere = pl.BlockSpec(memory_space=pl.ANY)
    params = pltpu.CompilerParams(vmem_limit_bytes=VMEM_LIMIT if rows <= 128 else 2 * VMEM_LIMIT)
    chunk = 8 if rows <= 128 else 1
    return pl.pallas_call(
        functools.partial(main_kernel, plan),
        out_shape=jax.ShapeDtypeStruct(both.shape, jnp.bfloat16),
        in_specs=[smem, vmem, vmem, vmem, vmem, anywhere]
        + [anywhere] * len(weights),
        out_specs=vmem,
        scratch_shapes=[
            pltpu.VMEM((width, 3 * width), jnp.bfloat16),
            pltpu.VMEM((width, width), jnp.bfloat16),
            pltpu.VMEM((total, width), jnp.bfloat16),
            pltpu.VMEM((total, 3 * width), jnp.bfloat16),
            pltpu.VMEM((total, width), jnp.bfloat16),
            pltpu.VMEM((total, width), jnp.bfloat16),
            pltpu.VMEM((total, 3 * width), jnp.bfloat16),
            pltpu.VMEM((total, width), jnp.float32),
            pltpu.VMEM((rows, 2 * rows), jnp.float32),
            pltpu.VMEM((chunk, rows, 2 * rows), jnp.float32),
            pltpu.VMEM((chunk, rows, 2 * rows), jnp.float32),
            pltpu.VMEM((chunk, 2, rows, 2 * rows), jnp.bfloat16),
            pltpu.SemaphoreType.DMA((4,)),
        ],
        compiler_params=params,
        cost_estimate=pl.CostEstimate(
            flops=12 * total * width * width,
            bytes_accessed=8 * width * width + 8 * total * width,
            transcendentals=total * 2048,
        ),
        name="main",
    )(counts, gain, both, normed, stats, front, *weights)


def swap(array, distance, devices):
    return lax.ppermute(array, "frame", [(f, f ^ distance) for f in range(devices)])


def join_kernel(axis, *refs):
    *sources, target = refs
    start = 0
    for source in sources:
        end = start + source.shape[axis]
        if axis == 0:
            target[start:end, :] = source[...]
        else:
            target[:, start:end] = source[...]
        start = end


def join(axis, *arrays):
    shape = list(arrays[0].shape)
    shape[axis] = sum(array.shape[axis] for array in arrays)
    vmem = pl.BlockSpec(memory_space=pltpu.VMEM)
    return pl.pallas_call(
        functools.partial(join_kernel, axis),
        out_shape=jax.ShapeDtypeStruct(shape, arrays[0].dtype),
        in_specs=[vmem] * len(arrays),
        out_specs=vmem,
        compiler_params=SMALL,
        name="join",
    )(*arrays)


def pack_kernel(patches, share, w_in, w_out, tokens, cot, joined, own, mine, to_x, to_y, held):
    depth = w_in.shape[0]
    half, block = depth // 2, 2 * share
    device = lax.axis_index("frame")
    chip, core = device // 2, device % 2
    joined[:, : w_in.shape[1]] = w_in[...]
    joined[:, w_in.shape[1] :] = w_out[...]
    held[...] = jnp.zeros_like(held)
    held[0, :patches] = tokens[0, 0]
    held[1, :patches] = cot[0, 0]

    def put(target, row, owner):
        rows = pl.ds(pl.multiple_of(owner * share, share), share)
        target[row : row + share, :] = held[0, rows, :]
        target[row + share : row + block, :] = held[1, rows, :]

    put(mine, 0, device)
    own[:depth, :] = joined[...]
    put(own, depth, device ^ 1)
    for target, first, last, away, core_by in ((to_x, 0, half, 1, 0), (to_y, half, 0, 2, 1)):
        target[:half, :] = joined[first : first + half, :]
        put(target, half, (chip ^ away) * 2)
        put(target, half + block, (chip ^ away) * 2 + 1)
        target[half + 2 * block : depth + 2 * block, :] = joined[last : last + half, :]
        put(target, depth + 2 * block, (chip ^ 3) * 2 + core_by)


def turn_kernel(half, by_x, by_y, pair_x, pair_y, to_dx, to_dy):
    to_dx[:half, :] = by_y[:half, :]
    to_dx[half:, :] = pair_y[: 2 * half, :]
    to_dy[:half, :] = by_x[half:, :]
    to_dy[half:, :] = pair_x[2 * half :, :]


def gather_in_rounds(input_weights, output_weights, tokens, cotangent, gain, share, devices):
    depth, in_columns = input_weights.shape
    out_columns = output_weights.shape[1]
    _, _, patches, width = tokens.shape
    half, block = depth // 2, 2 * share
    vmem = pl.BlockSpec(memory_space=pltpu.VMEM)

    def rows_of(count):
        return jax.ShapeDtypeStruct((count, width), jnp.bfloat16)

    joined, own, mine, to_x, to_y = pl.pallas_call(
        functools.partial(pack_kernel, patches, share),
        out_shape=tuple(
            map(rows_of, (depth, depth + block, block, depth + 3 * block, depth + 3 * block))
        ),
        in_specs=[vmem] * 4,
        out_specs=(vmem,) * 5,
        scratch_shapes=[pltpu.VMEM((2, devices * share, width), jnp.bfloat16)],
        compiler_params=SMALL,
        name="pack",
    )(input_weights, output_weights, tokens, cotangent)

    def by_clip(array, offset):
        return lax.ppermute(array, "clip", [(c, c ^ offset) for c in range(4)])

    def across(array):
        return [swap(array, 2, devices), swap(array, 4, devices)]

    def other_core(arrays):
        return [swap(array, 1, devices) for array in arrays]

    one, two = by_clip(joined, 1), by_clip(joined, 2)
    source, two = lax.optimization_barrier((joined, two))
    three = by_clip(source, 3)
    first = [swap(to_x, 2, devices), swap(to_y, 4, devices)]
    tail = half + 2 * block
    first += [swap(first[1][tail:], 2, devices), swap(first[0][tail:], 4, devices)]
    one, first[0], first[1] = lax.optimization_barrier((one, first[0], first[1]))
    second = [one, *across(one)]
    two, three, first[2], first[3], second[1], second[2] = lax.optimization_barrier(
        (two, three, first[2], first[3], second[1], second[2])
    )
    third = [join(0, two, three)]
    own, first[2] = lax.optimization_barrier((own, first[2]))
    first_other = other_core([own, *first])
    second_other = other_core(second)
    ready = [joined, *first, *first_other, *second, *second_other]
    third += across(third[0])

    def tokens_in(sources, both_ref):
        core = lax.axis_index("frame") % 2
        mine_ref, _, x_ref, y_ref, dx_ref, dy_ref, own2, x2, y2, dx2, dy2 = sources[:11]
        rows = pl.ds(pl.multiple_of(half + core * block, block), block)
        behind = slice(half, half + block)

        def diagonal(by_x, by_y):
            return jnp.where(core == 0, by_y[behind, :], by_x[behind, :])

        found = (
            mine_ref[...], own2[depth : depth + block, :],
            x_ref[rows, :], x2[rows, :], y_ref[rows, :], y2[rows, :],
            diagonal(dx_ref, dy_ref), diagonal(dx2, dy2),
        )
        for distance, value in enumerate(found):
            both_ref[distance] = value.reshape(2, share, width)

    table = [
        [(0, 0, 0, depth, 0)],
        [(0, 2, 0, half, 0), (0, 2, tail, half, half)],
        [(0, 4, 0, half, half), (0, 4, tail, half, 0)],
        [(0, 6, 0, half, 0)],
        [(0, 6, 0, half, half)],
    ]
    others = [[(1, d, 0, depth, 0)] for d in (0, 2, 4)]
    pairs = [[(2, d, 0, depth, 0), (3, d, depth, depth, 0)] for d in (0, 2, 4)]
    pairs += [
        [(1, 6, 0, half, 0), (2, 6, half, depth, 0)],
        [(1, 6, 0, half, half), (3, 6, half, depth, 0)],
    ]
    arrays = []
    for group in (table, others, pairs):
        arrays += [(core, parts) for core in (0, 1) for parts in group]

    def pieces(offsets, lanes, base):
        clip, frame = lax.axis_index("clip"), lax.axis_index("frame")
        found = []
        for ref, (core, parts) in enumerate(arrays):
            for offset, distance, first, rows, inside in parts:
                if offset in offsets:
                    row = (frame ^ distance ^ core) * depth + inside
                    found.append((base + ref, None, first, rows, lanes, row, clip ^ offset))
        return found

    def placed(parts, stride):
        return [(*part[:-1], part[-1] * stride) for part in parts]

    def compact():
        return [(*part[:-1], 0) for part in pieces((0,), (0, in_columns), 1)]

    inner, outer = (0, in_columns), (in_columns, out_columns)

    def columns_of(offsets):
        clip = lax.axis_index("clip")
        return [(clip ^ offset) * in_columns for offset in offsets]

    plan = {
        "front": compact,
        "tokens": tokens_in,
        "columns": in_columns,
        "spread": [False] * 11,
        "device": lambda: lax.axis_index("frame"),
        "late": lambda: placed(pieces((1, 2, 3), inner, 0), in_columns),
        "again": lambda: placed(pieces((0,), inner, 0), in_columns),
        "outer": lambda: placed(pieces((0, 1, 2, 3), outer, 0), out_columns),
        "placed": lambda: [
            (0, start, in_columns) for start in columns_of((0,))
        ],
        "missing": lambda: [(start, in_columns) for start in columns_of((1, 2, 3))],
    }
    fronted = run_front(gain, (devices, 2, share, width), [mine, *ready[:10]], plan)
    third[1], *fronted = lax.optimization_barrier((third[1], *fronted))
    to_dx, to_dy = pl.pallas_call(
        functools.partial(turn_kernel, half),
        out_shape=(rows_of(depth + half), rows_of(depth + half)),
        in_specs=[vmem] * 4,
        out_specs=(vmem, vmem),
        compiler_params=SMALL,
        name="turn",
    )(second[1], second[2], third[1], third[2])
    third += [swap(to_dx, 2, devices), swap(to_dy, 4, devices)]
    third += other_core(third)
    return fronted, [*ready, *third], plan


def gather_plainly(input_weights, output_weights, tokens, cotangent, gain, share, devices):
    _, slots, patches, width = tokens.shape
    whole = []
    for weights in (input_weights, output_weights):
        columns = lax.all_gather(weights, "clip", axis=1, tiled=True)
        whole.append(lax.all_gather(columns, "frame", axis=0, tiled=True))

    def by_destination(source):
        padded = jnp.pad(source[0], ((0, 0), (0, devices * share - patches), (0, 0)))
        return padded.reshape(slots, devices, share, width).transpose(1, 0, 2, 3)

    both = jnp.stack([by_destination(tokens), by_destination(cotangent)], axis=2)
    both = lax.all_to_all(both, "frame", split_axis=0, concat_axis=0, tiled=True)
    both = both.reshape(devices * slots, 2, share, width)

    def tokens_in(sources, both_ref):
        both_ref[...] = sources[1][...]

    inner, outer = [[(i, None, 0, w.shape[0], (0, w.shape[1]), 0, 0)] for i, w in enumerate(whole)]
    plan = {
        "front": lambda: inner,
        "tokens": tokens_in,
        "columns": whole[0].shape[1],
        "spread": [True, False],
        "device": lambda: 0,
        "late": lambda: [],
        "again": lambda: inner,
        "outer": lambda: outer,
        "placed": lambda: [(0, 0, whole[0].shape[1])],
        "missing": lambda: [],
    }
    return run_front(gain, both.shape, [whole[0], both], plan), whole, plan


def per_device(clips, devices, tokens, counts, norm_gain, input_weights, output_weights, cotangent):
    _, slots, patches, width = tokens.shape
    share = -(-patches // devices)
    share = -(-share // SUB) * SUB
    depth, in_columns = input_weights.shape
    fits = in_columns % 128 == 0 and output_weights.shape[1] % 128 == 0 and depth % 32 == 0
    small = clips == 4 and devices == 8 and slots == 1 and fits
    gather = gather_in_rounds if small else gather_plainly
    gain = norm_gain.reshape(1, width)
    fronted, weights, plan = gather(
        input_weights, output_weights, tokens, cotangent, gain, share, devices
    )
    back = run_main(counts, gain, fronted, weights, plan)
    back = back.reshape(devices, slots, 2, share, width)
    back = lax.all_to_all(back, "frame", split_axis=0, concat_axis=0, tiled=True)

    def in_order(which):
        rows = back[:, :, which].transpose(1, 0, 2, 3).reshape(slots, devices * share, width)
        return rows[None, :, :patches]

    return in_order(0), in_order(1)


def solution(mesh):
    in_specs = (
        P("clip", "frame", None, None),
        P("clip"),
        P(),
        P("frame", "clip"),
        P("frame", "clip"),
        P("clip", "frame", None, None),
    )
    out_specs = (P("clip", "frame", None, None), P("clip", "frame", None, None))
    body = functools.partial(per_device, mesh.shape["clip"], mesh.shape["frame"])
    return jax.shard_map(body, mesh=mesh, in_specs=in_specs, out_specs=out_specs, check_vma=False)
```

```python
import functools
import math

import jax
import jax.numpy as jnp
from jax import lax
from jax.experimental import pallas as pl
from jax.experimental.pallas import tpu as pltpu
from jax.sharding import PartitionSpec as P

DH = 64
PAIR = 2 * DH
SUB = 16
EPSILON = 1e-06
NEGATIVE = -1e30
NN = (((1,), (0,)), ((), ()))
NT = (((1,), (1,)), ((), ()))
TN = (((0,), (0,)), ((), ()))
VMEM_LIMIT = 27 * 1024 * 1024
SMALL = pltpu.CompilerParams(vmem_limit_bytes=6 * 1024 * 1024)


def dot(a, b, dims):
    return lax.dot_general(a, b, dims, preferred_element_type=jnp.float32)


def fetch(parts, refs, target, sem):
    copies = []
    for ref, index, first, depth, lanes, row, column in parts:
        source = refs[ref] if index is None else refs[ref].at[index]
        copies.append(
            pltpu.make_async_copy(
                source.at[pl.ds(first, depth), pl.ds(*lanes)],
                target.at[
                    pl.ds(pl.multiple_of(row, 16), depth),
                    pl.ds(pl.multiple_of(column, 128), lanes[1]),
                ],
                sem,
            )
        )
    for copy in copies:
        copy.start()
    return copies


def wait(copies):
    for copy in copies:
        copy.wait()


def load_rows(ref, which, group):
    frames, _, _, width = ref.shape
    return ref[:, which, group * SUB : (group + 1) * SUB, :].reshape(frames * SUB, width)


def front_kernel(plan, *refs):
    gain_ref, *sources = refs[:-6]
    both_ref, normed_ref, stats_ref, proj_ref, w_front, sems = refs[-6:]
    copies = fetch(plan["front"](), sources, w_front, sems.at[0])
    plan["tokens"](sources, both_ref)
    frames, _, patches, _ = both_ref.shape
    rows = frames * SUB
    for group in range(patches // SUB):
        here = pl.ds(group * rows, rows)
        wide = load_rows(both_ref, 0, group).astype(jnp.float32)
        average = jnp.mean(wide, axis=-1, keepdims=True)
        centred = wide - average
        variance = jnp.mean(centred * centred, axis=-1, keepdims=True)
        scale = lax.rsqrt(variance + EPSILON)
        normed_ref[here, :] = (centred * scale * gain_ref[...]).astype(jnp.bfloat16)
        stats_ref[here, 0:1] = average
        stats_ref[here, 1:2] = scale
    wait(copies)
    columns = w_front.shape[1]
    step = math.gcd(columns, 512)

    @pl.loop(0, columns // step)
    def _(j):
        here = pl.ds(pl.multiple_of(j * step, step), step)
        proj_ref[:, here] = dot(normed_ref[...], w_front[:, here], NN).astype(jnp.bfloat16)


def main_kernel(plan, counts_ref, gain_ref, both_ref, normed_ref, stats_ref, front_ref, *rest):
    weight_refs = rest[:-14]
    out_ref, w_in, w_out, grads, proj, ga, att, gproj, gnorm, bias, scores, gprobs, low, sems = rest[-14:]
    frames, _, patches, width = both_ref.shape
    groups = patches // SUB
    rows = frames * SUB
    count = counts_ref[0]

    device = plan["device"]()
    place = [
        pltpu.make_async_copy(
            front_ref.at[:, pl.ds(start, size)],
            proj.at[:, pl.ds(pl.multiple_of(target, 128), size)],
            sems.at[3],
        )
        for start, target, size in plan["placed"]()
    ]
    for copy in place:
        copy.start()
    outer = fetch(plan["outer"](), weight_refs, w_out, sems.at[1])
    late = [
        fetch(parts, weight_refs, w_in, sems.at[4 + i]) for i, parts in enumerate(plan["late"]())
    ]
    again = fetch(plan["again"](), weight_refs, w_in, sems.at[2])

    def real(index):
        return ((index // SUB) ^ device) < count

    live = real(lax.broadcasted_iota(jnp.int32, (rows, 1), 0)).astype(jnp.float32)
    for group in range(groups):
        here = pl.ds(group * rows, rows)
        grads[here, :] = (load_rows(both_ref, 1, group).astype(jnp.float32) * live).astype(
            jnp.bfloat16
        )
    key = lax.broadcasted_iota(jnp.int32, (rows, 2 * rows), 0)
    query = lax.broadcasted_iota(jnp.int32, (rows, 2 * rows), 1)
    bias[...] = jnp.where((query % SUB == key % SUB) & real(key), 0.0, NEGATIVE)
    lane = lax.broadcasted_iota(jnp.int32, (1, PAIR), 1)
    low_lanes = (lane < DH).astype(jnp.bfloat16)
    high_lanes = (lane >= DH).astype(jnp.bfloat16)

    wait(outer)
    step = min(width, 256)

    @pl.loop(0, width // step)
    def _(j):
        columns = pl.ds(pl.multiple_of(j * step, step), step)
        ga[:, columns] = dot(grads[...], w_out[columns, :], NT).astype(jnp.bfloat16)

    for (start, size), copies in zip(plan["missing"](), late):
        wait(copies)
        columns = pl.ds(pl.multiple_of(start, 128), size)
        proj[:, columns] = dot(normed_ref[...], w_in[:, columns], NN).astype(jnp.bfloat16)

    wait(place)

    def apart(block):
        return jnp.concatenate([block * low_lanes, block * high_lanes], axis=0)

    def stacked(block):
        return jnp.concatenate([block[:, :rows], block[:, rows:]], axis=0)

    def lanes(part, pair):
        return pl.ds(pl.multiple_of(part * width + pair * PAIR, PAIR), PAIR)

    chunk = scores.shape[0]
    unroll = min(chunk, 4)

    def each(body):
        @pl.loop(0, chunk // unroll)
        def _(i):
            for inner in range(unroll):
                body(i * unroll + inner)

    for group in range(groups):
        here = pl.ds(group * rows, rows)

        @pl.loop(0, width // (PAIR * chunk))
        def _(part):
            def products(item):
                pair = part * chunk + item
                q_two = apart(proj[here, lanes(0, pair)] * DH ** (-0.5))
                scores[item] = dot(proj[here, lanes(1, pair)], q_two, NT)
                ga_two = apart(ga[here, lanes(0, pair)])
                gprobs[item] = dot(proj[here, lanes(2, pair)], ga_two, NT)

            def softmax(item):
                masked = scores[item] + bias[...]
                expanded = jnp.exp(masked - jnp.max(masked, axis=0, keepdims=True))
                probs = expanded * (1.0 / jnp.sum(expanded, axis=0, keepdims=True))
                low[item, 0] = probs.astype(jnp.bfloat16)
                weighted = probs * gprobs[item]
                delta = jnp.sum(weighted, axis=0, keepdims=True)
                low[item, 1] = (weighted - probs * delta).astype(jnp.bfloat16)

            def results(item):
                pair = part * chunk + item
                probs_low, grad_scores = low[item, 0], low[item, 1]
                q_two = apart(proj[here, lanes(0, pair)] * DH ** (-0.5))
                k_two = apart(proj[here, lanes(1, pair)])
                v_two = apart(proj[here, lanes(2, pair)])
                ga_two = apart(ga[here, lanes(0, pair)])
                att[here, lanes(0, pair)] = dot(stacked(probs_low), v_two, TN).astype(jnp.bfloat16)
                gproj[here, lanes(0, pair)] = (
                    dot(stacked(grad_scores), k_two, TN) * DH ** (-0.5)
                ).astype(jnp.bfloat16)
                gproj[here, lanes(1, pair)] = dot(grad_scores, q_two, NN).astype(jnp.bfloat16)
                gproj[here, lanes(2, pair)] = dot(probs_low, ga_two, NN).astype(jnp.bfloat16)

            each(products)
            each(softmax)
            each(results)

    def store(which, group, value):
        for frame in range(frames):
            out_ref[pl.ds(frame ^ device, 1), which, group * SUB : (group + 1) * SUB, :] = value[
                frame * SUB : (frame + 1) * SUB
            ].reshape(1, SUB, width)

    for group in range(groups):
        here = pl.ds(group * rows, rows)
        mixed = dot(att[here, :], w_out[...], NN)
        wide = load_rows(both_ref, 0, group).astype(jnp.float32)
        store(0, group, (wide + live * mixed).astype(jnp.bfloat16))

    wait(again)

    @pl.loop(0, width // step)
    def _(j):
        columns = pl.ds(pl.multiple_of(j * step, step), step)
        gnorm[:, columns] = dot(gproj[...], w_in[columns, :], NT)

    for group in range(groups):
        here = pl.ds(group * rows, rows)
        grad = gnorm[here, :] * gain_ref[...]
        scale = stats_ref[here, 1:2]
        hat = (load_rows(both_ref, 0, group).astype(jnp.float32) - stats_ref[here, 0:1]) * scale
        grad_rows = scale * (
            grad
            - jnp.mean(grad, axis=-1, keepdims=True)
            - hat * jnp.mean(grad * hat, axis=-1, keepdims=True)
        )
        cot = load_rows(both_ref, 1, group).astype(jnp.float32)
        store(1, group, (cot + grad_rows).astype(jnp.bfloat16))


def run_front(gain, shape, sources, plan):
    frames, _, patches, width = shape
    total = frames * patches
    vmem = pl.BlockSpec(memory_space=pltpu.VMEM)
    anywhere = pl.BlockSpec(memory_space=pl.ANY)
    columns = plan["columns"]
    return pl.pallas_call(
        functools.partial(front_kernel, plan),
        out_shape=(
            jax.ShapeDtypeStruct(shape, jnp.bfloat16),
            jax.ShapeDtypeStruct((total, width), jnp.bfloat16),
            jax.ShapeDtypeStruct((total, 128), jnp.float32),
            jax.ShapeDtypeStruct((total, columns), jnp.bfloat16),
        ),
        in_specs=[vmem] + [anywhere if wide else vmem for wide in plan["spread"]],
        out_specs=(vmem, vmem, vmem, vmem),
        scratch_shapes=[
            pltpu.VMEM((width, columns), jnp.bfloat16),
            pltpu.SemaphoreType.DMA((1,)),
        ],
        compiler_params=pltpu.CompilerParams(vmem_limit_bytes=VMEM_LIMIT),
        cost_estimate=pl.CostEstimate(flops=total, bytes_accessed=total, transcendentals=0),
        name="front",
    )(gain, *sources)


def run_main(counts, gain, fronted, weights, plan):
    both, normed, stats, front = fronted
    frames, _, patches, width = both.shape
    total, rows = frames * patches, frames * SUB
    vmem = pl.BlockSpec(memory_space=pltpu.VMEM)
    smem = pl.BlockSpec(memory_space=pltpu.SMEM)
    anywhere = pl.BlockSpec(memory_space=pl.ANY)
    params = pltpu.CompilerParams(vmem_limit_bytes=VMEM_LIMIT if rows <= 128 else 2 * VMEM_LIMIT)
    chunk = 8 if rows <= 128 else 1
    return pl.pallas_call(
        functools.partial(main_kernel, plan),
        out_shape=jax.ShapeDtypeStruct(both.shape, jnp.bfloat16),
        in_specs=[smem, vmem, vmem, vmem, vmem, anywhere]
        + [anywhere] * len(weights),
        out_specs=vmem,
        scratch_shapes=[
            pltpu.VMEM((width, 3 * width), jnp.bfloat16),
            pltpu.VMEM((width, width), jnp.bfloat16),
            pltpu.VMEM((total, width), jnp.bfloat16),
            pltpu.VMEM((total, 3 * width), jnp.bfloat16),
            pltpu.VMEM((total, width), jnp.bfloat16),
            pltpu.VMEM((total, width), jnp.bfloat16),
            pltpu.VMEM((total, 3 * width), jnp.bfloat16),
            pltpu.VMEM((total, width), jnp.float32),
            pltpu.VMEM((rows, 2 * rows), jnp.float32),
            pltpu.VMEM((chunk, rows, 2 * rows), jnp.float32),
            pltpu.VMEM((chunk, rows, 2 * rows), jnp.float32),
            pltpu.VMEM((chunk, 2, rows, 2 * rows), jnp.bfloat16),
            pltpu.SemaphoreType.DMA((8,)),
        ],
        compiler_params=params,
        cost_estimate=pl.CostEstimate(
            flops=12 * total * width * width,
            bytes_accessed=8 * width * width + 8 * total * width,
            transcendentals=total * 2048,
        ),
        name="main",
    )(counts, gain, both, normed, stats, front, *weights)


def swap(array, distance, devices):
    return lax.ppermute(array, "frame", [(f, f ^ distance) for f in range(devices)])


def join_kernel(axis, *refs):
    *sources, target = refs
    start = 0
    for source in sources:
        end = start + source.shape[axis]
        if axis == 0:
            target[start:end, :] = source[...]
        else:
            target[:, start:end] = source[...]
        start = end


def join(axis, *arrays):
    shape = list(arrays[0].shape)
    shape[axis] = sum(array.shape[axis] for array in arrays)
    vmem = pl.BlockSpec(memory_space=pltpu.VMEM)
    return pl.pallas_call(
        functools.partial(join_kernel, axis),
        out_shape=jax.ShapeDtypeStruct(shape, arrays[0].dtype),
        in_specs=[vmem] * len(arrays),
        out_specs=vmem,
        compiler_params=SMALL,
        name="join",
    )(*arrays)


def pack_kernel(patches, share, *refs):
    sources, (joined, own, mine, to_x, to_y), held, fetched, sems = (
        refs[:4], refs[4:9], refs[9], refs[10:14], refs[14]
    )
    copies = [
        pltpu.make_async_copy(source, target, sems.at[i])
        for i, (source, target) in enumerate(zip(sources, fetched))
    ]
    for copy in copies:
        copy.start()
    w_in, w_out, tokens, cot = fetched
    depth = w_in.shape[0]
    half, block = depth // 2, 2 * share
    device = lax.axis_index("frame")
    chip, core = device // 2, device % 2
    full = patches // SUB * SUB
    held[:, full:] = jnp.zeros((2, held.shape[1] - full, held.shape[2]), held.dtype)
    wait(copies)
    joined[:, : w_in.shape[1]] = w_in[...]
    joined[:, w_in.shape[1] :] = w_out[...]
    held[0, :patches] = tokens[0, 0]
    held[1, :patches] = cot[0, 0]

    def put(target, row, owner):
        rows = pl.ds(pl.multiple_of(owner * share, share), share)
        target[row : row + share, :] = held[0, rows, :]
        target[row + share : row + block, :] = held[1, rows, :]

    put(mine, 0, device)
    own[:depth, :] = joined[...]
    put(own, depth, device ^ 1)
    for target, first, last, away, core_by in ((to_x, 0, half, 1, 0), (to_y, half, 0, 2, 1)):
        target[:half, :] = joined[first : first + half, :]
        put(target, half, (chip ^ away) * 2)
        put(target, half + block, (chip ^ away) * 2 + 1)
        target[half + 2 * block : depth + 2 * block, :] = joined[last : last + half, :]
        put(target, depth + 2 * block, (chip ^ 3) * 2 + core_by)


def turn_kernel(half, by_x, by_y, pair_x, pair_y, to_dx, to_dy):
    to_dx[:half, :] = by_y[:half, :]
    to_dx[half:, :] = pair_y[: 2 * half, :]
    to_dy[:half, :] = by_x[half:, :]
    to_dy[half:, :] = pair_x[2 * half :, :]


def gather_in_rounds(input_weights, output_weights, tokens, cotangent, gain, share, devices):
    depth, in_columns = input_weights.shape
    out_columns = output_weights.shape[1]
    _, _, patches, width = tokens.shape
    half, block = depth // 2, 2 * share
    vmem = pl.BlockSpec(memory_space=pltpu.VMEM)

    def rows_of(count):
        return jax.ShapeDtypeStruct((count, width), jnp.bfloat16)

    joined, own, mine, to_x, to_y = pl.pallas_call(
        functools.partial(pack_kernel, patches, share),
        out_shape=tuple(
            map(rows_of, (depth, depth + block, block, depth + 3 * block, depth + 3 * block))
        ),
        in_specs=[pl.BlockSpec(memory_space=pl.ANY)] * 4,
        out_specs=(vmem,) * 5,
        scratch_shapes=[pltpu.VMEM((2, devices * share, width), jnp.bfloat16)]
        + [pltpu.VMEM(a.shape, a.dtype) for a in (input_weights, output_weights, tokens, cotangent)]
        + [pltpu.SemaphoreType.DMA((4,))],
        compiler_params=SMALL,
        name="pack",
    )(input_weights, output_weights, tokens, cotangent)

    def by_clip(array, offset):
        return lax.ppermute(array, "clip", [(c, c ^ offset) for c in range(4)])

    def across(array):
        return [swap(array, 2, devices), swap(array, 4, devices)]

    def other_core(arrays):
        return [swap(array, 1, devices) for array in arrays]

    one, two = by_clip(joined, 1), by_clip(joined, 2)
    source, two = lax.optimization_barrier((joined, two))
    three = by_clip(source, 3)
    first = [swap(to_x, 2, devices), swap(to_y, 4, devices)]
    tail = half + 2 * block
    first += [swap(first[1][tail:], 2, devices), swap(first[0][tail:], 4, devices)]
    one, first[0], first[1] = lax.optimization_barrier((one, first[0], first[1]))
    second = [one, *across(one)]
    two, three, first[2], first[3] = lax.optimization_barrier((two, three, first[2], first[3]))
    third = [join(0, two, three)]
    second[1], second[2], own, *first = lax.optimization_barrier(
        (second[1], second[2], own, *first)
    )
    first_other = other_core([own, *first])
    second_other = other_core(second)
    ready = [joined, *first, *first_other, *second, *second_other]
    third += across(third[0])

    def tokens_in(sources, both_ref):
        core = lax.axis_index("frame") % 2
        mine_ref, _, x_ref, y_ref, dx_ref, dy_ref, own2, x2, y2, dx2, dy2 = sources[:11]
        rows = pl.ds(pl.multiple_of(half + core * block, block), block)
        behind = slice(half, half + block)

        def diagonal(by_x, by_y):
            return jnp.where(core == 0, by_y[behind, :], by_x[behind, :])

        found = (
            mine_ref[...], own2[depth : depth + block, :],
            x_ref[rows, :], x2[rows, :], y_ref[rows, :], y2[rows, :],
            diagonal(dx_ref, dy_ref), diagonal(dx2, dy2),
        )
        for distance, value in enumerate(found):
            both_ref[distance] = value.reshape(2, share, width)

    table = [
        [(0, 0, 0, depth, 0)],
        [(0, 2, 0, half, 0), (0, 2, tail, half, half)],
        [(0, 4, 0, half, half), (0, 4, tail, half, 0)],
        [(0, 6, 0, half, 0)],
        [(0, 6, 0, half, half)],
    ]
    others = [[(1, d, 0, depth, 0)] for d in (0, 2, 4)]
    pairs = [[(2, d, 0, depth, 0), (3, d, depth, depth, 0)] for d in (0, 2, 4)]
    pairs += [
        [(1, 6, 0, half, 0), (2, 6, half, depth, 0)],
        [(1, 6, 0, half, half), (3, 6, half, depth, 0)],
    ]
    arrays = []
    for group in (table, others, pairs):
        arrays += [(core, parts) for core in (0, 1) for parts in group]

    def pieces(offsets, lanes, base):
        clip, frame = lax.axis_index("clip"), lax.axis_index("frame")
        found = []
        for ref, (core, parts) in enumerate(arrays):
            for offset, distance, first, rows, inside in parts:
                if offset in offsets:
                    row = (frame ^ distance ^ core) * depth + inside
                    found.append((base + ref, None, first, rows, lanes, row, clip ^ offset))
        return found

    def placed(parts, stride):
        return [(*part[:-1], part[-1] * stride) for part in parts]

    def compact():
        return [(*part[:-1], 0) for part in pieces((0,), (0, in_columns), 1)]

    inner, outer = (0, in_columns), (in_columns, out_columns)

    def columns_of(offsets):
        clip = lax.axis_index("clip")
        return [(clip ^ offset) * in_columns for offset in offsets]

    plan = {
        "front": compact,
        "tokens": tokens_in,
        "columns": in_columns,
        "spread": [False] * 11,
        "device": lambda: lax.axis_index("frame"),
        "late": lambda: [placed(pieces((i,), inner, 0), in_columns) for i in (1, 2, 3)],
        "again": lambda: placed(pieces((0,), inner, 0), in_columns),
        "outer": lambda: placed(pieces((0, 1, 2, 3), outer, 0), out_columns),
        "placed": lambda: [
            (0, start, in_columns) for start in columns_of((0,))
        ],
        "missing": lambda: [(start, in_columns) for start in columns_of((1, 2, 3))],
    }
    fronted = run_front(gain, (devices, 2, share, width), [mine, *ready[:10]], plan)
    to_dx, to_dy = pl.pallas_call(
        functools.partial(turn_kernel, half),
        out_shape=(rows_of(depth + half), rows_of(depth + half)),
        in_specs=[vmem] * 4,
        out_specs=(vmem, vmem),
        compiler_params=SMALL,
        name="turn",
    )(second[1], second[2], third[1], third[2])
    third += [swap(to_dx, 2, devices), swap(to_dy, 4, devices)]
    third[3], *fronted = lax.optimization_barrier((third[3], *fronted))
    third += other_core(third)
    return fronted, [*ready, *third], plan


def gather_plainly(input_weights, output_weights, tokens, cotangent, gain, share, devices):
    _, slots, patches, width = tokens.shape
    whole = []
    for weights in (input_weights, output_weights):
        columns = lax.all_gather(weights, "clip", axis=1, tiled=True)
        whole.append(lax.all_gather(columns, "frame", axis=0, tiled=True))

    def by_destination(source):
        padded = jnp.pad(source[0], ((0, 0), (0, devices * share - patches), (0, 0)))
        return padded.reshape(slots, devices, share, width).transpose(1, 0, 2, 3)

    both = jnp.stack([by_destination(tokens), by_destination(cotangent)], axis=2)
    both = lax.all_to_all(both, "frame", split_axis=0, concat_axis=0, tiled=True)
    both = both.reshape(devices * slots, 2, share, width)

    def tokens_in(sources, both_ref):
        both_ref[...] = sources[1][...]

    inner, outer = [[(i, None, 0, w.shape[0], (0, w.shape[1]), 0, 0)] for i, w in enumerate(whole)]
    plan = {
        "front": lambda: inner,
        "tokens": tokens_in,
        "columns": whole[0].shape[1],
        "spread": [True, False],
        "device": lambda: 0,
        "late": lambda: [],
        "again": lambda: inner,
        "outer": lambda: outer,
        "placed": lambda: [(0, 0, whole[0].shape[1])],
        "missing": lambda: [],
    }
    return run_front(gain, both.shape, [whole[0], both], plan), whole, plan


def per_device(clips, devices, tokens, counts, norm_gain, input_weights, output_weights, cotangent):
    _, slots, patches, width = tokens.shape
    share = -(-patches // devices)
    share = -(-share // SUB) * SUB
    depth, in_columns = input_weights.shape
    fits = in_columns % 128 == 0 and output_weights.shape[1] % 128 == 0 and depth % 32 == 0
    small = clips == 4 and devices == 8 and slots == 1 and fits
    gather = gather_in_rounds if small else gather_plainly
    gain = norm_gain.reshape(1, width)
    fronted, weights, plan = gather(
        input_weights, output_weights, tokens, cotangent, gain, share, devices
    )
    back = run_main(counts, gain, fronted, weights, plan)
    back = back.reshape(devices, slots, 2, share, width)
    back = lax.all_to_all(back, "frame", split_axis=0, concat_axis=0, tiled=True)

    def in_order(which):
        rows = back[:, :, which].transpose(1, 0, 2, 3).reshape(slots, devices * share, width)
        return rows[None, :, :patches]

    return in_order(0), in_order(1)


def solution(mesh):
    in_specs = (
        P("clip", "frame", None, None),
        P("clip"),
        P(),
        P("frame", "clip"),
        P("frame", "clip"),
        P("clip", "frame", None, None),
    )
    out_specs = (P("clip", "frame", None, None), P("clip", "frame", None, None))
    body = functools.partial(per_device, mesh.shape["clip"], mesh.shape["frame"])
    return jax.shard_map(body, mesh=mesh, in_specs=in_specs, out_specs=out_specs, check_vma=False)
```

```python
import functools
import math

import jax
import jax.numpy as jnp
from jax import lax
from jax.experimental import pallas as pl
from jax.experimental.pallas import tpu as pltpu
from jax.sharding import PartitionSpec as P

DH = 64
PAIR = 2 * DH
SUB = 16
EPSILON = 1e-06
NEGATIVE = -1e30
NN = (((1,), (0,)), ((), ()))
NT = (((1,), (1,)), ((), ()))
TN = (((0,), (0,)), ((), ()))
VMEM_LIMIT = 27 * 1024 * 1024
PACK_LIMIT = 58 * 1024 * 1024
SMALL = pltpu.CompilerParams(vmem_limit_bytes=6 * 1024 * 1024)


def dot(a, b, dims):
    return lax.dot_general(a, b, dims, preferred_element_type=jnp.float32)


def wait(copies):
    for copy in copies:
        copy.wait()


def load_rows(ref, which, group):
    frames, _, _, width = ref.shape
    return ref[:, which, group * SUB : (group + 1) * SUB, :].reshape(frames * SUB, width)


def beside(ref, starts, size):
    return jnp.concatenate(
        [ref[:, pl.ds(pl.multiple_of(start, 128), size)] for start in starts], axis=1
    )


def chunks(columns):
    step = math.gcd(columns, 256)
    return [(start, step) for start in range(0, columns, step)]


def stack_rows(view, refs, block, lanes):
    return jnp.concatenate(
        [view.piece(refs, block, *part, lanes) for parts in view.rows for part in parts], axis=0
    )


def stack_columns(view, refs, parts, start, size):
    return jnp.concatenate(
        [
            jnp.concatenate(
                [view.piece(refs, block, *part, (start, size)) for part in parts], axis=0
            )
            for block in range(view.blocks)
        ],
        axis=1,
    )


def front_kernel(view, gain_ref, *refs):
    sources = refs[:-5]
    both_ref, normed_ref, stats_ref, proj_ref, natural = refs[-5:]
    view.tokens(sources, both_ref)
    frames, _, patches, _ = both_ref.shape
    rows = frames * SUB
    for group in range(patches // SUB):
        here = pl.ds(group * rows, rows)
        wide = load_rows(both_ref, 0, group).astype(jnp.float32)
        average = jnp.mean(wide, axis=-1, keepdims=True)
        centred = wide - average
        variance = jnp.mean(centred * centred, axis=-1, keepdims=True)
        scale = lax.rsqrt(variance + EPSILON)
        natural[here, :] = (centred * scale * gain_ref[...]).astype(jnp.bfloat16)
        stats_ref[here, 0:1] = average
        stats_ref[here, 1:2] = scale
    normed_ref[...] = beside(natural, *view.row_order())
    for start, size in chunks(proj_ref.shape[1]):
        weight = stack_rows(view, sources, 0, (start, size))
        proj_ref[:, start : start + size] = dot(normed_ref[...], weight, NN).astype(jnp.bfloat16)


def main_kernel(view, counts_ref, gain_ref, both_ref, normed_ref, stats_ref, front_ref, *rest):
    weights = rest[:-11]
    out_ref, grads, proj, ga, att, gproj, wide_sum, bias, scores, gprobs, low = rest[-11:]
    frames, _, patches, width = both_ref.shape
    groups = patches // SUB
    rows = frames * SUB
    count = counts_ref[0]
    device = view.device()
    in_columns, out_columns = view.in_columns, view.out_columns
    row_starts, row_size = view.row_order()
    block_order = view.block_order()

    def column(block, stride, start=0):
        return pl.multiple_of(block_order[block] * stride + start, 128)

    def put_rows(target, parts, value):
        done = 0
        for index, first, depth in parts:
            start = pl.multiple_of(row_starts[index] + first, 128)
            target[:, pl.ds(start, depth)] = value[:, done : done + depth]
            done += depth

    def real(index):
        return ((index // SUB) ^ device) < count

    live = real(lax.broadcasted_iota(jnp.int32, (rows, 1), 0)).astype(jnp.float32)
    for group in range(groups):
        here = pl.ds(group * rows, rows)
        grads[here, :] = (load_rows(both_ref, 1, group).astype(jnp.float32) * live).astype(
            jnp.bfloat16
        )
    key = lax.broadcasted_iota(jnp.int32, (rows, 2 * rows), 0)
    query = lax.broadcasted_iota(jnp.int32, (rows, 2 * rows), 1)
    bias[...] = jnp.where((query % SUB == key % SUB) & real(key), 0.0, NEGATIVE)
    lane = lax.broadcasted_iota(jnp.int32, (1, PAIR), 1)
    low_lanes = (lane < DH).astype(jnp.bfloat16)
    high_lanes = (lane >= DH).astype(jnp.bfloat16)

    grads_ordered = beside(grads, [column(i, out_columns) for i in range(view.blocks)], out_columns)
    for parts in view.rows:
        weight = stack_columns(view, weights, parts, in_columns, out_columns)
        put_rows(ga, parts, dot(grads_ordered, weight, NT).astype(jnp.bfloat16))

    proj[:, pl.ds(column(0, in_columns), in_columns)] = front_ref[...]
    for block in range(1, view.blocks):
        for start, size in chunks(in_columns):
            weight = stack_rows(view, weights, block, (start, size))
            proj[:, pl.ds(column(block, in_columns, start), size)] = dot(
                normed_ref[...], weight, NN
            ).astype(jnp.bfloat16)

    def apart(block):
        return jnp.concatenate([block * low_lanes, block * high_lanes], axis=0)

    def stacked(block):
        return jnp.concatenate([block[:, :rows], block[:, rows:]], axis=0)

    def lanes(part, pair):
        return pl.ds(pl.multiple_of(part * width + pair * PAIR, PAIR), PAIR)

    chunk = scores.shape[0]
    unroll = min(chunk, 4)

    def each(body):
        @pl.loop(0, chunk // unroll)
        def _(i):
            for inner in range(unroll):
                body(i * unroll + inner)

    for group in range(groups):
        here = pl.ds(group * rows, rows)

        @pl.loop(0, width // (PAIR * chunk))
        def _(part):
            def products(item):
                pair = part * chunk + item
                q_two = apart(proj[here, lanes(0, pair)] * DH ** (-0.5))
                scores[item] = dot(proj[here, lanes(1, pair)], q_two, NT)
                ga_two = apart(ga[here, lanes(0, pair)])
                gprobs[item] = dot(proj[here, lanes(2, pair)], ga_two, NT)

            def softmax(item):
                masked = scores[item] + bias[...]
                expanded = jnp.exp(masked - jnp.max(masked, axis=0, keepdims=True))
                probs = expanded * (1.0 / jnp.sum(expanded, axis=0, keepdims=True))
                low[item, 0] = probs.astype(jnp.bfloat16)
                weighted = probs * gprobs[item]
                delta = jnp.sum(weighted, axis=0, keepdims=True)
                low[item, 1] = (weighted - probs * delta).astype(jnp.bfloat16)

            def results(item):
                pair = part * chunk + item
                probs_low, grad_scores = low[item, 0], low[item, 1]
                q_two = apart(proj[here, lanes(0, pair)] * DH ** (-0.5))
                k_two = apart(proj[here, lanes(1, pair)])
                v_two = apart(proj[here, lanes(2, pair)])
                ga_two = apart(ga[here, lanes(0, pair)])
                att[here, lanes(0, pair)] = dot(stacked(probs_low), v_two, TN).astype(jnp.bfloat16)
                gproj[here, lanes(0, pair)] = (
                    dot(stacked(grad_scores), k_two, TN) * DH ** (-0.5)
                ).astype(jnp.bfloat16)
                gproj[here, lanes(1, pair)] = dot(grad_scores, q_two, NN).astype(jnp.bfloat16)
                gproj[here, lanes(2, pair)] = dot(probs_low, ga_two, NN).astype(jnp.bfloat16)

            each(products)
            each(softmax)
            each(results)

    def store(which, group, value):
        for frame in range(frames):
            out_ref[pl.ds(frame ^ device, 1), which, group * SUB : (group + 1) * SUB, :] = value[
                frame * SUB : (frame + 1) * SUB
            ].reshape(1, SUB, width)

    att_ordered = beside(att, row_starts, row_size)
    for block in range(view.blocks):
        for start, size in chunks(out_columns):
            weight = stack_rows(view, weights, block, (in_columns + start, size))
            wide_sum[:, pl.ds(column(block, out_columns, start), size)] = dot(
                att_ordered, weight, NN
            )

    for group in range(groups):
        here = pl.ds(group * rows, rows)
        wide = load_rows(both_ref, 0, group).astype(jnp.float32)
        store(0, group, (wide + live * wide_sum[here, :]).astype(jnp.bfloat16))

    gproj_ordered = beside(gproj, [column(i, in_columns) for i in range(view.blocks)], in_columns)
    for parts in view.rows:
        weight = stack_columns(view, weights, parts, 0, in_columns)
        put_rows(wide_sum, parts, dot(gproj_ordered, weight, NT))

    for group in range(groups):
        here = pl.ds(group * rows, rows)
        grad = wide_sum[here, :] * gain_ref[...]
        scale = stats_ref[here, 1:2]
        hat = (load_rows(both_ref, 0, group).astype(jnp.float32) - stats_ref[here, 0:1]) * scale
        grad_rows = scale * (
            grad
            - jnp.mean(grad, axis=-1, keepdims=True)
            - hat * jnp.mean(grad * hat, axis=-1, keepdims=True)
        )
        cot = load_rows(both_ref, 1, group).astype(jnp.float32)
        store(1, group, (cot + grad_rows).astype(jnp.bfloat16))


def run_front(gain, shape, sources, view):
    frames, _, patches, width = shape
    total = frames * patches
    vmem = pl.BlockSpec(memory_space=pltpu.VMEM)
    return pl.pallas_call(
        functools.partial(front_kernel, view),
        out_shape=(
            jax.ShapeDtypeStruct(shape, jnp.bfloat16),
            jax.ShapeDtypeStruct((total, width), jnp.bfloat16),
            jax.ShapeDtypeStruct((total, 128), jnp.float32),
            jax.ShapeDtypeStruct((total, view.in_columns), jnp.bfloat16),
        ),
        in_specs=[vmem] * (1 + len(sources)),
        out_specs=(vmem,) * 4,
        scratch_shapes=[pltpu.VMEM((total, width), jnp.bfloat16)],
        compiler_params=pltpu.CompilerParams(vmem_limit_bytes=VMEM_LIMIT),
        cost_estimate=pl.CostEstimate(flops=total, bytes_accessed=total, transcendentals=0),
        name="front",
    )(gain, *sources)


def run_main(counts, gain, fronted, weights, view):
    both, normed, stats, front = fronted
    frames, _, patches, width = both.shape
    total, rows = frames * patches, frames * SUB
    vmem = pl.BlockSpec(memory_space=pltpu.VMEM)
    smem = pl.BlockSpec(memory_space=pltpu.SMEM)
    chunk = 8 if rows <= 128 else 1
    return pl.pallas_call(
        functools.partial(main_kernel, view),
        out_shape=jax.ShapeDtypeStruct(both.shape, jnp.bfloat16),
        in_specs=[smem] + [vmem] * (5 + len(weights)),
        out_specs=vmem,
        scratch_shapes=[
            pltpu.VMEM((total, width), jnp.bfloat16),
            pltpu.VMEM((total, 3 * width), jnp.bfloat16),
            pltpu.VMEM((total, width), jnp.bfloat16),
            pltpu.VMEM((total, width), jnp.bfloat16),
            pltpu.VMEM((total, 3 * width), jnp.bfloat16),
            pltpu.VMEM((total, width), jnp.float32),
            pltpu.VMEM((rows, 2 * rows), jnp.float32),
            pltpu.VMEM((chunk, rows, 2 * rows), jnp.float32),
            pltpu.VMEM((chunk, rows, 2 * rows), jnp.float32),
            pltpu.VMEM((chunk, 2, rows, 2 * rows), jnp.bfloat16),
        ],
        compiler_params=pltpu.CompilerParams(
            vmem_limit_bytes=VMEM_LIMIT if rows <= 128 else 2 * VMEM_LIMIT
        ),
        cost_estimate=pl.CostEstimate(
            flops=12 * total * width * width,
            bytes_accessed=8 * width * width + 8 * total * width,
            transcendentals=total * 2048,
        ),
        name="main",
    )(counts, gain, both, normed, stats, front, *weights)


class View:
    def __init__(self, blocks, rows, in_columns, out_columns, piece, tokens, device, row_order, block_order):
        self.blocks, self.rows = blocks, rows
        self.in_columns, self.out_columns = in_columns, out_columns
        self.piece, self.tokens, self.device = piece, tokens, device
        self.row_order, self.block_order = row_order, block_order


def swap(array, distance, devices):
    return lax.ppermute(array, "frame", [(f, f ^ distance) for f in range(devices)])


def join_kernel(axis, *refs):
    *sources, target = refs
    start = 0
    for source in sources:
        end = start + source.shape[axis]
        if axis == 0:
            target[start:end, :] = source[...]
        else:
            target[:, start:end] = source[...]
        start = end


def join(axis, *arrays):
    shape = list(arrays[0].shape)
    shape[axis] = sum(array.shape[axis] for array in arrays)
    vmem = pl.BlockSpec(memory_space=pltpu.VMEM)
    return pl.pallas_call(
        functools.partial(join_kernel, axis),
        out_shape=jax.ShapeDtypeStruct(shape, arrays[0].dtype),
        in_specs=[vmem] * len(arrays),
        out_specs=vmem,
        compiler_params=SMALL,
        name="join",
    )(*arrays)


def pack_kernel(patches, share, *refs):
    sources, (joined, own, mine, to_x, to_y), held, fetched, sems = (
        refs[:4], refs[4:9], refs[9], refs[10:14], refs[14]
    )
    copies = [
        pltpu.make_async_copy(source, target, sems.at[i])
        for i, (source, target) in enumerate(zip(sources, fetched))
    ]
    for copy in copies:
        copy.start()
    w_in, w_out, tokens, cot = fetched
    depth = w_in.shape[0]
    half, block = depth // 2, 2 * share
    device = lax.axis_index("frame")
    chip, core = device // 2, device % 2
    full = patches // SUB * SUB
    held[:, full:] = jnp.zeros((2, held.shape[1] - full, held.shape[2]), held.dtype)
    wait(copies)
    joined[:, : w_in.shape[1]] = w_in[...]
    joined[:, w_in.shape[1] :] = w_out[...]
    held[0, :patches] = tokens[0, 0]
    held[1, :patches] = cot[0, 0]

    def put(target, row, owner):
        rows = pl.ds(pl.multiple_of(owner * share, share), share)
        target[row : row + share, :] = held[0, rows, :]
        target[row + share : row + block, :] = held[1, rows, :]

    put(mine, 0, device)
    own[:depth, :] = joined[...]
    put(own, depth, device ^ 1)
    for target, first, last, away, core_by in ((to_x, 0, half, 1, 0), (to_y, half, 0, 2, 1)):
        target[:half, :] = joined[first : first + half, :]
        put(target, half, (chip ^ away) * 2)
        put(target, half + block, (chip ^ away) * 2 + 1)
        target[half + 2 * block : depth + 2 * block, :] = joined[last : last + half, :]
        put(target, depth + 2 * block, (chip ^ 3) * 2 + core_by)


def turn_kernel(half, by_x, by_y, pair_x, pair_y, to_dx, to_dy):
    to_dx[:half, :] = by_y[:half, :]
    to_dx[half:, :] = pair_y[: 2 * half, :]
    to_dy[:half, :] = by_x[half:, :]
    to_dy[half:, :] = pair_x[2 * half :, :]


def gather_in_rounds(input_weights, output_weights, tokens, cotangent, gain, share, devices):
    depth, in_columns = input_weights.shape
    out_columns = output_weights.shape[1]
    _, _, patches, width = tokens.shape
    half, block = depth // 2, 2 * share
    vmem = pl.BlockSpec(memory_space=pltpu.VMEM)

    def rows_of(count):
        return jax.ShapeDtypeStruct((count, width), jnp.bfloat16)

    joined, own, mine, to_x, to_y = pl.pallas_call(
        functools.partial(pack_kernel, patches, share),
        out_shape=tuple(
            map(rows_of, (depth, depth + block, block, depth + 3 * block, depth + 3 * block))
        ),
        in_specs=[pl.BlockSpec(memory_space=pltpu.HBM)] * 4,
        out_specs=(vmem,) * 5,
        scratch_shapes=[pltpu.VMEM((2, devices * share, width), jnp.bfloat16)]
        + [pltpu.VMEM(a.shape, a.dtype) for a in (input_weights, output_weights, tokens, cotangent)]
        + [pltpu.SemaphoreType.DMA((4,))],
        compiler_params=pltpu.CompilerParams(vmem_limit_bytes=PACK_LIMIT),
        name="pack",
    )(input_weights, output_weights, tokens, cotangent)

    def by_clip(array, offset):
        return lax.ppermute(array, "clip", [(c, c ^ offset) for c in range(4)])

    def across(array):
        return [swap(array, 2, devices), swap(array, 4, devices)]

    def other_core(arrays):
        return [swap(array, 1, devices) for array in arrays]

    one, two, three = by_clip(joined, 1), by_clip(joined, 2), by_clip(joined, 3)
    first = [swap(to_x, 2, devices), swap(to_y, 4, devices)]
    tail = half + 2 * block
    first += [swap(first[1][tail:], 2, devices), swap(first[0][tail:], 4, devices)]
    one, first[0], first[1] = lax.optimization_barrier((one, first[0], first[1]))
    second = [one, *across(one)]
    two, three, first[2], first[3] = lax.optimization_barrier((two, three, first[2], first[3]))
    third = [join(0, two, three)]
    second[1], second[2], own, *first = lax.optimization_barrier(
        (second[1], second[2], own, *first)
    )
    first_other = other_core([own, *first])
    second_other = other_core(second)
    ready = [joined, *first, *first_other, *second, *second_other]
    third += across(third[0])

    def tokens_in(sources, both_ref):
        core = lax.axis_index("frame") % 2
        mine_ref, _, x_ref, y_ref, dx_ref, dy_ref, own2, x2, y2, dx2, dy2 = sources[:11]
        rows = pl.ds(pl.multiple_of(half + core * block, block), block)
        behind = slice(half, half + block)

        def diagonal(by_x, by_y):
            return jnp.where(core == 0, by_y[behind, :], by_x[behind, :])

        found = (
            mine_ref[...], own2[depth : depth + block, :],
            x_ref[rows, :], x2[rows, :], y_ref[rows, :], y2[rows, :],
            diagonal(dx_ref, dy_ref), diagonal(dx2, dy2),
        )
        for distance, value in enumerate(found):
            both_ref[distance] = value.reshape(2, share, width)

    table = [
        [(0, 0, 0, depth, 0)],
        [(0, 2, 0, half, 0), (0, 2, tail, half, half)],
        [(0, 4, 0, half, half), (0, 4, tail, half, 0)],
        [(0, 6, 0, half, 0)],
        [(0, 6, 0, half, half)],
    ]
    others = [[(1, d, 0, depth, 0)] for d in (0, 2, 4)]
    pairs = [[(2, d, 0, depth, 0), (3, d, depth, depth, 0)] for d in (0, 2, 4)]
    pairs += [
        [(1, 6, 0, half, 0), (2, 6, half, depth, 0)],
        [(1, 6, 0, half, half), (3, 6, half, depth, 0)],
    ]
    arrays = []
    for group in (table, others, pairs):
        arrays += [(core, parts) for core in (0, 1) for parts in group]

    def piece(base):
        def value(refs, offset, distance, first, depth, lanes):
            found = [
                (inside, refs[base + ref][start : start + size, lanes[0] : lanes[0] + lanes[1]])
                for ref, (core, parts) in enumerate(arrays)
                for source, away, start, size, inside in parts
                if (source, away ^ core) == (offset, distance)
            ]
            return jnp.concatenate([held for _, held in sorted(found, key=lambda f: f[0])], axis=0)

        return value

    def view(base):
        return View(
            4,
            [[(d, 0, depth), (d + 1, 0, depth)] for d in range(0, devices, 2)],
            in_columns,
            out_columns,
            piece(base),
            tokens_in,
            lambda: lax.axis_index("frame"),
            lambda: ([(lax.axis_index("frame") ^ d) * depth for d in range(devices)], depth),
            lambda: [lax.axis_index("clip") ^ offset for offset in range(4)],
        )

    fronted = run_front(gain, (devices, 2, share, width), [mine, *ready[:10]], view(1))
    to_dx, to_dy = pl.pallas_call(
        functools.partial(turn_kernel, half),
        out_shape=(rows_of(depth + half), rows_of(depth + half)),
        in_specs=[vmem] * 4,
        out_specs=(vmem, vmem),
        compiler_params=SMALL,
        name="turn",
    )(second[1], second[2], third[1], third[2])
    third += [swap(to_dx, 2, devices), swap(to_dy, 4, devices)]
    third[3], *fronted = lax.optimization_barrier((third[3], *fronted))
    third += other_core(third)
    return fronted, [*ready, *third], view(0)


def gather_plainly(input_weights, output_weights, tokens, cotangent, gain, share, devices):
    _, slots, patches, width = tokens.shape
    whole = []
    for weights in (input_weights, output_weights):
        columns = lax.all_gather(weights, "clip", axis=1, tiled=True)
        whole.append(lax.all_gather(columns, "frame", axis=0, tiled=True))

    def by_destination(source):
        padded = jnp.pad(source[0], ((0, 0), (0, devices * share - patches), (0, 0)))
        return padded.reshape(slots, devices, share, width).transpose(1, 0, 2, 3)

    both = jnp.stack([by_destination(tokens), by_destination(cotangent)], axis=2)
    both = lax.all_to_all(both, "frame", split_axis=0, concat_axis=0, tiled=True)
    both = both.reshape(devices * slots, 2, share, width)

    def tokens_in(sources, both_ref):
        both_ref[...] = sources[2][...]

    in_columns, out_columns = whole[0].shape[1], whole[1].shape[1]

    def piece(refs, block, index, first, depth, lanes):
        outer = lanes[0] >= in_columns
        start = lanes[0] - in_columns * outer
        return refs[int(outer)][first : first + depth, start : start + lanes[1]]

    step = math.gcd(width, 256)
    view = View(
        1,
        [[(0, first, step)] for first in range(0, width, step)],
        in_columns,
        out_columns,
        piece,
        tokens_in,
        lambda: 0,
        lambda: ([0], width),
        lambda: [0],
    )
    return run_front(gain, both.shape, [*whole, both], view), whole, view


def per_device(clips, devices, tokens, counts, norm_gain, input_weights, output_weights, cotangent):
    _, slots, patches, width = tokens.shape
    share = -(-patches // devices)
    share = -(-share // SUB) * SUB
    depth, in_columns = input_weights.shape
    fits = in_columns % 128 == 0 and output_weights.shape[1] % 128 == 0 and depth % 32 == 0
    small = clips == 4 and devices == 8 and slots == 1 and fits
    gather = gather_in_rounds if small else gather_plainly
    gain = norm_gain.reshape(1, width)
    fronted, weights, view = gather(
        input_weights, output_weights, tokens, cotangent, gain, share, devices
    )
    back = run_main(counts, gain, fronted, weights, view)
    back = back.reshape(devices, slots, 2, share, width)
    back = lax.all_to_all(back, "frame", split_axis=0, concat_axis=0, tiled=True)

    def in_order(which):
        rows = back[:, :, which].transpose(1, 0, 2, 3).reshape(slots, devices * share, width)
        return rows[None, :, :patches]

    return in_order(0), in_order(1)


def solution(mesh):
    in_specs = (
        P("clip", "frame", None, None),
        P("clip"),
        P(),
        P("frame", "clip"),
        P("frame", "clip"),
        P("clip", "frame", None, None),
    )
    out_specs = (P("clip", "frame", None, None), P("clip", "frame", None, None))
    body = functools.partial(per_device, mesh.shape["clip"], mesh.shape["frame"])
    return jax.shard_map(body, mesh=mesh, in_specs=in_specs, out_specs=out_specs, check_vma=False)
```

```python
import functools
import math

import jax
import jax.numpy as jnp
from jax import lax
from jax.experimental import pallas as pl
from jax.experimental.pallas import tpu as pltpu
from jax.sharding import PartitionSpec as P

DH = 64
PAIR = 2 * DH
SUB = 16
EPSILON = 1e-06
NEGATIVE = -1e30
NN = (((1,), (0,)), ((), ()))
NT = (((1,), (1,)), ((), ()))
TN = (((0,), (0,)), ((), ()))
VMEM_LIMIT = 27 * 1024 * 1024
PACK_LIMIT = 58 * 1024 * 1024
SMALL = pltpu.CompilerParams(vmem_limit_bytes=6 * 1024 * 1024)


def dot(a, b, dims):
    return lax.dot_general(a, b, dims, preferred_element_type=jnp.float32)


def wait(copies):
    for copy in copies:
        copy.wait()


def load_rows(ref, which, group):
    frames, _, _, width = ref.shape
    return ref[:, which, group * SUB : (group + 1) * SUB, :].reshape(frames * SUB, width)


def beside(ref, starts, size):
    return jnp.concatenate(
        [ref[:, pl.ds(pl.multiple_of(start, 128), size)] for start in starts], axis=1
    )


def chunks(columns):
    step = math.gcd(columns, 256)
    return [(start, step) for start in range(0, columns, step)]


def stack_rows(view, refs, block, lanes):
    return jnp.concatenate(
        [view.piece(refs, block, *part, lanes) for parts in view.rows for part in parts], axis=0
    )


def stack_columns(view, refs, parts, start, size):
    return jnp.concatenate(
        [
            jnp.concatenate(
                [view.piece(refs, block, *part, (start, size)) for part in parts], axis=0
            )
            for block in range(view.blocks)
        ],
        axis=1,
    )


def front_kernel(view, gain_ref, *refs):
    sources = refs[:-5]
    both_ref, normed_ref, stats_ref, proj_ref, natural = refs[-5:]
    view.tokens(sources, both_ref)
    frames, _, patches, _ = both_ref.shape
    rows = frames * SUB
    for group in range(patches // SUB):
        here = pl.ds(group * rows, rows)
        wide = load_rows(both_ref, 0, group).astype(jnp.float32)
        average = jnp.mean(wide, axis=-1, keepdims=True)
        centred = wide - average
        variance = jnp.mean(centred * centred, axis=-1, keepdims=True)
        scale = lax.rsqrt(variance + EPSILON)
        natural[here, :] = (centred * scale * gain_ref[...]).astype(jnp.bfloat16)
        stats_ref[here, 0:1] = average
        stats_ref[here, 1:2] = scale
    normed_ref[...] = beside(natural, *view.row_order())
    for block in range(view.early):
        for start, size in chunks(view.in_columns):
            weight = stack_rows(view, sources, block, (start, size))
            here = pl.ds(block * view.in_columns + start, size)
            proj_ref[:, here] = dot(normed_ref[...], weight, NN).astype(jnp.bfloat16)


def main_kernel(view, counts_ref, gain_ref, both_ref, normed_ref, stats_ref, front_ref, *rest):
    weights = rest[:-11]
    out_ref, grads, proj, ga, att, gproj, wide_sum, bias, scores, gprobs, low = rest[-11:]
    frames, _, patches, width = both_ref.shape
    groups = patches // SUB
    rows = frames * SUB
    count = counts_ref[0]
    device = view.device()
    in_columns, out_columns = view.in_columns, view.out_columns
    row_starts, row_size = view.row_order()
    block_order = view.block_order()

    def column(block, stride, start=0):
        return pl.multiple_of(block_order[block] * stride + start, 128)

    def put_rows(target, parts, value):
        done = 0
        for index, first, depth in parts:
            start = pl.multiple_of(row_starts[index] + first, 128)
            target[:, pl.ds(start, depth)] = value[:, done : done + depth]
            done += depth

    def real(index):
        return ((index // SUB) ^ device) < count

    live = real(lax.broadcasted_iota(jnp.int32, (rows, 1), 0)).astype(jnp.float32)
    for group in range(groups):
        here = pl.ds(group * rows, rows)
        grads[here, :] = (load_rows(both_ref, 1, group).astype(jnp.float32) * live).astype(
            jnp.bfloat16
        )
    key = lax.broadcasted_iota(jnp.int32, (rows, 2 * rows), 0)
    query = lax.broadcasted_iota(jnp.int32, (rows, 2 * rows), 1)
    bias[...] = jnp.where((query % SUB == key % SUB) & real(key), 0.0, NEGATIVE)
    lane = lax.broadcasted_iota(jnp.int32, (1, PAIR), 1)
    low_lanes = (lane < DH).astype(jnp.bfloat16)
    high_lanes = (lane >= DH).astype(jnp.bfloat16)

    grads_ordered = beside(grads, [column(i, out_columns) for i in range(view.blocks)], out_columns)
    for parts in view.rows:
        weight = stack_columns(view, weights, parts, in_columns, out_columns)
        put_rows(ga, parts, dot(grads_ordered, weight, NT).astype(jnp.bfloat16))

    for block in range(view.early):
        held = front_ref[:, block * in_columns : (block + 1) * in_columns]
        proj[:, pl.ds(column(block, in_columns), in_columns)] = held
    for block in range(view.early, view.blocks):
        for start, size in chunks(in_columns):
            weight = stack_rows(view, weights, block, (start, size))
            proj[:, pl.ds(column(block, in_columns, start), size)] = dot(
                normed_ref[...], weight, NN
            ).astype(jnp.bfloat16)

    def apart(block):
        return jnp.concatenate([block * low_lanes, block * high_lanes], axis=0)

    def stacked(block):
        return jnp.concatenate([block[:, :rows], block[:, rows:]], axis=0)

    def lanes(part, pair):
        return pl.ds(pl.multiple_of(part * width + pair * PAIR, PAIR), PAIR)

    chunk = scores.shape[0]
    unroll = min(chunk, 4)

    def each(body):
        @pl.loop(0, chunk // unroll)
        def _(i):
            for inner in range(unroll):
                body(i * unroll + inner)

    for group in range(groups):
        here = pl.ds(group * rows, rows)

        @pl.loop(0, width // (PAIR * chunk))
        def _(part):
            def products(item):
                pair = part * chunk + item
                q_two = apart(proj[here, lanes(0, pair)] * DH ** (-0.5))
                scores[item] = dot(proj[here, lanes(1, pair)], q_two, NT)
                ga_two = apart(ga[here, lanes(0, pair)])
                gprobs[item] = dot(proj[here, lanes(2, pair)], ga_two, NT)

            def softmax(item):
                masked = scores[item] + bias[...]
                expanded = jnp.exp(masked - jnp.max(masked, axis=0, keepdims=True))
                probs = expanded * (1.0 / jnp.sum(expanded, axis=0, keepdims=True))
                low[item, 0] = probs.astype(jnp.bfloat16)
                weighted = probs * gprobs[item]
                delta = jnp.sum(weighted, axis=0, keepdims=True)
                low[item, 1] = (weighted - probs * delta).astype(jnp.bfloat16)

            def results(item):
                pair = part * chunk + item
                probs_low, grad_scores = low[item, 0], low[item, 1]
                q_two = apart(proj[here, lanes(0, pair)] * DH ** (-0.5))
                k_two = apart(proj[here, lanes(1, pair)])
                v_two = apart(proj[here, lanes(2, pair)])
                ga_two = apart(ga[here, lanes(0, pair)])
                att[here, lanes(0, pair)] = dot(stacked(probs_low), v_two, TN).astype(jnp.bfloat16)
                gproj[here, lanes(0, pair)] = (
                    dot(stacked(grad_scores), k_two, TN) * DH ** (-0.5)
                ).astype(jnp.bfloat16)
                gproj[here, lanes(1, pair)] = dot(grad_scores, q_two, NN).astype(jnp.bfloat16)
                gproj[here, lanes(2, pair)] = dot(probs_low, ga_two, NN).astype(jnp.bfloat16)

            each(products)
            each(softmax)
            each(results)

    def store(which, group, value):
        for frame in range(frames):
            out_ref[pl.ds(frame ^ device, 1), which, group * SUB : (group + 1) * SUB, :] = value[
                frame * SUB : (frame + 1) * SUB
            ].reshape(1, SUB, width)

    att_ordered = beside(att, row_starts, row_size)
    for block in range(view.blocks):
        for start, size in chunks(out_columns):
            weight = stack_rows(view, weights, block, (in_columns + start, size))
            wide_sum[:, pl.ds(column(block, out_columns, start), size)] = dot(
                att_ordered, weight, NN
            )

    for group in range(groups):
        here = pl.ds(group * rows, rows)
        wide = load_rows(both_ref, 0, group).astype(jnp.float32)
        store(0, group, (wide + live * wide_sum[here, :]).astype(jnp.bfloat16))

    gproj_ordered = beside(gproj, [column(i, in_columns) for i in range(view.blocks)], in_columns)
    for parts in view.rows:
        weight = stack_columns(view, weights, parts, 0, in_columns)
        put_rows(wide_sum, parts, dot(gproj_ordered, weight, NT))

    for group in range(groups):
        here = pl.ds(group * rows, rows)
        grad = wide_sum[here, :] * gain_ref[...]
        scale = stats_ref[here, 1:2]
        hat = (load_rows(both_ref, 0, group).astype(jnp.float32) - stats_ref[here, 0:1]) * scale
        grad_rows = scale * (
            grad
            - jnp.mean(grad, axis=-1, keepdims=True)
            - hat * jnp.mean(grad * hat, axis=-1, keepdims=True)
        )
        cot = load_rows(both_ref, 1, group).astype(jnp.float32)
        store(1, group, (cot + grad_rows).astype(jnp.bfloat16))


def run_front(gain, shape, sources, view):
    frames, _, patches, width = shape
    total = frames * patches
    vmem = pl.BlockSpec(memory_space=pltpu.VMEM)
    return pl.pallas_call(
        functools.partial(front_kernel, view),
        out_shape=(
            jax.ShapeDtypeStruct(shape, jnp.bfloat16),
            jax.ShapeDtypeStruct((total, width), jnp.bfloat16),
            jax.ShapeDtypeStruct((total, 128), jnp.float32),
            jax.ShapeDtypeStruct((total, view.early * view.in_columns), jnp.bfloat16),
        ),
        in_specs=[vmem] * (1 + len(sources)),
        out_specs=(vmem,) * 4,
        scratch_shapes=[pltpu.VMEM((total, width), jnp.bfloat16)],
        compiler_params=pltpu.CompilerParams(vmem_limit_bytes=VMEM_LIMIT),
        cost_estimate=pl.CostEstimate(flops=total, bytes_accessed=total, transcendentals=0),
        name="front",
    )(gain, *sources)


def run_main(counts, gain, fronted, weights, view):
    both, normed, stats, front = fronted
    frames, _, patches, width = both.shape
    total, rows = frames * patches, frames * SUB
    vmem = pl.BlockSpec(memory_space=pltpu.VMEM)
    smem = pl.BlockSpec(memory_space=pltpu.SMEM)
    chunk = 8 if rows <= 128 else 1
    return pl.pallas_call(
        functools.partial(main_kernel, view),
        out_shape=jax.ShapeDtypeStruct(both.shape, jnp.bfloat16),
        in_specs=[smem] + [vmem] * (5 + len(weights)),
        out_specs=vmem,
        scratch_shapes=[
            pltpu.VMEM((total, width), jnp.bfloat16),
            pltpu.VMEM((total, 3 * width), jnp.bfloat16),
            pltpu.VMEM((total, width), jnp.bfloat16),
            pltpu.VMEM((total, width), jnp.bfloat16),
            pltpu.VMEM((total, 3 * width), jnp.bfloat16),
            pltpu.VMEM((total, width), jnp.float32),
            pltpu.VMEM((rows, 2 * rows), jnp.float32),
            pltpu.VMEM((chunk, rows, 2 * rows), jnp.float32),
            pltpu.VMEM((chunk, rows, 2 * rows), jnp.float32),
            pltpu.VMEM((chunk, 2, rows, 2 * rows), jnp.bfloat16),
        ],
        compiler_params=pltpu.CompilerParams(
            vmem_limit_bytes=VMEM_LIMIT if rows <= 128 else 2 * VMEM_LIMIT
        ),
        cost_estimate=pl.CostEstimate(
            flops=12 * total * width * width,
            bytes_accessed=8 * width * width + 8 * total * width,
            transcendentals=total * 2048,
        ),
        name="main",
    )(counts, gain, both, normed, stats, front, *weights)


class View:
    def __init__(self, blocks, early, rows, in_columns, out_columns, piece, tokens, device, row_order, block_order):
        self.blocks, self.early, self.rows = blocks, early, rows
        self.in_columns, self.out_columns = in_columns, out_columns
        self.piece, self.tokens, self.device = piece, tokens, device
        self.row_order, self.block_order = row_order, block_order


def swap(array, distance, devices):
    return lax.ppermute(array, "frame", [(f, f ^ distance) for f in range(devices)])


def join_kernel(axis, *refs):
    *sources, target = refs
    start = 0
    for source in sources:
        end = start + source.shape[axis]
        if axis == 0:
            target[start:end, :] = source[...]
        else:
            target[:, start:end] = source[...]
        start = end


def join(axis, *arrays):
    shape = list(arrays[0].shape)
    shape[axis] = sum(array.shape[axis] for array in arrays)
    vmem = pl.BlockSpec(memory_space=pltpu.VMEM)
    return pl.pallas_call(
        functools.partial(join_kernel, axis),
        out_shape=jax.ShapeDtypeStruct(shape, arrays[0].dtype),
        in_specs=[vmem] * len(arrays),
        out_specs=vmem,
        compiler_params=SMALL,
        name="join",
    )(*arrays)


def pack_kernel(patches, share, *refs):
    sources, (joined, own, mine, to_x, to_y), held, fetched, sems = (
        refs[:4], refs[4:9], refs[9], refs[10:14], refs[14]
    )
    copies = [
        pltpu.make_async_copy(source, target, sems.at[i])
        for i, (source, target) in enumerate(zip(sources, fetched))
    ]
    for copy in copies:
        copy.start()
    w_in, w_out, tokens, cot = fetched
    depth = w_in.shape[0]
    half, block = depth // 2, 2 * share
    device = lax.axis_index("frame")
    chip, core = device // 2, device % 2
    full = patches // SUB * SUB
    held[:, full:] = jnp.zeros((2, held.shape[1] - full, held.shape[2]), held.dtype)
    wait(copies)
    joined[:, : w_in.shape[1]] = w_in[...]
    joined[:, w_in.shape[1] :] = w_out[...]
    held[0, :patches] = tokens[0, 0]
    held[1, :patches] = cot[0, 0]

    def put(target, row, owner):
        rows = pl.ds(pl.multiple_of(owner * share, share), share)
        target[row : row + share, :] = held[0, rows, :]
        target[row + share : row + block, :] = held[1, rows, :]

    put(mine, 0, device)
    own[:depth, :] = joined[...]
    put(own, depth, device ^ 1)
    for target, first, last, away, core_by in ((to_x, 0, half, 1, 0), (to_y, half, 0, 2, 1)):
        target[:half, :] = joined[first : first + half, :]
        put(target, half, (chip ^ away) * 2)
        put(target, half + block, (chip ^ away) * 2 + 1)
        target[half + 2 * block : depth + 2 * block, :] = joined[last : last + half, :]
        put(target, depth + 2 * block, (chip ^ 3) * 2 + core_by)


def pick_kernel(half, top_ref, bottom_ref, out_ref):
    out_ref[:half, :] = top_ref[:half, :]
    out_ref[half:, :] = bottom_ref[:half, :]


def gather_in_rounds(input_weights, output_weights, tokens, cotangent, gain, share, devices):
    depth, in_columns = input_weights.shape
    out_columns = output_weights.shape[1]
    _, _, patches, width = tokens.shape
    half, block = depth // 2, 2 * share
    vmem = pl.BlockSpec(memory_space=pltpu.VMEM)

    def rows_of(count):
        return jax.ShapeDtypeStruct((count, width), jnp.bfloat16)

    joined, own, mine, to_x, to_y = pl.pallas_call(
        functools.partial(pack_kernel, patches, share),
        out_shape=tuple(
            map(rows_of, (depth, depth + block, block, depth + 3 * block, depth + 3 * block))
        ),
        in_specs=[pl.BlockSpec(memory_space=pltpu.HBM)] * 4,
        out_specs=(vmem,) * 5,
        scratch_shapes=[pltpu.VMEM((2, devices * share, width), jnp.bfloat16)]
        + [pltpu.VMEM(a.shape, a.dtype) for a in (input_weights, output_weights, tokens, cotangent)]
        + [pltpu.SemaphoreType.DMA((4,))],
        compiler_params=pltpu.CompilerParams(vmem_limit_bytes=PACK_LIMIT),
        name="pack",
    )(input_weights, output_weights, tokens, cotangent)

    def by_clip(array, offset):
        return lax.ppermute(array, "clip", [(c, c ^ offset) for c in range(4)])

    def across(array):
        return [swap(array, 2, devices), swap(array, 4, devices)]

    def both_cores(arrays):
        packed = join(0, *arrays)
        return [packed, swap(packed, 1, devices)]

    one, two, three = by_clip(joined, 1), by_clip(joined, 2), by_clip(joined, 3)
    first = [swap(to_x, 2, devices), swap(to_y, 4, devices)]
    tail = half + 2 * block
    first += [swap(first[1][tail:], 2, devices), swap(first[0][tail:], 4, devices)]
    one, first[0], first[1] = lax.optimization_barrier((one, first[0], first[1]))
    second = [one, *across(one)]
    two, three, first[2], first[3] = lax.optimization_barrier((two, three, first[2], first[3]))
    third = [join(0, two, three)]
    diagonal_own = pl.pallas_call(
        functools.partial(pick_kernel, half),
        out_shape=rows_of(depth),
        in_specs=[vmem] * 2,
        out_specs=vmem,
        compiler_params=SMALL,
        name="pick",
    )(first[2], first[3])
    by_diagonal = [by_clip(diagonal_own, 2), by_clip(diagonal_own, 1)]
    second[1], second[2], own, *first = lax.optimization_barrier(
        (second[1], second[2], own, *first)
    )
    ready = both_cores([own, *first]) + both_cores(second)
    third += across(third[0])

    bounds = [0]
    for array in (own, *first):
        bounds.append(bounds[-1] + array.shape[0])

    def tokens_in(sources, both_ref):
        core = lax.axis_index("frame") % 2
        mine_ref, here, there = sources[:3]

        def straight(ref, which):
            start = bounds[which] + half + core * block
            return ref[pl.ds(pl.multiple_of(start, SUB), block), :]

        def diagonal(ref):
            by_x, by_y = (
                ref[bounds[which] + half : bounds[which] + half + block, :] for which in (3, 4)
            )
            return jnp.where(core == 0, by_y, by_x)

        found = (
            mine_ref[...], there[depth : depth + block, :],
            straight(here, 1), straight(there, 1), straight(here, 2), straight(there, 2),
            diagonal(here), diagonal(there),
        )
        for distance, value in enumerate(found):
            both_ref[distance] = value.reshape(2, share, width)

    x_row, y_row, dx_row, dy_row = bounds[1:5]
    table = [
        [
            (0, 0, 0, depth, 0),
            (0, 2, x_row, half, 0), (0, 2, x_row + tail, half, half),
            (0, 4, y_row, half, half), (0, 4, y_row + tail, half, 0),
            (0, 6, dx_row, half, 0), (0, 6, dy_row, half, half),
        ],
        [(1, d, d // 2 * depth, depth, 0) for d in (0, 2, 4)],
        [(2 + i, d, (d + i) * depth, depth, 0) for d in (0, 2, 4) for i in (0, 1)]
        + [(2, 6, 6 * depth, depth, 0), (1, 6, 7 * depth, depth, 0)],
        [(3, 6, 0, half, 0), (3, 6, half, half, half)],
    ]
    arrays = [(core, parts) for parts in table for core in (0, 1)]

    def piece(base):
        def value(refs, offset, distance, first, depth, lanes):
            found = [
                (inside, refs[base + ref][start : start + size, lanes[0] : lanes[0] + lanes[1]])
                for ref, (core, parts) in enumerate(arrays)
                for source, away, start, size, inside in parts
                if (source, away ^ core) == (offset, distance)
            ]
            return jnp.concatenate([held for _, held in sorted(found, key=lambda f: f[0])], axis=0)

        return value

    def view(base):
        return View(
            4,
            1,
            [[(d, 0, depth), (d + 1, 0, depth)] for d in range(0, devices, 2)],
            in_columns,
            out_columns,
            piece(base),
            tokens_in,
            lambda: lax.axis_index("frame"),
            lambda: ([(lax.axis_index("frame") ^ d) * depth for d in range(devices)], depth),
            lambda: [lax.axis_index("clip") ^ offset for offset in range(4)],
        )

    fronted = run_front(gain, (devices, 2, share, width), [mine, *ready[:2]], view(1))
    third[1], third[2], *fronted = lax.optimization_barrier((third[1], third[2], *fronted))
    last = [
        swap(third[2][depth : depth + half], 2, devices),
        swap(third[1][depth + half :], 4, devices),
    ]
    weights = [*ready, *both_cores([*third, *by_diagonal]), *both_cores(last)]
    return fronted, weights, view(0)


def gather_plainly(input_weights, output_weights, tokens, cotangent, gain, share, devices):
    _, slots, patches, width = tokens.shape
    whole = []
    for weights in (input_weights, output_weights):
        columns = lax.all_gather(weights, "clip", axis=1, tiled=True)
        whole.append(lax.all_gather(columns, "frame", axis=0, tiled=True))

    def by_destination(source):
        padded = jnp.pad(source[0], ((0, 0), (0, devices * share - patches), (0, 0)))
        return padded.reshape(slots, devices, share, width).transpose(1, 0, 2, 3)

    both = jnp.stack([by_destination(tokens), by_destination(cotangent)], axis=2)
    both = lax.all_to_all(both, "frame", split_axis=0, concat_axis=0, tiled=True)
    both = both.reshape(devices * slots, 2, share, width)

    def tokens_in(sources, both_ref):
        both_ref[...] = sources[2][...]

    in_columns, out_columns = whole[0].shape[1], whole[1].shape[1]

    def piece(refs, block, index, first, depth, lanes):
        outer = lanes[0] >= in_columns
        start = lanes[0] - in_columns * outer
        return refs[int(outer)][first : first + depth, start : start + lanes[1]]

    step = math.gcd(width, 256)
    view = View(
        1,
        1,
        [[(0, first, step)] for first in range(0, width, step)],
        in_columns,
        out_columns,
        piece,
        tokens_in,
        lambda: 0,
        lambda: ([0], width),
        lambda: [0],
    )
    return run_front(gain, both.shape, [*whole, both], view), whole, view


def per_device(clips, devices, tokens, counts, norm_gain, input_weights, output_weights, cotangent):
    _, slots, patches, width = tokens.shape
    share = -(-patches // devices)
    share = -(-share // SUB) * SUB
    depth, in_columns = input_weights.shape
    fits = in_columns % 128 == 0 and output_weights.shape[1] % 128 == 0 and depth % 32 == 0
    small = clips == 4 and devices == 8 and slots == 1 and fits
    gather = gather_in_rounds if small else gather_plainly
    gain = norm_gain.reshape(1, width)
    fronted, weights, view = gather(
        input_weights, output_weights, tokens, cotangent, gain, share, devices
    )
    back = run_main(counts, gain, fronted, weights, view)
    back = back.reshape(devices, slots, 2, share, width)
    back = lax.all_to_all(back, "frame", split_axis=0, concat_axis=0, tiled=True)

    def in_order(which):
        rows = back[:, :, which].transpose(1, 0, 2, 3).reshape(slots, devices * share, width)
        return rows[None, :, :patches]

    return in_order(0), in_order(1)


def solution(mesh):
    in_specs = (
        P("clip", "frame", None, None),
        P("clip"),
        P(),
        P("frame", "clip"),
        P("frame", "clip"),
        P("clip", "frame", None, None),
    )
    out_specs = (P("clip", "frame", None, None), P("clip", "frame", None, None))
    body = functools.partial(per_device, mesh.shape["clip"], mesh.shape["frame"])
    return jax.shard_map(body, mesh=mesh, in_specs=in_specs, out_specs=out_specs, check_vma=False)
```

```python
import functools
import math

import jax
import jax.numpy as jnp
from jax import lax
from jax.experimental import pallas as pl
from jax.experimental.pallas import tpu as pltpu
from jax.sharding import PartitionSpec as P

DH = 64
PAIR = 2 * DH
SUB = 16
EPSILON = 1e-06
NEGATIVE = -1e30
NN = (((1,), (0,)), ((), ()))
NT = (((1,), (1,)), ((), ()))
TN = (((0,), (0,)), ((), ()))
VMEM_LIMIT = 27 * 1024 * 1024
PACK_LIMIT = 58 * 1024 * 1024
SMALL = pltpu.CompilerParams(vmem_limit_bytes=6 * 1024 * 1024)


def dot(a, b, dims):
    return lax.dot_general(a, b, dims, preferred_element_type=jnp.float32)


def wait(copies):
    for copy in copies:
        copy.wait()


def load_rows(ref, which, group):
    frames, _, _, width = ref.shape
    return ref[:, which, group * SUB : (group + 1) * SUB, :].reshape(frames * SUB, width)


def beside(ref, starts, size):
    return jnp.concatenate(
        [ref[:, pl.ds(pl.multiple_of(start, 128), size)] for start in starts], axis=1
    )


def chunks(columns):
    step = math.gcd(columns, 256)
    return [(start, step) for start in range(0, columns, step)]


def stack_rows(view, refs, block, lanes, groups=None):
    groups = view.rows if groups is None else groups
    return jnp.concatenate(
        [view.piece(refs, block, *part, lanes) for parts in groups for part in parts], axis=0
    )


def stack_columns(view, refs, parts, start, size):
    return jnp.concatenate(
        [
            jnp.concatenate(
                [view.piece(refs, block, *part, (start, size)) for part in parts], axis=0
            )
            for block in range(view.blocks)
        ],
        axis=1,
    )


def front_kernel(view, gain_ref, *refs):
    sources = refs[:-5]
    both_ref, normed_ref, stats_ref, proj_ref, natural = refs[-5:]
    view.tokens(sources, both_ref)
    frames, _, patches, _ = both_ref.shape
    rows = frames * SUB
    for group in range(patches // SUB):
        here = pl.ds(group * rows, rows)
        wide = load_rows(both_ref, 0, group).astype(jnp.float32)
        average = jnp.mean(wide, axis=-1, keepdims=True)
        centred = wide - average
        variance = jnp.mean(centred * centred, axis=-1, keepdims=True)
        scale = lax.rsqrt(variance + EPSILON)
        natural[here, :] = (centred * scale * gain_ref[...]).astype(jnp.bfloat16)
        stats_ref[here, 0:1] = average
        stats_ref[here, 1:2] = scale
    normed_ref[...] = beside(natural, *view.row_order())
    for block in range(view.early):
        for start, size in chunks(view.in_columns):
            weight = stack_rows(view, sources, block, (start, size))
            here = pl.ds(block * view.in_columns + start, size)
            proj_ref[:, here] = dot(normed_ref[...], weight, NN).astype(jnp.bfloat16)


def put_rows(view, target, parts, value):
    row_starts, _ = view.row_order()
    done = 0
    for index, first, depth in parts:
        start = pl.multiple_of(row_starts[index] + first, 128)
        target[:, pl.ds(start, depth)] = value[:, done : done + depth]
        done += depth


def live_rows(view, counts_ref, rows):
    frame = (lax.broadcasted_iota(jnp.int32, (rows, 1), 0) // SUB) ^ view.device()
    return (frame < counts_ref[0]).astype(jnp.float32)


def masked_cotangent(view, counts_ref, both_ref, natural):
    frames, _, patches, _ = both_ref.shape
    rows = frames * SUB
    live = live_rows(view, counts_ref, rows)
    for group in range(patches // SUB):
        wide = load_rows(both_ref, 1, group).astype(jnp.float32)
        natural[pl.ds(group * rows, rows), :] = (wide * live).astype(jnp.bfloat16)
    starts = [block * view.out_columns for block in view.block_order()]
    return beside(natural, starts, view.out_columns)


def grad_attended(view, weights, ordered, groups, target):
    for parts in groups:
        weight = stack_columns(view, weights, parts, view.in_columns, view.out_columns)
        put_rows(view, target, parts, dot(ordered, weight, NT).astype(jnp.bfloat16))


def early_depth(view):
    return sum(part[2] for parts in view.early_rows for part in parts)


def middle_kernel(view, counts_ref, both_ref, normed_ref, *rest):
    weights = rest[:-4]
    ordered_ref, ga_ref, partial_ref, natural = rest[-4:]
    ordered_ref[...] = masked_cotangent(view, counts_ref, both_ref, natural)
    grad_attended(view, weights, ordered_ref[...], view.early_rows, ga_ref)
    depth = early_depth(view)
    for block in range(view.early, view.blocks):
        for start, size in chunks(view.in_columns):
            weight = stack_rows(view, weights, block, (start, size), view.early_rows)
            here = pl.ds((block - view.early) * view.in_columns + start, size)
            partial_ref[:, here] = dot(normed_ref[:, :depth], weight, NN)


def main_kernel(view, counts_ref, gain_ref, both_ref, normed_ref, stats_ref, front_ref, *rest):
    weights = rest[:-10]
    out_ref, proj, ga, att, gproj, wide_sum, bias, scores, gprobs, low = rest[-10:]
    middle = weights[:3] if view.early_rows else None
    weights = weights[3:] if view.early_rows else weights
    frames, _, patches, width = both_ref.shape
    groups = patches // SUB
    rows = frames * SUB
    count = counts_ref[0]
    device = view.device()
    in_columns, out_columns = view.in_columns, view.out_columns
    row_starts, row_size = view.row_order()
    block_order = view.block_order()

    def column(block, stride, start=0):
        return pl.multiple_of(block_order[block] * stride + start, 128)

    def real(index):
        return ((index // SUB) ^ device) < count

    live = live_rows(view, counts_ref, rows)
    key = lax.broadcasted_iota(jnp.int32, (rows, 2 * rows), 0)
    query = lax.broadcasted_iota(jnp.int32, (rows, 2 * rows), 1)
    bias[...] = jnp.where((query % SUB == key % SUB) & real(key), 0.0, NEGATIVE)
    lane = lax.broadcasted_iota(jnp.int32, (1, PAIR), 1)
    low_lanes = (lane < DH).astype(jnp.bfloat16)
    high_lanes = (lane >= DH).astype(jnp.bfloat16)

    depth = early_depth(view)
    late_rows = view.rows[len(view.early_rows) :]
    if middle:
        ordered, ga_early, partial = middle
        ga[...] = ga_early[...]
        grad_attended(view, weights, ordered[...], late_rows, ga)
    else:
        ordered = masked_cotangent(view, counts_ref, both_ref, att)
        grad_attended(view, weights, ordered, late_rows, ga)

    for block in range(view.early):
        held = front_ref[:, block * in_columns : (block + 1) * in_columns]
        proj[:, pl.ds(column(block, in_columns), in_columns)] = held
    for block in range(view.early, view.blocks):
        for start, size in chunks(in_columns):
            weight = stack_rows(view, weights, block, (start, size), late_rows)
            value = dot(normed_ref[:, depth:], weight, NN)
            if middle:
                here = pl.ds((block - view.early) * in_columns + start, size)
                value = value + partial[:, here]
            proj[:, pl.ds(column(block, in_columns, start), size)] = value.astype(jnp.bfloat16)

    def apart(block):
        return jnp.concatenate([block * low_lanes, block * high_lanes], axis=0)

    def stacked(block):
        return jnp.concatenate([block[:, :rows], block[:, rows:]], axis=0)

    def lanes(part, pair):
        return pl.ds(pl.multiple_of(part * width + pair * PAIR, PAIR), PAIR)

    chunk = scores.shape[0]
    unroll = min(chunk, 4)

    def each(body):
        @pl.loop(0, chunk // unroll)
        def _(i):
            for inner in range(unroll):
                body(i * unroll + inner)

    for group in range(groups):
        here = pl.ds(group * rows, rows)

        @pl.loop(0, width // (PAIR * chunk))
        def _(part):
            def products(item):
                pair = part * chunk + item
                q_two = apart(proj[here, lanes(0, pair)] * DH ** (-0.5))
                scores[item] = dot(proj[here, lanes(1, pair)], q_two, NT)
                ga_two = apart(ga[here, lanes(0, pair)])
                gprobs[item] = dot(proj[here, lanes(2, pair)], ga_two, NT)

            def softmax(item):
                masked = scores[item] + bias[...]
                expanded = jnp.exp(masked - jnp.max(masked, axis=0, keepdims=True))
                probs = expanded * (1.0 / jnp.sum(expanded, axis=0, keepdims=True))
                low[item, 0] = probs.astype(jnp.bfloat16)
                weighted = probs * gprobs[item]
                delta = jnp.sum(weighted, axis=0, keepdims=True)
                low[item, 1] = (weighted - probs * delta).astype(jnp.bfloat16)

            def results(item):
                pair = part * chunk + item
                probs_low, grad_scores = low[item, 0], low[item, 1]
                q_two = apart(proj[here, lanes(0, pair)] * DH ** (-0.5))
                k_two = apart(proj[here, lanes(1, pair)])
                v_two = apart(proj[here, lanes(2, pair)])
                ga_two = apart(ga[here, lanes(0, pair)])
                att[here, lanes(0, pair)] = dot(stacked(probs_low), v_two, TN).astype(jnp.bfloat16)
                gproj[here, lanes(0, pair)] = (
                    dot(stacked(grad_scores), k_two, TN) * DH ** (-0.5)
                ).astype(jnp.bfloat16)
                gproj[here, lanes(1, pair)] = dot(grad_scores, q_two, NN).astype(jnp.bfloat16)
                gproj[here, lanes(2, pair)] = dot(probs_low, ga_two, NN).astype(jnp.bfloat16)

            each(products)
            each(softmax)
            each(results)

    def store(which, group, value):
        for frame in range(frames):
            out_ref[pl.ds(frame ^ device, 1), which, group * SUB : (group + 1) * SUB, :] = value[
                frame * SUB : (frame + 1) * SUB
            ].reshape(1, SUB, width)

    att_ordered = beside(att, row_starts, row_size)
    for block in range(view.blocks):
        for start, size in chunks(out_columns):
            weight = stack_rows(view, weights, block, (in_columns + start, size))
            wide_sum[:, pl.ds(column(block, out_columns, start), size)] = dot(
                att_ordered, weight, NN
            )

    for group in range(groups):
        here = pl.ds(group * rows, rows)
        wide = load_rows(both_ref, 0, group).astype(jnp.float32)
        store(0, group, (wide + live * wide_sum[here, :]).astype(jnp.bfloat16))

    gproj_ordered = beside(gproj, [column(i, in_columns) for i in range(view.blocks)], in_columns)
    for parts in view.rows:
        weight = stack_columns(view, weights, parts, 0, in_columns)
        put_rows(view, wide_sum, parts, dot(gproj_ordered, weight, NT))

    for group in range(groups):
        here = pl.ds(group * rows, rows)
        grad = wide_sum[here, :] * gain_ref[...]
        scale = stats_ref[here, 1:2]
        hat = (load_rows(both_ref, 0, group).astype(jnp.float32) - stats_ref[here, 0:1]) * scale
        grad_rows = scale * (
            grad
            - jnp.mean(grad, axis=-1, keepdims=True)
            - hat * jnp.mean(grad * hat, axis=-1, keepdims=True)
        )
        cot = load_rows(both_ref, 1, group).astype(jnp.float32)
        store(1, group, (cot + grad_rows).astype(jnp.bfloat16))


def run_front(gain, shape, sources, view):
    frames, _, patches, width = shape
    total = frames * patches
    vmem = pl.BlockSpec(memory_space=pltpu.VMEM)
    return pl.pallas_call(
        functools.partial(front_kernel, view),
        out_shape=(
            jax.ShapeDtypeStruct(shape, jnp.bfloat16),
            jax.ShapeDtypeStruct((total, width), jnp.bfloat16),
            jax.ShapeDtypeStruct((total, 128), jnp.float32),
            jax.ShapeDtypeStruct((total, view.early * view.in_columns), jnp.bfloat16),
        ),
        in_specs=[vmem] * (1 + len(sources)),
        out_specs=(vmem,) * 4,
        scratch_shapes=[pltpu.VMEM((total, width), jnp.bfloat16)],
        compiler_params=pltpu.CompilerParams(vmem_limit_bytes=VMEM_LIMIT),
        cost_estimate=pl.CostEstimate(flops=total, bytes_accessed=total, transcendentals=0),
        name="front",
    )(gain, *sources)


def run_middle(counts, fronted, weights, view):
    both, normed, _, _ = fronted
    total, width = normed.shape
    vmem = pl.BlockSpec(memory_space=pltpu.VMEM)
    columns = (view.blocks - view.early) * view.in_columns
    return pl.pallas_call(
        functools.partial(middle_kernel, view),
        out_shape=(
            jax.ShapeDtypeStruct((total, width), jnp.bfloat16),
            jax.ShapeDtypeStruct((total, width), jnp.bfloat16),
            jax.ShapeDtypeStruct((total, columns), jnp.float32),
        ),
        in_specs=[pl.BlockSpec(memory_space=pltpu.SMEM)] + [vmem] * (2 + len(weights)),
        out_specs=(vmem,) * 3,
        scratch_shapes=[pltpu.VMEM((total, width), jnp.bfloat16)],
        compiler_params=pltpu.CompilerParams(vmem_limit_bytes=VMEM_LIMIT),
        cost_estimate=pl.CostEstimate(flops=total, bytes_accessed=total, transcendentals=0),
        name="middle",
    )(counts, both, normed, *weights)


def run_main(counts, gain, fronted, weights, view):
    both, normed, stats, front = fronted
    frames, _, patches, width = both.shape
    total, rows = frames * patches, frames * SUB
    vmem = pl.BlockSpec(memory_space=pltpu.VMEM)
    smem = pl.BlockSpec(memory_space=pltpu.SMEM)
    chunk = 8 if rows <= 128 else 1
    return pl.pallas_call(
        functools.partial(main_kernel, view),
        out_shape=jax.ShapeDtypeStruct(both.shape, jnp.bfloat16),
        in_specs=[smem] + [vmem] * (5 + len(weights)),
        out_specs=vmem,
        scratch_shapes=[
            pltpu.VMEM((total, 3 * width), jnp.bfloat16),
            pltpu.VMEM((total, width), jnp.bfloat16),
            pltpu.VMEM((total, width), jnp.bfloat16),
            pltpu.VMEM((total, 3 * width), jnp.bfloat16),
            pltpu.VMEM((total, width), jnp.float32),
            pltpu.VMEM((rows, 2 * rows), jnp.float32),
            pltpu.VMEM((chunk, rows, 2 * rows), jnp.float32),
            pltpu.VMEM((chunk, rows, 2 * rows), jnp.float32),
            pltpu.VMEM((chunk, 2, rows, 2 * rows), jnp.bfloat16),
        ],
        compiler_params=pltpu.CompilerParams(
            vmem_limit_bytes=VMEM_LIMIT if rows <= 128 else 2 * VMEM_LIMIT
        ),
        cost_estimate=pl.CostEstimate(
            flops=12 * total * width * width,
            bytes_accessed=8 * width * width + 8 * total * width,
            transcendentals=total * 2048,
        ),
        name="main",
    )(counts, gain, both, normed, stats, front, *weights)


class View:
    def __init__(self, blocks, early, rows, early_rows, in_columns, out_columns, piece, tokens, device, row_order, block_order):
        self.blocks, self.early = blocks, early
        self.rows, self.early_rows = rows, early_rows
        self.in_columns, self.out_columns = in_columns, out_columns
        self.piece, self.tokens, self.device = piece, tokens, device
        self.row_order, self.block_order = row_order, block_order


def swap(array, distance, devices):
    return lax.ppermute(array, "frame", [(f, f ^ distance) for f in range(devices)])


def join_kernel(axis, *refs):
    *sources, target = refs
    start = 0
    for source in sources:
        end = start + source.shape[axis]
        if axis == 0:
            target[start:end, :] = source[...]
        else:
            target[:, start:end] = source[...]
        start = end


def join(axis, *arrays):
    shape = list(arrays[0].shape)
    shape[axis] = sum(array.shape[axis] for array in arrays)
    vmem = pl.BlockSpec(memory_space=pltpu.VMEM)
    return pl.pallas_call(
        functools.partial(join_kernel, axis),
        out_shape=jax.ShapeDtypeStruct(shape, arrays[0].dtype),
        in_specs=[vmem] * len(arrays),
        out_specs=vmem,
        compiler_params=SMALL,
        name="join",
    )(*arrays)


def pack_kernel(patches, share, *refs):
    sources, (joined, own, mine, to_x, to_y), held, fetched, sems = (
        refs[:4], refs[4:9], refs[9], refs[10:14], refs[14]
    )
    copies = [
        pltpu.make_async_copy(source, target, sems.at[i])
        for i, (source, target) in enumerate(zip(sources, fetched))
    ]
    for copy in copies:
        copy.start()
    w_in, w_out, tokens, cot = fetched
    depth = w_in.shape[0]
    half, block = depth // 2, 2 * share
    device = lax.axis_index("frame")
    chip, core = device // 2, device % 2
    full = patches // SUB * SUB
    held[:, full:] = jnp.zeros((2, held.shape[1] - full, held.shape[2]), held.dtype)
    wait(copies)
    joined[:, : w_in.shape[1]] = w_in[...]
    joined[:, w_in.shape[1] :] = w_out[...]
    held[0, :patches] = tokens[0, 0]
    held[1, :patches] = cot[0, 0]

    def put(target, row, owner):
        rows = pl.ds(pl.multiple_of(owner * share, share), share)
        target[row : row + share, :] = held[0, rows, :]
        target[row + share : row + block, :] = held[1, rows, :]

    put(mine, 0, device)
    own[:depth, :] = joined[...]
    put(own, depth, device ^ 1)
    for target, first, last, away, core_by in ((to_x, 0, half, 1, 0), (to_y, half, 0, 2, 1)):
        target[:half, :] = joined[first : first + half, :]
        put(target, half, (chip ^ away) * 2)
        put(target, half + block, (chip ^ away) * 2 + 1)
        target[half + 2 * block : depth + 2 * block, :] = joined[last : last + half, :]
        put(target, depth + 2 * block, (chip ^ 3) * 2 + core_by)


def turn_kernel(half, by_x, by_y, pair_x, pair_y, to_dx, to_dy):
    to_dx[:half, :] = by_y[:half, :]
    to_dx[half:, :] = pair_y[: 2 * half, :]
    to_dy[:half, :] = by_x[half:, :]
    to_dy[half:, :] = pair_x[2 * half :, :]


def gather_in_rounds(
    counts, input_weights, output_weights, tokens, cotangent, gain, share, devices
):
    depth, in_columns = input_weights.shape
    out_columns = output_weights.shape[1]
    _, _, patches, width = tokens.shape
    half, block = depth // 2, 2 * share
    vmem = pl.BlockSpec(memory_space=pltpu.VMEM)

    def rows_of(count):
        return jax.ShapeDtypeStruct((count, width), jnp.bfloat16)

    joined, own, mine, to_x, to_y = pl.pallas_call(
        functools.partial(pack_kernel, patches, share),
        out_shape=tuple(
            map(rows_of, (depth, depth + block, block, depth + 3 * block, depth + 3 * block))
        ),
        in_specs=[pl.BlockSpec(memory_space=pltpu.HBM)] * 4,
        out_specs=(vmem,) * 5,
        scratch_shapes=[pltpu.VMEM((2, devices * share, width), jnp.bfloat16)]
        + [pltpu.VMEM(a.shape, a.dtype) for a in (input_weights, output_weights, tokens, cotangent)]
        + [pltpu.SemaphoreType.DMA((4,))],
        compiler_params=pltpu.CompilerParams(vmem_limit_bytes=PACK_LIMIT),
        name="pack",
    )(input_weights, output_weights, tokens, cotangent)

    def by_clip(array, offset):
        return lax.ppermute(array, "clip", [(c, c ^ offset) for c in range(4)])

    def across(array):
        return [swap(array, 2, devices), swap(array, 4, devices)]

    def other_core(arrays):
        return [swap(array, 1, devices) for array in arrays]

    one, two, three = by_clip(joined, 1), by_clip(joined, 2), by_clip(joined, 3)
    first = [swap(to_x, 2, devices), swap(to_y, 4, devices)]
    tail = half + 2 * block
    first += [swap(first[1][tail:], 2, devices), swap(first[0][tail:], 4, devices)]
    one, first[0], first[1] = lax.optimization_barrier((one, first[0], first[1]))
    second = [one, *across(one)]
    two, three, first[2], first[3] = lax.optimization_barrier((two, three, first[2], first[3]))
    third = [join(0, two, three)]
    third += across(third[0])
    second[1], second[2], own, third[0], *first = lax.optimization_barrier(
        (second[1], second[2], own, third[0], *first)
    )
    first_other = other_core([own, *first])
    second_other = other_core(second)
    ready = [joined, *first, *first_other, *second, *second_other]

    def tokens_in(sources, both_ref):
        core = lax.axis_index("frame") % 2
        mine_ref, _, x_ref, y_ref, dx_ref, dy_ref, own2, x2, y2, dx2, dy2 = sources[:11]
        rows = pl.ds(pl.multiple_of(half + core * block, block), block)
        behind = slice(half, half + block)

        def diagonal(by_x, by_y):
            return jnp.where(core == 0, by_y[behind, :], by_x[behind, :])

        found = (
            mine_ref[...], own2[depth : depth + block, :],
            x_ref[rows, :], x2[rows, :], y_ref[rows, :], y2[rows, :],
            diagonal(dx_ref, dy_ref), diagonal(dx2, dy2),
        )
        for distance, value in enumerate(found):
            both_ref[distance] = value.reshape(2, share, width)

    table = [
        [(0, 0, 0, depth, 0)],
        [(0, 2, 0, half, 0), (0, 2, tail, half, half)],
        [(0, 4, 0, half, half), (0, 4, tail, half, 0)],
        [(0, 6, 0, half, 0)],
        [(0, 6, 0, half, half)],
    ]
    others = [[(1, d, 0, depth, 0)] for d in (0, 2, 4)]
    pairs = [[(2, d, 0, depth, 0), (3, d, depth, depth, 0)] for d in (0, 2, 4)]
    long = half + depth
    pairs += [
        [
            (1, 6, 0, half, 0), (2, 6, half, depth, 0),
            (1, 6, long, half, half), (3, 6, long + half, depth, 0),
        ],
    ]
    arrays = []
    for group in (table, others, pairs):
        arrays += [(core, parts) for core in (0, 1) for parts in group]

    def piece(present):
        def value(refs, offset, distance, first, depth, lanes):
            found = [
                (inside, refs[present.index(ref)][start : start + size, lanes[0] : lanes[0] + lanes[1]])
                for ref, (core, parts) in enumerate(arrays)
                for source, away, start, size, inside in parts
                if (source, away ^ core) == (offset, distance)
            ]
            return jnp.concatenate([held for _, held in sorted(found, key=lambda f: f[0])], axis=0)

        return value

    row_groups = [[(d, 0, depth), (d + 1, 0, depth)] for d in range(0, devices, 2)]

    def view(present):
        return View(
            4,
            1,
            row_groups,
            row_groups[:3],
            in_columns,
            out_columns,
            piece(present),
            tokens_in,
            lambda: lax.axis_index("frame"),
            lambda: ([(lax.axis_index("frame") ^ d) * depth for d in range(devices)], depth),
            lambda: [lax.axis_index("clip") ^ offset for offset in range(4)],
        )

    fronted = run_front(
        gain, (devices, 2, share, width), [mine, *ready[:10]], view([None, *range(10)])
    )
    to_dx, to_dy = pl.pallas_call(
        functools.partial(turn_kernel, half),
        out_shape=(rows_of(depth + half), rows_of(depth + half)),
        in_specs=[vmem] * 4,
        out_specs=(vmem, vmem),
        compiler_params=SMALL,
        name="turn",
    )(second[1], second[2], third[1], third[2])
    last = [swap(to_dx, 2, devices), swap(to_dy, 4, devices)]
    third_other = other_core(third)
    middle = run_middle(
        counts, fronted, [*ready, *third, *third_other], view([*range(16), 16, 17, 18, 20, 21, 22])
    )
    last[0], *middle = lax.optimization_barrier((last[0], *middle))
    last = join(0, *last)
    weights = [*middle, *ready, *third, last, *third_other, swap(last, 1, devices)]
    return fronted, weights, view(list(range(24)))


def gather_plainly(
    counts, input_weights, output_weights, tokens, cotangent, gain, share, devices
):
    _, slots, patches, width = tokens.shape
    whole = []
    for weights in (input_weights, output_weights):
        columns = lax.all_gather(weights, "clip", axis=1, tiled=True)
        whole.append(lax.all_gather(columns, "frame", axis=0, tiled=True))

    def by_destination(source):
        padded = jnp.pad(source[0], ((0, 0), (0, devices * share - patches), (0, 0)))
        return padded.reshape(slots, devices, share, width).transpose(1, 0, 2, 3)

    both = jnp.stack([by_destination(tokens), by_destination(cotangent)], axis=2)
    both = lax.all_to_all(both, "frame", split_axis=0, concat_axis=0, tiled=True)
    both = both.reshape(devices * slots, 2, share, width)

    def tokens_in(sources, both_ref):
        both_ref[...] = sources[2][...]

    in_columns, out_columns = whole[0].shape[1], whole[1].shape[1]

    def piece(refs, block, index, first, depth, lanes):
        outer = lanes[0] >= in_columns
        start = lanes[0] - in_columns * outer
        return refs[int(outer)][first : first + depth, start : start + lanes[1]]

    step = math.gcd(width, 256)
    view = View(
        1,
        1,
        [[(0, first, step)] for first in range(0, width, step)],
        [],
        in_columns,
        out_columns,
        piece,
        tokens_in,
        lambda: 0,
        lambda: ([0], width),
        lambda: [0],
    )
    return run_front(gain, both.shape, [*whole, both], view), whole, view


def per_device(clips, devices, tokens, counts, norm_gain, input_weights, output_weights, cotangent):
    _, slots, patches, width = tokens.shape
    share = -(-patches // devices)
    share = -(-share // SUB) * SUB
    depth, in_columns = input_weights.shape
    fits = in_columns % 128 == 0 and output_weights.shape[1] % 128 == 0 and depth % 32 == 0
    small = clips == 4 and devices == 8 and slots == 1 and fits
    gather = gather_in_rounds if small else gather_plainly
    gain = norm_gain.reshape(1, width)
    fronted, weights, view = gather(
        counts, input_weights, output_weights, tokens, cotangent, gain, share, devices
    )
    back = run_main(counts, gain, fronted, weights, view)
    back = back.reshape(devices, slots, 2, share, width)
    back = lax.all_to_all(back, "frame", split_axis=0, concat_axis=0, tiled=True)

    def in_order(which):
        rows = back[:, :, which].transpose(1, 0, 2, 3).reshape(slots, devices * share, width)
        return rows[None, :, :patches]

    return in_order(0), in_order(1)


def solution(mesh):
    in_specs = (
        P("clip", "frame", None, None),
        P("clip"),
        P(),
        P("frame", "clip"),
        P("frame", "clip"),
        P("clip", "frame", None, None),
    )
    out_specs = (P("clip", "frame", None, None), P("clip", "frame", None, None))
    body = functools.partial(per_device, mesh.shape["clip"], mesh.shape["frame"])
    return jax.shard_map(body, mesh=mesh, in_specs=in_specs, out_specs=out_specs, check_vma=False)
```

```python
import functools
import math

import jax
import jax.numpy as jnp
from jax import lax
from jax.experimental import pallas as pl
from jax.experimental.pallas import tpu as pltpu
from jax.sharding import PartitionSpec as P

DH = 64
PAIR = 2 * DH
SUB = 16
EPSILON = 1e-06
NEGATIVE = -1e30
NN = (((1,), (0,)), ((), ()))
NT = (((1,), (1,)), ((), ()))
TN = (((0,), (0,)), ((), ()))
VMEM_LIMIT = 27 * 1024 * 1024
PACK_LIMIT = 58 * 1024 * 1024
SMALL = pltpu.CompilerParams(vmem_limit_bytes=6 * 1024 * 1024)


def dot(a, b, dims):
    return lax.dot_general(a, b, dims, preferred_element_type=jnp.float32)


def wait(copies):
    for copy in copies:
        copy.wait()


def load_rows(ref, which, group):
    frames, _, _, width = ref.shape
    return ref[:, which, group * SUB : (group + 1) * SUB, :].reshape(frames * SUB, width)


def beside(ref, starts, size):
    return jnp.concatenate(
        [ref[:, pl.ds(pl.multiple_of(start, 128), size)] for start in starts], axis=1
    )


def chunks(columns):
    step = math.gcd(columns, 256)
    return [(start, step) for start in range(0, columns, step)]


def stack_rows(view, refs, block, lanes, groups=None):
    groups = view.rows if groups is None else groups
    return jnp.concatenate(
        [view.piece(refs, block, *part, lanes) for parts in groups for part in parts], axis=0
    )


def stack_columns(view, refs, parts, start, size):
    return jnp.concatenate(
        [
            jnp.concatenate(
                [view.piece(refs, block, *part, (start, size)) for part in parts], axis=0
            )
            for block in range(view.blocks)
        ],
        axis=1,
    )


def front_kernel(view, gain_ref, *refs):
    sources = refs[:-5]
    both_ref, normed_ref, stats_ref, proj_ref, natural = refs[-5:]
    view.tokens(sources, both_ref)
    frames, _, patches, _ = both_ref.shape
    rows = frames * SUB
    for group in range(patches // SUB):
        here = pl.ds(group * rows, rows)
        wide = load_rows(both_ref, 0, group).astype(jnp.float32)
        average = jnp.mean(wide, axis=-1, keepdims=True)
        centred = wide - average
        variance = jnp.mean(centred * centred, axis=-1, keepdims=True)
        scale = lax.rsqrt(variance + EPSILON)
        natural[here, :] = (centred * scale * gain_ref[...]).astype(jnp.bfloat16)
        stats_ref[here, 0:1] = average
        stats_ref[here, 1:2] = scale
    normed_ref[...] = beside(natural, *view.row_order())
    for block in range(view.early):
        for start, size in chunks(view.in_columns):
            weight = stack_rows(view, sources, block, (start, size))
            here = pl.ds(block * view.in_columns + start, size)
            proj_ref[:, here] = dot(normed_ref[...], weight, NN).astype(jnp.bfloat16)


def put_rows(view, target, parts, value):
    row_starts, _ = view.row_order()
    done = 0
    for index, first, depth in parts:
        start = pl.multiple_of(row_starts[index] + first, 128)
        target[:, pl.ds(start, depth)] = value[:, done : done + depth]
        done += depth


def live_rows(view, counts_ref, rows):
    frame = (lax.broadcasted_iota(jnp.int32, (rows, 1), 0) // SUB) ^ view.device()
    return (frame < counts_ref[0]).astype(jnp.float32)


def masked_cotangent(view, counts_ref, both_ref, natural):
    frames, _, patches, _ = both_ref.shape
    rows = frames * SUB
    live = live_rows(view, counts_ref, rows)
    for group in range(patches // SUB):
        wide = load_rows(both_ref, 1, group).astype(jnp.float32)
        natural[pl.ds(group * rows, rows), :] = (wide * live).astype(jnp.bfloat16)
    starts = [block * view.out_columns for block in view.block_order()]
    return beside(natural, starts, view.out_columns)


def grad_attended(view, weights, ordered, groups, target):
    for parts in groups:
        weight = stack_columns(view, weights, parts, view.in_columns, view.out_columns)
        put_rows(view, target, parts, dot(ordered, weight, NT).astype(jnp.bfloat16))


def early_depth(view):
    return sum(part[2] for parts in view.early_rows for part in parts)


def middle_kernel(view, counts_ref, both_ref, normed_ref, *rest):
    weights = rest[:-4]
    ordered_ref, ga_ref, partial_ref, natural = rest[-4:]
    ordered_ref[...] = masked_cotangent(view, counts_ref, both_ref, natural)
    grad_attended(view, weights, ordered_ref[...], view.early_rows, ga_ref)
    depth = early_depth(view)
    for block in range(view.early, view.blocks):
        for start, size in chunks(view.in_columns):
            weight = stack_rows(view, weights, block, (start, size), view.early_rows)
            here = pl.ds((block - view.early) * view.in_columns + start, size)
            partial_ref[:, here] = dot(normed_ref[:, :depth], weight, NN)


def main_kernel(view, counts_ref, gain_ref, both_ref, normed_ref, stats_ref, front_ref, *rest):
    weights = rest[:-10]
    out_ref, proj, ga, att, gproj, wide_sum, bias, scores, gprobs, low = rest[-10:]
    middle = weights[:3] if view.early_rows else None
    weights = weights[3:] if view.early_rows else weights
    frames, _, patches, width = both_ref.shape
    groups = patches // SUB
    rows = frames * SUB
    count = counts_ref[0]
    device = view.device()
    in_columns, out_columns = view.in_columns, view.out_columns
    row_starts, row_size = view.row_order()
    block_order = view.block_order()

    def column(block, stride, start=0):
        return pl.multiple_of(block_order[block] * stride + start, 128)

    def real(index):
        return ((index // SUB) ^ device) < count

    live = live_rows(view, counts_ref, rows)
    key = lax.broadcasted_iota(jnp.int32, (rows, 2 * rows), 0)
    query = lax.broadcasted_iota(jnp.int32, (rows, 2 * rows), 1)
    bias[...] = jnp.where((query % SUB == key % SUB) & real(key), 0.0, NEGATIVE)
    lane = lax.broadcasted_iota(jnp.int32, (1, PAIR), 1)
    low_lanes = (lane < DH).astype(jnp.bfloat16)
    high_lanes = (lane >= DH).astype(jnp.bfloat16)

    depth = early_depth(view)
    late_rows = view.rows[len(view.early_rows) :]
    if middle:
        ordered, ga_early, partial = middle
        ga[...] = ga_early[...]
        grad_attended(view, weights, ordered[...], late_rows, ga)
    else:
        ordered = masked_cotangent(view, counts_ref, both_ref, att)
        grad_attended(view, weights, ordered, late_rows, ga)

    for block in range(view.early):
        held = front_ref[:, block * in_columns : (block + 1) * in_columns]
        proj[:, pl.ds(column(block, in_columns), in_columns)] = held
    for block in range(view.early, view.blocks):
        for start, size in chunks(in_columns):
            weight = stack_rows(view, weights, block, (start, size), late_rows)
            value = dot(normed_ref[:, depth:], weight, NN)
            if middle:
                here = pl.ds((block - view.early) * in_columns + start, size)
                value = value + partial[:, here]
            proj[:, pl.ds(column(block, in_columns, start), size)] = value.astype(jnp.bfloat16)

    def apart(block):
        return jnp.concatenate([block * low_lanes, block * high_lanes], axis=0)

    def stacked(block):
        return jnp.concatenate([block[:, :rows], block[:, rows:]], axis=0)

    def lanes(part, pair):
        return pl.ds(pl.multiple_of(part * width + pair * PAIR, PAIR), PAIR)

    chunk = scores.shape[0]
    unroll = min(chunk, 4)

    def each(body):
        @pl.loop(0, chunk // unroll)
        def _(i):
            for inner in range(unroll):
                body(i * unroll + inner)

    for group in range(groups):
        here = pl.ds(group * rows, rows)

        @pl.loop(0, width // (PAIR * chunk))
        def _(part):
            def products(item):
                pair = part * chunk + item
                q_two = apart(proj[here, lanes(0, pair)] * DH ** (-0.5))
                scores[item] = dot(proj[here, lanes(1, pair)], q_two, NT)
                ga_two = apart(ga[here, lanes(0, pair)])
                gprobs[item] = dot(proj[here, lanes(2, pair)], ga_two, NT)

            def softmax(item):
                masked = scores[item] + bias[...]
                expanded = jnp.exp(masked - jnp.max(masked, axis=0, keepdims=True))
                probs = expanded * (1.0 / jnp.sum(expanded, axis=0, keepdims=True))
                low[item, 0] = probs.astype(jnp.bfloat16)
                weighted = probs * gprobs[item]
                delta = jnp.sum(weighted, axis=0, keepdims=True)
                low[item, 1] = (weighted - probs * delta).astype(jnp.bfloat16)

            def results(item):
                pair = part * chunk + item
                probs_low, grad_scores = low[item, 0], low[item, 1]
                q_two = apart(proj[here, lanes(0, pair)] * DH ** (-0.5))
                k_two = apart(proj[here, lanes(1, pair)])
                v_two = apart(proj[here, lanes(2, pair)])
                ga_two = apart(ga[here, lanes(0, pair)])
                att[here, lanes(0, pair)] = dot(stacked(probs_low), v_two, TN).astype(jnp.bfloat16)
                gproj[here, lanes(0, pair)] = (
                    dot(stacked(grad_scores), k_two, TN) * DH ** (-0.5)
                ).astype(jnp.bfloat16)
                gproj[here, lanes(1, pair)] = dot(grad_scores, q_two, NN).astype(jnp.bfloat16)
                gproj[here, lanes(2, pair)] = dot(probs_low, ga_two, NN).astype(jnp.bfloat16)

            each(products)
            each(softmax)
            each(results)

    def store(which, group, value):
        for frame in range(frames):
            out_ref[pl.ds(frame ^ device, 1), which, group * SUB : (group + 1) * SUB, :] = value[
                frame * SUB : (frame + 1) * SUB
            ].reshape(1, SUB, width)

    att_ordered = beside(att, row_starts, row_size)
    for block in range(view.blocks):
        for start, size in chunks(out_columns):
            weight = stack_rows(view, weights, block, (in_columns + start, size))
            wide_sum[:, pl.ds(column(block, out_columns, start), size)] = dot(
                att_ordered, weight, NN
            )

    for group in range(groups):
        here = pl.ds(group * rows, rows)
        wide = load_rows(both_ref, 0, group).astype(jnp.float32)
        store(0, group, (wide + live * wide_sum[here, :]).astype(jnp.bfloat16))

    gproj_ordered = beside(gproj, [column(i, in_columns) for i in range(view.blocks)], in_columns)
    for parts in view.rows:
        weight = stack_columns(view, weights, parts, 0, in_columns)
        put_rows(view, wide_sum, parts, dot(gproj_ordered, weight, NT))

    for group in range(groups):
        here = pl.ds(group * rows, rows)
        grad = wide_sum[here, :] * gain_ref[...]
        scale = stats_ref[here, 1:2]
        hat = (load_rows(both_ref, 0, group).astype(jnp.float32) - stats_ref[here, 0:1]) * scale
        grad_rows = scale * (
            grad
            - jnp.mean(grad, axis=-1, keepdims=True)
            - hat * jnp.mean(grad * hat, axis=-1, keepdims=True)
        )
        cot = load_rows(both_ref, 1, group).astype(jnp.float32)
        store(1, group, (cot + grad_rows).astype(jnp.bfloat16))


def run_front(gain, shape, sources, view):
    frames, _, patches, width = shape
    total = frames * patches
    vmem = pl.BlockSpec(memory_space=pltpu.VMEM)
    return pl.pallas_call(
        functools.partial(front_kernel, view),
        out_shape=(
            jax.ShapeDtypeStruct(shape, jnp.bfloat16),
            jax.ShapeDtypeStruct((total, width), jnp.bfloat16),
            jax.ShapeDtypeStruct((total, 128), jnp.float32),
            jax.ShapeDtypeStruct((total, view.early * view.in_columns), jnp.bfloat16),
        ),
        in_specs=[vmem] * (1 + len(sources)),
        out_specs=(vmem,) * 4,
        scratch_shapes=[pltpu.VMEM((total, width), jnp.bfloat16)],
        compiler_params=pltpu.CompilerParams(vmem_limit_bytes=VMEM_LIMIT),
        cost_estimate=pl.CostEstimate(flops=total, bytes_accessed=total, transcendentals=0),
        name="front",
    )(gain, *sources)


def run_middle(counts, fronted, weights, view):
    both, normed, _, _ = fronted
    total, width = normed.shape
    vmem = pl.BlockSpec(memory_space=pltpu.VMEM)
    columns = (view.blocks - view.early) * view.in_columns
    return pl.pallas_call(
        functools.partial(middle_kernel, view),
        out_shape=(
            jax.ShapeDtypeStruct((total, width), jnp.bfloat16),
            jax.ShapeDtypeStruct((total, width), jnp.bfloat16),
            jax.ShapeDtypeStruct((total, columns), jnp.float32),
        ),
        in_specs=[pl.BlockSpec(memory_space=pltpu.SMEM)] + [vmem] * (2 + len(weights)),
        out_specs=(vmem,) * 3,
        scratch_shapes=[pltpu.VMEM((total, width), jnp.bfloat16)],
        compiler_params=pltpu.CompilerParams(vmem_limit_bytes=VMEM_LIMIT),
        cost_estimate=pl.CostEstimate(flops=total, bytes_accessed=total, transcendentals=0),
        name="middle",
    )(counts, both, normed, *weights)


def run_main(counts, gain, fronted, weights, view):
    both, normed, stats, front = fronted
    frames, _, patches, width = both.shape
    total, rows = frames * patches, frames * SUB
    vmem = pl.BlockSpec(memory_space=pltpu.VMEM)
    smem = pl.BlockSpec(memory_space=pltpu.SMEM)
    chunk = 8 if rows <= 128 else 1
    return pl.pallas_call(
        functools.partial(main_kernel, view),
        out_shape=jax.ShapeDtypeStruct(both.shape, jnp.bfloat16),
        in_specs=[smem] + [vmem] * (5 + len(weights)),
        out_specs=vmem,
        scratch_shapes=[
            pltpu.VMEM((total, 3 * width), jnp.bfloat16),
            pltpu.VMEM((total, width), jnp.bfloat16),
            pltpu.VMEM((total, width), jnp.bfloat16),
            pltpu.VMEM((total, 3 * width), jnp.bfloat16),
            pltpu.VMEM((total, width), jnp.float32),
            pltpu.VMEM((rows, 2 * rows), jnp.float32),
            pltpu.VMEM((chunk, rows, 2 * rows), jnp.float32),
            pltpu.VMEM((chunk, rows, 2 * rows), jnp.float32),
            pltpu.VMEM((chunk, 2, rows, 2 * rows), jnp.bfloat16),
        ],
        compiler_params=pltpu.CompilerParams(
            vmem_limit_bytes=VMEM_LIMIT if rows <= 128 else 2 * VMEM_LIMIT
        ),
        cost_estimate=pl.CostEstimate(
            flops=12 * total * width * width,
            bytes_accessed=8 * width * width + 8 * total * width,
            transcendentals=total * 2048,
        ),
        name="main",
    )(counts, gain, both, normed, stats, front, *weights)


class View:
    def __init__(self, blocks, early, rows, early_rows, in_columns, out_columns, piece, tokens, device, row_order, block_order):
        self.blocks, self.early = blocks, early
        self.rows, self.early_rows = rows, early_rows
        self.in_columns, self.out_columns = in_columns, out_columns
        self.piece, self.tokens, self.device = piece, tokens, device
        self.row_order, self.block_order = row_order, block_order


def swap(array, distance, devices):
    return lax.ppermute(array, "frame", [(f, f ^ distance) for f in range(devices)])


def join_kernel(axis, *refs):
    *sources, target = refs
    start = 0
    for source in sources:
        end = start + source.shape[axis]
        if axis == 0:
            target[start:end, :] = source[...]
        else:
            target[:, start:end] = source[...]
        start = end


def join(axis, *arrays):
    shape = list(arrays[0].shape)
    shape[axis] = sum(array.shape[axis] for array in arrays)
    vmem = pl.BlockSpec(memory_space=pltpu.VMEM)
    return pl.pallas_call(
        functools.partial(join_kernel, axis),
        out_shape=jax.ShapeDtypeStruct(shape, arrays[0].dtype),
        in_specs=[vmem] * len(arrays),
        out_specs=vmem,
        compiler_params=SMALL,
        name="join",
    )(*arrays)


def pack_kernel(patches, share, *refs):
    sources, (joined, own, mine, to_x, to_y), held, fetched, sems = (
        refs[:4], refs[4:9], refs[9], refs[10:14], refs[14]
    )
    copies = [
        pltpu.make_async_copy(source, target, sems.at[i])
        for i, (source, target) in enumerate(zip(sources, fetched))
    ]
    for copy in copies:
        copy.start()
    w_in, w_out, tokens, cot = fetched
    depth = w_in.shape[0]
    half, block = depth // 2, 2 * share
    device = lax.axis_index("frame")
    chip, core = device // 2, device % 2
    full = patches // SUB * SUB
    held[:, full:] = jnp.zeros((2, held.shape[1] - full, held.shape[2]), held.dtype)
    wait(copies)
    joined[:, : w_in.shape[1]] = w_in[...]
    joined[:, w_in.shape[1] :] = w_out[...]
    held[0, :patches] = tokens[0, 0]
    held[1, :patches] = cot[0, 0]

    def put(target, row, owner):
        rows = pl.ds(pl.multiple_of(owner * share, share), share)
        target[row : row + share, :] = held[0, rows, :]
        target[row + share : row + block, :] = held[1, rows, :]

    put(mine, 0, device)
    own[:depth, :] = joined[...]
    put(own, depth, device ^ 1)
    for target, first, last, away, core_by in ((to_x, 0, half, 1, 0), (to_y, half, 0, 2, 1)):
        target[:half, :] = joined[first : first + half, :]
        put(target, half, (chip ^ away) * 2)
        put(target, half + block, (chip ^ away) * 2 + 1)
        target[half + 2 * block : depth + 2 * block, :] = joined[last : last + half, :]
        put(target, depth + 2 * block, (chip ^ 3) * 2 + core_by)


def trim_kernel(half, block, x_ref, y_ref, dx_ref, dy_ref, x_out, y_out, d_out):
    other = 1 - lax.axis_index("frame") % 2
    tail = half + 2 * block
    for source, target in ((x_ref, x_out), (y_ref, y_out)):
        rows = pl.ds(pl.multiple_of(half + other * block, SUB), block)
        target[:half, :] = source[:half, :]
        target[half : half + block, :] = source[rows, :]
        target[half + block :, :] = source[tail : tail + half, :]
    d_out[:half, :] = dx_ref[:half, :]
    d_out[half : 2 * half, :] = dy_ref[:half, :]
    d_out[2 * half :, :] = jnp.where(
        other == 0, dy_ref[half : half + block, :], dx_ref[half : half + block, :]
    )


def turn_kernel(half, by_x, by_y, pair_x, pair_y, to_dx, to_dy):
    to_dx[:half, :] = by_y[:half, :]
    to_dx[half:, :] = pair_y[: 2 * half, :]
    to_dy[:half, :] = by_x[half:, :]
    to_dy[half:, :] = pair_x[2 * half :, :]


def gather_in_rounds(
    counts, input_weights, output_weights, tokens, cotangent, gain, share, devices
):
    depth, in_columns = input_weights.shape
    out_columns = output_weights.shape[1]
    _, _, patches, width = tokens.shape
    half, block = depth // 2, 2 * share
    vmem = pl.BlockSpec(memory_space=pltpu.VMEM)

    def rows_of(count):
        return jax.ShapeDtypeStruct((count, width), jnp.bfloat16)

    joined, own, mine, to_x, to_y = pl.pallas_call(
        functools.partial(pack_kernel, patches, share),
        out_shape=tuple(
            map(rows_of, (depth, depth + block, block, depth + 3 * block, depth + 3 * block))
        ),
        in_specs=[pl.BlockSpec(memory_space=pltpu.HBM)] * 4,
        out_specs=(vmem,) * 5,
        scratch_shapes=[pltpu.VMEM((2, devices * share, width), jnp.bfloat16)]
        + [pltpu.VMEM(a.shape, a.dtype) for a in (input_weights, output_weights, tokens, cotangent)]
        + [pltpu.SemaphoreType.DMA((4,))],
        compiler_params=pltpu.CompilerParams(vmem_limit_bytes=PACK_LIMIT),
        name="pack",
    )(input_weights, output_weights, tokens, cotangent)

    def by_clip(array, offset):
        return lax.ppermute(array, "clip", [(c, c ^ offset) for c in range(4)])

    def across(array):
        return [swap(array, 2, devices), swap(array, 4, devices)]

    def other_core(arrays):
        return [swap(array, 1, devices) for array in arrays]

    one, two, three = by_clip(joined, 1), by_clip(joined, 2), by_clip(joined, 3)
    first = [swap(to_x, 2, devices), swap(to_y, 4, devices)]
    tail = half + 2 * block
    first += [swap(first[1][tail:], 2, devices), swap(first[0][tail:], 4, devices)]
    one, first[0], first[1] = lax.optimization_barrier((one, first[0], first[1]))
    second = [one, *across(one)]
    two, three, first[2], first[3] = lax.optimization_barrier((two, three, first[2], first[3]))
    third = [join(0, two, three)]
    second[1], second[2], own, *first = lax.optimization_barrier(
        (second[1], second[2], own, *first)
    )
    first_other = other_core(
        [
            own,
            *pl.pallas_call(
                functools.partial(trim_kernel, half, block),
                out_shape=(rows_of(depth + block),) * 3,
                in_specs=[vmem] * 4,
                out_specs=(vmem,) * 3,
                compiler_params=SMALL,
                name="trim",
            )(*first),
        ]
    )
    second_other = other_core(second)
    ready = [joined, *first, *first_other, *second, *second_other]
    third += across(third[0])

    def tokens_in(sources, both_ref):
        core = lax.axis_index("frame") % 2
        mine_ref, _, x_ref, y_ref, dx_ref, dy_ref, own2, x2, y2, d2 = sources[:10]
        rows = pl.ds(pl.multiple_of(half + core * block, SUB), block)
        behind = slice(half, half + block)
        found = (
            mine_ref[...], own2[depth : depth + block, :],
            x_ref[rows, :], x2[behind, :], y_ref[rows, :], y2[behind, :],
            jnp.where(core == 0, dy_ref[behind, :], dx_ref[behind, :]),
            d2[depth : depth + block, :],
        )
        for distance, value in enumerate(found):
            both_ref[distance] = value.reshape(2, share, width)

    table = [
        [(0, 0, 0, depth, 0)],
        [(0, 2, 0, half, 0), (0, 2, tail, half, half)],
        [(0, 4, 0, half, half), (0, 4, tail, half, 0)],
        [(0, 6, 0, half, 0)],
        [(0, 6, 0, half, half)],
    ]
    trimmed = [
        [(0, 0, 0, depth, 0)],
        [(0, 2, 0, half, 0), (0, 2, half + block, half, half)],
        [(0, 4, 0, half, half), (0, 4, half + block, half, 0)],
        [(0, 6, 0, depth, 0)],
    ]
    others = [[(1, d, 0, depth, 0)] for d in (0, 2, 4)]
    pairs = [[(2, d, 0, depth, 0), (3, d, depth, depth, 0)] for d in (0, 2, 4)]
    long = half + depth
    pairs += [
        [
            (1, 6, 0, half, 0), (2, 6, half, depth, 0),
            (1, 6, long, half, half), (3, 6, long + half, depth, 0),
        ],
    ]
    arrays = [(core, parts) for core, group in enumerate((table, trimmed)) for parts in group]
    for group in (others, pairs):
        arrays += [(core, parts) for core in (0, 1) for parts in group]

    def piece(present):
        def value(refs, offset, distance, first, depth, lanes):
            found = [
                (inside, refs[present.index(ref)][start : start + size, lanes[0] : lanes[0] + lanes[1]])
                for ref, (core, parts) in enumerate(arrays)
                for source, away, start, size, inside in parts
                if (source, away ^ core) == (offset, distance)
            ]
            return jnp.concatenate([held for _, held in sorted(found, key=lambda f: f[0])], axis=0)

        return value

    row_groups = [[(d, 0, depth), (d + 1, 0, depth)] for d in range(0, devices, 2)]

    def view(present):
        return View(
            4,
            1,
            row_groups,
            row_groups[:3],
            in_columns,
            out_columns,
            piece(present),
            tokens_in,
            lambda: lax.axis_index("frame"),
            lambda: ([(lax.axis_index("frame") ^ d) * depth for d in range(devices)], depth),
            lambda: [lax.axis_index("clip") ^ offset for offset in range(4)],
        )

    fronted = run_front(
        gain, (devices, 2, share, width), [mine, *ready[:9]], view([None, *range(9)])
    )
    to_dx, to_dy = pl.pallas_call(
        functools.partial(turn_kernel, half),
        out_shape=(rows_of(depth + half), rows_of(depth + half)),
        in_specs=[vmem] * 4,
        out_specs=(vmem, vmem),
        compiler_params=SMALL,
        name="turn",
    )(second[1], second[2], third[1], third[2])
    last = [swap(to_dx, 2, devices), swap(to_dy, 4, devices)]
    last[0], *fronted = lax.optimization_barrier((last[0], *fronted))
    third_other = other_core(third)
    last[0], third_other[1], third_other[2] = lax.optimization_barrier(
        (last[0], third_other[1], third_other[2])
    )
    middle = run_middle(
        counts, fronted, [*ready, *third, *third_other], view([*range(15), 15, 16, 17, 19, 20, 21])
    )
    last = join(0, *last)
    weights = [*middle, *ready, *third, last, *third_other, swap(last, 1, devices)]
    return fronted, weights, view(list(range(23)))


def gather_plainly(
    counts, input_weights, output_weights, tokens, cotangent, gain, share, devices
):
    _, slots, patches, width = tokens.shape
    whole = []
    for weights in (input_weights, output_weights):
        columns = lax.all_gather(weights, "clip", axis=1, tiled=True)
        whole.append(lax.all_gather(columns, "frame", axis=0, tiled=True))

    def by_destination(source):
        padded = jnp.pad(source[0], ((0, 0), (0, devices * share - patches), (0, 0)))
        return padded.reshape(slots, devices, share, width).transpose(1, 0, 2, 3)

    both = jnp.stack([by_destination(tokens), by_destination(cotangent)], axis=2)
    both = lax.all_to_all(both, "frame", split_axis=0, concat_axis=0, tiled=True)
    both = both.reshape(devices * slots, 2, share, width)

    def tokens_in(sources, both_ref):
        both_ref[...] = sources[2][...]

    in_columns, out_columns = whole[0].shape[1], whole[1].shape[1]

    def piece(refs, block, index, first, depth, lanes):
        outer = lanes[0] >= in_columns
        start = lanes[0] - in_columns * outer
        return refs[int(outer)][first : first + depth, start : start + lanes[1]]

    step = math.gcd(width, 256)
    view = View(
        1,
        1,
        [[(0, first, step)] for first in range(0, width, step)],
        [],
        in_columns,
        out_columns,
        piece,
        tokens_in,
        lambda: 0,
        lambda: ([0], width),
        lambda: [0],
    )
    return run_front(gain, both.shape, [*whole, both], view), whole, view


def per_device(clips, devices, tokens, counts, norm_gain, input_weights, output_weights, cotangent):
    _, slots, patches, width = tokens.shape
    share = -(-patches // devices)
    share = -(-share // SUB) * SUB
    depth, in_columns = input_weights.shape
    fits = in_columns % 128 == 0 and output_weights.shape[1] % 128 == 0 and depth % 32 == 0
    small = clips == 4 and devices == 8 and slots == 1 and fits
    gather = gather_in_rounds if small else gather_plainly
    gain = norm_gain.reshape(1, width)
    fronted, weights, view = gather(
        counts, input_weights, output_weights, tokens, cotangent, gain, share, devices
    )
    back = run_main(counts, gain, fronted, weights, view)
    back = back.reshape(devices, slots, 2, share, width)
    back = lax.all_to_all(back, "frame", split_axis=0, concat_axis=0, tiled=True)

    def in_order(which):
        rows = back[:, :, which].transpose(1, 0, 2, 3).reshape(slots, devices * share, width)
        return rows[None, :, :patches]

    return in_order(0), in_order(1)


def solution(mesh):
    in_specs = (
        P("clip", "frame", None, None),
        P("clip"),
        P(),
        P("frame", "clip"),
        P("frame", "clip"),
        P("clip", "frame", None, None),
    )
    out_specs = (P("clip", "frame", None, None), P("clip", "frame", None, None))
    body = functools.partial(per_device, mesh.shape["clip"], mesh.shape["frame"])
    return jax.shard_map(body, mesh=mesh, in_specs=in_specs, out_specs=out_specs, check_vma=False)
```

```python
import functools
import math

import jax
import jax.numpy as jnp
from jax import lax
from jax.experimental import pallas as pl
from jax.experimental.pallas import tpu as pltpu
from jax.sharding import PartitionSpec as P

DH = 64
PAIR = 2 * DH
SUB = 16
EPSILON = 1e-06
NEGATIVE = -1e30
NN = (((1,), (0,)), ((), ()))
NT = (((1,), (1,)), ((), ()))
TN = (((0,), (0,)), ((), ()))
VMEM_LIMIT = 27 * 1024 * 1024
PACK_LIMIT = 58 * 1024 * 1024
SMALL = pltpu.CompilerParams(vmem_limit_bytes=6 * 1024 * 1024)


def dot(a, b, dims):
    return lax.dot_general(a, b, dims, preferred_element_type=jnp.float32)


def wait(copies):
    for copy in copies:
        copy.wait()


def load_rows(ref, which, group):
    frames, _, _, width = ref.shape
    return ref[:, which, group * SUB : (group + 1) * SUB, :].reshape(frames * SUB, width)


def beside(ref, starts, size):
    return jnp.concatenate(
        [ref[:, pl.ds(pl.multiple_of(start, 128), size)] for start in starts], axis=1
    )


def chunks(columns):
    step = math.gcd(columns, 256)
    return [(start, step) for start in range(0, columns, step)]


def stack_rows(view, refs, block, lanes, groups=None):
    groups = view.rows if groups is None else groups
    return jnp.concatenate(
        [view.piece(refs, block, *part, lanes) for parts in groups for part in parts], axis=0
    )


def stack_columns(view, refs, parts, start, size):
    return jnp.concatenate(
        [
            jnp.concatenate(
                [view.piece(refs, block, *part, (start, size)) for part in parts], axis=0
            )
            for block in range(view.blocks)
        ],
        axis=1,
    )


def front_kernel(view, gain_ref, *refs):
    sources = refs[:-5]
    both_ref, normed_ref, stats_ref, proj_ref, natural = refs[-5:]
    view.tokens(sources, both_ref)
    frames, _, patches, _ = both_ref.shape
    rows = frames * SUB
    for group in range(patches // SUB):
        here = pl.ds(group * rows, rows)
        wide = load_rows(both_ref, 0, group).astype(jnp.float32)
        average = jnp.mean(wide, axis=-1, keepdims=True)
        centred = wide - average
        variance = jnp.mean(centred * centred, axis=-1, keepdims=True)
        scale = lax.rsqrt(variance + EPSILON)
        natural[here, :] = (centred * scale * gain_ref[...]).astype(jnp.bfloat16)
        stats_ref[here, 0:1] = average
        stats_ref[here, 1:2] = scale
    normed_ref[...] = beside(natural, *view.row_order())
    for block in range(view.early):
        for start, size in chunks(view.in_columns):
            weight = stack_rows(view, sources, block, (start, size))
            here = pl.ds(block * view.in_columns + start, size)
            proj_ref[:, here] = dot(normed_ref[...], weight, NN).astype(jnp.bfloat16)


def put_rows(view, target, parts, value):
    row_starts, _ = view.row_order()
    done = 0
    for index, first, depth in parts:
        start = pl.multiple_of(row_starts[index] + first, 128)
        target[:, pl.ds(start, depth)] = value[:, done : done + depth]
        done += depth


def live_rows(view, counts_ref, rows):
    frame = (lax.broadcasted_iota(jnp.int32, (rows, 1), 0) // SUB) ^ view.device()
    return (frame < counts_ref[0]).astype(jnp.float32)


def masked_cotangent(view, counts_ref, both_ref, natural):
    frames, _, patches, _ = both_ref.shape
    rows = frames * SUB
    live = live_rows(view, counts_ref, rows)
    for group in range(patches // SUB):
        wide = load_rows(both_ref, 1, group).astype(jnp.float32)
        natural[pl.ds(group * rows, rows), :] = (wide * live).astype(jnp.bfloat16)
    starts = [block * view.out_columns for block in view.block_order()]
    return beside(natural, starts, view.out_columns)


def grad_attended(view, weights, ordered, groups, target):
    for parts in groups:
        weight = stack_columns(view, weights, parts, view.in_columns, view.out_columns)
        put_rows(view, target, parts, dot(ordered, weight, NT).astype(jnp.bfloat16))


def early_depth(view):
    return sum(part[2] for parts in view.early_rows for part in parts)


def middle_kernel(view, counts_ref, both_ref, normed_ref, *rest):
    weights = rest[:-4]
    ordered_ref, ga_ref, partial_ref, natural = rest[-4:]
    ordered_ref[...] = masked_cotangent(view, counts_ref, both_ref, natural)
    grad_attended(view, weights, ordered_ref[...], view.early_rows, ga_ref)
    depth = early_depth(view)
    for block in range(view.early, view.blocks):
        for start, size in chunks(view.in_columns):
            weight = stack_rows(view, weights, block, (start, size), view.early_rows)
            here = pl.ds((block - view.early) * view.in_columns + start, size)
            partial_ref[:, here] = dot(normed_ref[:, :depth], weight, NN)


def main_kernel(view, counts_ref, gain_ref, both_ref, normed_ref, stats_ref, front_ref, *rest):
    weights = rest[:-10]
    out_ref, proj, ga, att, gproj, wide_sum, bias, scores, gprobs, low = rest[-10:]
    middle = weights[:3] if view.early_rows else None
    weights = weights[3:] if view.early_rows else weights
    frames, _, patches, width = both_ref.shape
    groups = patches // SUB
    rows = frames * SUB
    count = counts_ref[0]
    device = view.device()
    in_columns, out_columns = view.in_columns, view.out_columns
    row_starts, row_size = view.row_order()
    block_order = view.block_order()

    def column(block, stride, start=0):
        return pl.multiple_of(block_order[block] * stride + start, 128)

    def real(index):
        return ((index // SUB) ^ device) < count

    live = live_rows(view, counts_ref, rows)
    key = lax.broadcasted_iota(jnp.int32, (rows, 2 * rows), 0)
    query = lax.broadcasted_iota(jnp.int32, (rows, 2 * rows), 1)
    bias[...] = jnp.where((query % SUB == key % SUB) & real(key), 0.0, NEGATIVE)
    lane = lax.broadcasted_iota(jnp.int32, (1, PAIR), 1)
    low_lanes = (lane < DH).astype(jnp.bfloat16)
    high_lanes = (lane >= DH).astype(jnp.bfloat16)

    depth = early_depth(view)
    late_rows = view.rows[len(view.early_rows) :]
    if middle:
        ordered, ga_early, partial = middle
        ga[...] = ga_early[...]
        grad_attended(view, weights, ordered[...], late_rows, ga)
    else:
        ordered = masked_cotangent(view, counts_ref, both_ref, att)
        grad_attended(view, weights, ordered, late_rows, ga)

    for block in range(view.early):
        held = front_ref[:, block * in_columns : (block + 1) * in_columns]
        proj[:, pl.ds(column(block, in_columns), in_columns)] = held
    for block in range(view.early, view.blocks):
        for start, size in chunks(in_columns):
            weight = stack_rows(view, weights, block, (start, size), late_rows)
            value = dot(normed_ref[:, depth:], weight, NN)
            if middle:
                here = pl.ds((block - view.early) * in_columns + start, size)
                value = value + partial[:, here]
            proj[:, pl.ds(column(block, in_columns, start), size)] = value.astype(jnp.bfloat16)

    def apart(block):
        return jnp.concatenate([block * low_lanes, block * high_lanes], axis=0)

    def stacked(block):
        return jnp.concatenate([block[:, :rows], block[:, rows:]], axis=0)

    def lanes(part, pair):
        return pl.ds(pl.multiple_of(part * width + pair * PAIR, PAIR), PAIR)

    chunk = scores.shape[0]
    unroll = min(chunk, 4)

    def each(body):
        @pl.loop(0, chunk // unroll)
        def _(i):
            for inner in range(unroll):
                body(i * unroll + inner)

    for group in range(groups):
        here = pl.ds(group * rows, rows)

        @pl.loop(0, width // (PAIR * chunk))
        def _(part):
            def products(item):
                pair = part * chunk + item
                q_two = apart(proj[here, lanes(0, pair)] * DH ** (-0.5))
                scores[item] = dot(proj[here, lanes(1, pair)], q_two, NT)
                ga_two = apart(ga[here, lanes(0, pair)])
                gprobs[item] = dot(proj[here, lanes(2, pair)], ga_two, NT)

            def softmax(item):
                masked = scores[item] + bias[...]
                expanded = jnp.exp(masked - jnp.max(masked, axis=0, keepdims=True))
                probs = expanded * (1.0 / jnp.sum(expanded, axis=0, keepdims=True))
                low[item, 0] = probs.astype(jnp.bfloat16)
                weighted = probs * gprobs[item]
                delta = jnp.sum(weighted, axis=0, keepdims=True)
                low[item, 1] = (weighted - probs * delta).astype(jnp.bfloat16)

            def results(item):
                pair = part * chunk + item
                probs_low, grad_scores = low[item, 0], low[item, 1]
                q_two = apart(proj[here, lanes(0, pair)] * DH ** (-0.5))
                k_two = apart(proj[here, lanes(1, pair)])
                v_two = apart(proj[here, lanes(2, pair)])
                ga_two = apart(ga[here, lanes(0, pair)])
                att[here, lanes(0, pair)] = dot(stacked(probs_low), v_two, TN).astype(jnp.bfloat16)
                gproj[here, lanes(0, pair)] = (
                    dot(stacked(grad_scores), k_two, TN) * DH ** (-0.5)
                ).astype(jnp.bfloat16)
                gproj[here, lanes(1, pair)] = dot(grad_scores, q_two, NN).astype(jnp.bfloat16)
                gproj[here, lanes(2, pair)] = dot(probs_low, ga_two, NN).astype(jnp.bfloat16)

            each(products)
            each(softmax)
            each(results)

    def store(which, group, value):
        for frame in range(frames):
            out_ref[pl.ds(frame ^ device, 1), which, group * SUB : (group + 1) * SUB, :] = value[
                frame * SUB : (frame + 1) * SUB
            ].reshape(1, SUB, width)

    att_ordered = beside(att, row_starts, row_size)
    for block in range(view.blocks):
        for start, size in chunks(out_columns):
            weight = stack_rows(view, weights, block, (in_columns + start, size))
            wide_sum[:, pl.ds(column(block, out_columns, start), size)] = dot(
                att_ordered, weight, NN
            )

    for group in range(groups):
        here = pl.ds(group * rows, rows)
        wide = load_rows(both_ref, 0, group).astype(jnp.float32)
        store(0, group, (wide + live * wide_sum[here, :]).astype(jnp.bfloat16))

    gproj_ordered = beside(gproj, [column(i, in_columns) for i in range(view.blocks)], in_columns)
    for parts in view.rows:
        weight = stack_columns(view, weights, parts, 0, in_columns)
        put_rows(view, wide_sum, parts, dot(gproj_ordered, weight, NT))

    for group in range(groups):
        here = pl.ds(group * rows, rows)
        grad = wide_sum[here, :] * gain_ref[...]
        scale = stats_ref[here, 1:2]
        hat = (load_rows(both_ref, 0, group).astype(jnp.float32) - stats_ref[here, 0:1]) * scale
        grad_rows = scale * (
            grad
            - jnp.mean(grad, axis=-1, keepdims=True)
            - hat * jnp.mean(grad * hat, axis=-1, keepdims=True)
        )
        cot = load_rows(both_ref, 1, group).astype(jnp.float32)
        store(1, group, (cot + grad_rows).astype(jnp.bfloat16))


def run_front(gain, shape, sources, view):
    frames, _, patches, width = shape
    total = frames * patches
    vmem = pl.BlockSpec(memory_space=pltpu.VMEM)
    return pl.pallas_call(
        functools.partial(front_kernel, view),
        out_shape=(
            jax.ShapeDtypeStruct(shape, jnp.bfloat16),
            jax.ShapeDtypeStruct((total, width), jnp.bfloat16),
            jax.ShapeDtypeStruct((total, 128), jnp.float32),
            jax.ShapeDtypeStruct((total, view.early * view.in_columns), jnp.bfloat16),
        ),
        in_specs=[vmem] * (1 + len(sources)),
        out_specs=(vmem,) * 4,
        scratch_shapes=[pltpu.VMEM((total, width), jnp.bfloat16)],
        compiler_params=pltpu.CompilerParams(vmem_limit_bytes=VMEM_LIMIT),
        cost_estimate=pl.CostEstimate(flops=total, bytes_accessed=total, transcendentals=0),
        name="front",
    )(gain, *sources)


def run_middle(counts, fronted, weights, view):
    both, normed, _, _ = fronted
    total, width = normed.shape
    vmem = pl.BlockSpec(memory_space=pltpu.VMEM)
    columns = (view.blocks - view.early) * view.in_columns
    return pl.pallas_call(
        functools.partial(middle_kernel, view),
        out_shape=(
            jax.ShapeDtypeStruct((total, width), jnp.bfloat16),
            jax.ShapeDtypeStruct((total, width), jnp.bfloat16),
            jax.ShapeDtypeStruct((total, columns), jnp.float32),
        ),
        in_specs=[pl.BlockSpec(memory_space=pltpu.SMEM)] + [vmem] * (2 + len(weights)),
        out_specs=(vmem,) * 3,
        scratch_shapes=[pltpu.VMEM((total, width), jnp.bfloat16)],
        compiler_params=pltpu.CompilerParams(vmem_limit_bytes=VMEM_LIMIT),
        cost_estimate=pl.CostEstimate(flops=total, bytes_accessed=total, transcendentals=0),
        name="middle",
    )(counts, both, normed, *weights)


def run_main(counts, gain, fronted, weights, view):
    both, normed, stats, front = fronted
    frames, _, patches, width = both.shape
    total, rows = frames * patches, frames * SUB
    vmem = pl.BlockSpec(memory_space=pltpu.VMEM)
    smem = pl.BlockSpec(memory_space=pltpu.SMEM)
    chunk = 8 if rows <= 128 else 1
    return pl.pallas_call(
        functools.partial(main_kernel, view),
        out_shape=jax.ShapeDtypeStruct(both.shape, jnp.bfloat16),
        in_specs=[smem] + [vmem] * (5 + len(weights)),
        out_specs=vmem,
        scratch_shapes=[
            pltpu.VMEM((total, 3 * width), jnp.bfloat16),
            pltpu.VMEM((total, width), jnp.bfloat16),
            pltpu.VMEM((total, width), jnp.bfloat16),
            pltpu.VMEM((total, 3 * width), jnp.bfloat16),
            pltpu.VMEM((total, width), jnp.float32),
            pltpu.VMEM((rows, 2 * rows), jnp.float32),
            pltpu.VMEM((chunk, rows, 2 * rows), jnp.float32),
            pltpu.VMEM((chunk, rows, 2 * rows), jnp.float32),
            pltpu.VMEM((chunk, 2, rows, 2 * rows), jnp.bfloat16),
        ],
        compiler_params=pltpu.CompilerParams(
            vmem_limit_bytes=VMEM_LIMIT if rows <= 128 else 2 * VMEM_LIMIT
        ),
        cost_estimate=pl.CostEstimate(
            flops=12 * total * width * width,
            bytes_accessed=8 * width * width + 8 * total * width,
            transcendentals=total * 2048,
        ),
        name="main",
    )(counts, gain, both, normed, stats, front, *weights)


class View:
    def __init__(self, blocks, early, rows, early_rows, in_columns, out_columns, piece, tokens, device, row_order, block_order):
        self.blocks, self.early = blocks, early
        self.rows, self.early_rows = rows, early_rows
        self.in_columns, self.out_columns = in_columns, out_columns
        self.piece, self.tokens, self.device = piece, tokens, device
        self.row_order, self.block_order = row_order, block_order


def swap(array, distance, devices):
    return lax.ppermute(array, "frame", [(f, f ^ distance) for f in range(devices)])


def join_kernel(axis, *refs):
    *sources, target = refs
    start = 0
    for source in sources:
        end = start + source.shape[axis]
        if axis == 0:
            target[start:end, :] = source[...]
        else:
            target[:, start:end] = source[...]
        start = end


def join(axis, *arrays):
    shape = list(arrays[0].shape)
    shape[axis] = sum(array.shape[axis] for array in arrays)
    vmem = pl.BlockSpec(memory_space=pltpu.VMEM)
    return pl.pallas_call(
        functools.partial(join_kernel, axis),
        out_shape=jax.ShapeDtypeStruct(shape, arrays[0].dtype),
        in_specs=[vmem] * len(arrays),
        out_specs=vmem,
        compiler_params=SMALL,
        name="join",
    )(*arrays)


def pack_kernel(patches, share, *refs):
    sources, (joined, own, mine, to_x, to_y), held, fetched, sems = (
        refs[:4], refs[4:9], refs[9], refs[10:14], refs[14]
    )
    copies = [
        pltpu.make_async_copy(source, target, sems.at[i])
        for i, (source, target) in enumerate(zip(sources, fetched))
    ]
    for copy in copies:
        copy.start()
    w_in, w_out, tokens, cot = fetched
    depth = w_in.shape[0]
    half, block = depth // 2, 2 * share
    device = lax.axis_index("frame")
    chip, core = device // 2, device % 2
    full = patches // SUB * SUB
    held[:, full:] = jnp.zeros((2, held.shape[1] - full, held.shape[2]), held.dtype)
    wait(copies)
    joined[:, : w_in.shape[1]] = w_in[...]
    joined[:, w_in.shape[1] :] = w_out[...]
    held[0, :patches] = tokens[0, 0]
    held[1, :patches] = cot[0, 0]

    def put(target, row, owner):
        rows = pl.ds(pl.multiple_of(owner * share, share), share)
        target[row : row + share, :] = held[0, rows, :]
        target[row + share : row + block, :] = held[1, rows, :]

    put(mine, 0, device)
    own[:depth, :] = joined[...]
    put(own, depth, device ^ 1)
    for target, first, last, away, core_by in ((to_x, 0, half, 1, 0), (to_y, half, 0, 2, 1)):
        target[:half, :] = joined[first : first + half, :]
        put(target, half, (chip ^ away) * 2)
        put(target, half + block, (chip ^ away) * 2 + 1)
        target[half + 2 * block : depth + 2 * block, :] = joined[last : last + half, :]
        put(target, depth + 2 * block, (chip ^ 3) * 2 + core_by)


def turn_kernel(half, by_x, by_y, pair_x, pair_y, to_dx, to_dy):
    to_dx[:half, :] = by_y[:half, :]
    to_dx[half:, :] = pair_y[: 2 * half, :]
    to_dy[:half, :] = by_x[half:, :]
    to_dy[half:, :] = pair_x[2 * half :, :]


def gather_in_rounds(
    counts, input_weights, output_weights, tokens, cotangent, gain, share, devices
):
    depth, in_columns = input_weights.shape
    out_columns = output_weights.shape[1]
    _, _, patches, width = tokens.shape
    half, block = depth // 2, 2 * share
    vmem = pl.BlockSpec(memory_space=pltpu.VMEM)

    def rows_of(count):
        return jax.ShapeDtypeStruct((count, width), jnp.bfloat16)

    joined, own, mine, to_x, to_y = pl.pallas_call(
        functools.partial(pack_kernel, patches, share),
        out_shape=tuple(
            map(rows_of, (depth, depth + block, block, depth + 3 * block, depth + 3 * block))
        ),
        in_specs=[pl.BlockSpec(memory_space=pltpu.HBM)] * 4,
        out_specs=(vmem,) * 5,
        scratch_shapes=[pltpu.VMEM((2, devices * share, width), jnp.bfloat16)]
        + [pltpu.VMEM(a.shape, a.dtype) for a in (input_weights, output_weights, tokens, cotangent)]
        + [pltpu.SemaphoreType.DMA((4,))],
        compiler_params=pltpu.CompilerParams(vmem_limit_bytes=PACK_LIMIT),
        name="pack",
    )(input_weights, output_weights, tokens, cotangent)

    def by_clip(array, offset):
        return lax.ppermute(array, "clip", [(c, c ^ offset) for c in range(4)])

    def across(array):
        return [swap(array, 2, devices), swap(array, 4, devices)]

    def other_core(arrays):
        return [swap(array, 1, devices) for array in arrays]

    one, two, three = by_clip(joined, 1), by_clip(joined, 2), by_clip(joined, 3)
    first = [swap(to_x, 2, devices), swap(to_y, 4, devices)]
    tail = half + 2 * block
    first += [swap(first[1][tail:], 2, devices), swap(first[0][tail:], 4, devices)]
    one, first[0], first[1] = lax.optimization_barrier((one, first[0], first[1]))
    second = [one, *across(one)]
    two, three, first[2], first[3] = lax.optimization_barrier((two, three, first[2], first[3]))
    third = [join(0, two, three)]
    second[1], second[2], own, *first = lax.optimization_barrier(
        (second[1], second[2], own, *first)
    )
    first_other = other_core([own, *first])
    second_other = other_core(second)
    ready = [joined, *first, *first_other, *second, *second_other]
    third += across(third[0])

    def tokens_in(sources, both_ref):
        core = lax.axis_index("frame") % 2
        mine_ref, _, x_ref, y_ref, dx_ref, dy_ref, own2, x2, y2, dx2, dy2 = sources[:11]
        rows = pl.ds(pl.multiple_of(half + core * block, block), block)
        behind = slice(half, half + block)

        def diagonal(by_x, by_y):
            return jnp.where(core == 0, by_y[behind, :], by_x[behind, :])

        found = (
            mine_ref[...], own2[depth : depth + block, :],
            x_ref[rows, :], x2[rows, :], y_ref[rows, :], y2[rows, :],
            diagonal(dx_ref, dy_ref), diagonal(dx2, dy2),
        )
        for distance, value in enumerate(found):
            both_ref[distance] = value.reshape(2, share, width)

    table = [
        [(0, 0, 0, depth, 0)],
        [(0, 2, 0, half, 0), (0, 2, tail, half, half)],
        [(0, 4, 0, half, half), (0, 4, tail, half, 0)],
        [(0, 6, 0, half, 0)],
        [(0, 6, 0, half, half)],
    ]
    others = [[(1, d, 0, depth, 0)] for d in (0, 2, 4)]
    pairs = [[(2, d, 0, depth, 0), (3, d, depth, depth, 0)] for d in (0, 2, 4)]
    pairs += [
        [(1, 6, 0, half, 0), (2, 6, half, depth, 0)],
        [(1, 6, 0, half, half), (3, 6, half, depth, 0)],
    ]
    arrays = []
    for group in (table, others, pairs):
        arrays += [(core, parts) for core in (0, 1) for parts in group]

    def piece(present):
        def value(refs, offset, distance, first, depth, lanes):
            found = [
                (inside, refs[present.index(ref)][start : start + size, lanes[0] : lanes[0] + lanes[1]])
                for ref, (core, parts) in enumerate(arrays)
                for source, away, start, size, inside in parts
                if (source, away ^ core) == (offset, distance)
            ]
            return jnp.concatenate([held for _, held in sorted(found, key=lambda f: f[0])], axis=0)

        return value

    row_groups = [[(d, 0, depth), (d + 1, 0, depth)] for d in range(0, devices, 2)]

    def view(present):
        return View(
            4,
            1,
            row_groups,
            row_groups[:3],
            in_columns,
            out_columns,
            piece(present),
            tokens_in,
            lambda: lax.axis_index("frame"),
            lambda: ([(lax.axis_index("frame") ^ d) * depth for d in range(devices)], depth),
            lambda: [lax.axis_index("clip") ^ offset for offset in range(4)],
        )

    fronted = run_front(
        gain, (devices, 2, share, width), [mine, *ready[:10]], view([None, *range(10)])
    )
    to_dx, to_dy = pl.pallas_call(
        functools.partial(turn_kernel, half),
        out_shape=(rows_of(depth + half), rows_of(depth + half)),
        in_specs=[vmem] * 4,
        out_specs=(vmem, vmem),
        compiler_params=SMALL,
        name="turn",
    )(second[1], second[2], third[1], third[2])
    third += [swap(to_dx, 2, devices), swap(to_dy, 4, devices)]
    held, *fronted = lax.optimization_barrier((third[0], *fronted))
    third_other = other_core([held, *third[1:]])
    middle = run_middle(
        counts,
        fronted,
        [*ready, *third[:3], *third_other[:3]],
        view([*range(16), 16, 17, 18, 21, 22, 23]),
    )
    weights = [*middle, *ready, *third, *third_other]
    return fronted, weights, view(list(range(26)))


def gather_plainly(
    counts, input_weights, output_weights, tokens, cotangent, gain, share, devices
):
    _, slots, patches, width = tokens.shape
    whole = []
    for weights in (input_weights, output_weights):
        columns = lax.all_gather(weights, "clip", axis=1, tiled=True)
        whole.append(lax.all_gather(columns, "frame", axis=0, tiled=True))

    def by_destination(source):
        padded = jnp.pad(source[0], ((0, 0), (0, devices * share - patches), (0, 0)))
        return padded.reshape(slots, devices, share, width).transpose(1, 0, 2, 3)

    both = jnp.stack([by_destination(tokens), by_destination(cotangent)], axis=2)
    both = lax.all_to_all(both, "frame", split_axis=0, concat_axis=0, tiled=True)
    both = both.reshape(devices * slots, 2, share, width)

    def tokens_in(sources, both_ref):
        both_ref[...] = sources[2][...]

    in_columns, out_columns = whole[0].shape[1], whole[1].shape[1]

    def piece(refs, block, index, first, depth, lanes):
        outer = lanes[0] >= in_columns
        start = lanes[0] - in_columns * outer
        return refs[int(outer)][first : first + depth, start : start + lanes[1]]

    step = math.gcd(width, 256)
    view = View(
        1,
        1,
        [[(0, first, step)] for first in range(0, width, step)],
        [],
        in_columns,
        out_columns,
        piece,
        tokens_in,
        lambda: 0,
        lambda: ([0], width),
        lambda: [0],
    )
    return run_front(gain, both.shape, [*whole, both], view), whole, view


def per_device(clips, devices, tokens, counts, norm_gain, input_weights, output_weights, cotangent):
    _, slots, patches, width = tokens.shape
    share = -(-patches // devices)
    share = -(-share // SUB) * SUB
    depth, in_columns = input_weights.shape
    fits = in_columns % 128 == 0 and output_weights.shape[1] % 128 == 0 and depth % 32 == 0
    small = clips == 4 and devices == 8 and slots == 1 and fits
    gather = gather_in_rounds if small else gather_plainly
    gain = norm_gain.reshape(1, width)
    fronted, weights, view = gather(
        counts, input_weights, output_weights, tokens, cotangent, gain, share, devices
    )
    back = run_main(counts, gain, fronted, weights, view)
    back = back.reshape(devices, slots, 2, share, width)
    back = lax.all_to_all(back, "frame", split_axis=0, concat_axis=0, tiled=True)

    def in_order(which):
        rows = back[:, :, which].transpose(1, 0, 2, 3).reshape(slots, devices * share, width)
        return rows[None, :, :patches]

    return in_order(0), in_order(1)


def solution(mesh):
    in_specs = (
        P("clip", "frame", None, None),
        P("clip"),
        P(),
        P("frame", "clip"),
        P("frame", "clip"),
        P("clip", "frame", None, None),
    )
    out_specs = (P("clip", "frame", None, None), P("clip", "frame", None, None))
    body = functools.partial(per_device, mesh.shape["clip"], mesh.shape["frame"])
    return jax.shard_map(body, mesh=mesh, in_specs=in_specs, out_specs=out_specs, check_vma=False)
```

```python
import functools
import math

import jax
import jax.numpy as jnp
from jax import lax
from jax.experimental import pallas as pl
from jax.experimental.pallas import tpu as pltpu
from jax.sharding import PartitionSpec as P

DH = 64
PAIR = 2 * DH
SUB = 16
EPSILON = 1e-06
NEGATIVE = -1e30
NN = (((1,), (0,)), ((), ()))
NT = (((1,), (1,)), ((), ()))
TN = (((0,), (0,)), ((), ()))
VMEM_LIMIT = 27 * 1024 * 1024
PACK_LIMIT = 58 * 1024 * 1024
SMALL = pltpu.CompilerParams(vmem_limit_bytes=6 * 1024 * 1024)


def dot(a, b, dims):
    return lax.dot_general(a, b, dims, preferred_element_type=jnp.float32)


def wait(copies):
    for copy in copies:
        copy.wait()


def load_rows(ref, which, group):
    frames, _, _, width = ref.shape
    return ref[:, which, group * SUB : (group + 1) * SUB, :].reshape(frames * SUB, width)


def beside(ref, starts, size):
    return jnp.concatenate(
        [ref[:, pl.ds(pl.multiple_of(start, 128), size)] for start in starts], axis=1
    )


def chunks(columns):
    step = math.gcd(columns, 256)
    return [(start, step) for start in range(0, columns, step)]


def stack_rows(view, refs, block, lanes, groups=None):
    groups = view.rows if groups is None else groups
    return jnp.concatenate(
        [view.piece(refs, block, *part, lanes) for parts in groups for part in parts], axis=0
    )


def stack_columns(view, refs, parts, start, size):
    return jnp.concatenate(
        [
            jnp.concatenate(
                [view.piece(refs, block, *part, (start, size)) for part in parts], axis=0
            )
            for block in range(view.blocks)
        ],
        axis=1,
    )


def front_kernel(view, gain_ref, *refs):
    sources = refs[:-5]
    both_ref, normed_ref, stats_ref, proj_ref, natural = refs[-5:]
    view.tokens(sources, both_ref)
    frames, _, patches, _ = both_ref.shape
    rows = frames * SUB
    for group in range(patches // SUB):
        here = pl.ds(group * rows, rows)
        wide = load_rows(both_ref, 0, group).astype(jnp.float32)
        average = jnp.mean(wide, axis=-1, keepdims=True)
        centred = wide - average
        variance = jnp.mean(centred * centred, axis=-1, keepdims=True)
        scale = lax.rsqrt(variance + EPSILON)
        natural[here, :] = (centred * scale * gain_ref[...]).astype(jnp.bfloat16)
        stats_ref[here, 0:1] = average
        stats_ref[here, 1:2] = scale
    normed_ref[...] = beside(natural, *view.row_order())
    for block in range(view.early):
        for start, size in chunks(view.in_columns):
            weight = stack_rows(view, sources, block, (start, size))
            here = pl.ds(block * view.in_columns + start, size)
            proj_ref[:, here] = dot(normed_ref[...], weight, NN).astype(jnp.bfloat16)


def put_rows(view, target, parts, value):
    row_starts, _ = view.row_order()
    done = 0
    for index, first, depth in parts:
        start = pl.multiple_of(row_starts[index] + first, 128)
        target[:, pl.ds(start, depth)] = value[:, done : done + depth]
        done += depth


def live_rows(view, counts_ref, rows):
    frame = (lax.broadcasted_iota(jnp.int32, (rows, 1), 0) // SUB) ^ view.device()
    return (frame < counts_ref[0]).astype(jnp.float32)


def masked_cotangent(view, counts_ref, both_ref, natural):
    frames, _, patches, _ = both_ref.shape
    rows = frames * SUB
    live = live_rows(view, counts_ref, rows)
    for group in range(patches // SUB):
        wide = load_rows(both_ref, 1, group).astype(jnp.float32)
        natural[pl.ds(group * rows, rows), :] = (wide * live).astype(jnp.bfloat16)
    starts = [block * view.out_columns for block in view.block_order()]
    return beside(natural, starts, view.out_columns)


def grad_attended(view, weights, ordered, groups, target):
    for parts in groups:
        weight = stack_columns(view, weights, parts, view.in_columns, view.out_columns)
        put_rows(view, target, parts, dot(ordered, weight, NT).astype(jnp.bfloat16))


def early_depth(view):
    return sum(part[2] for parts in view.early_rows for part in parts)


def middle_kernel(view, counts_ref, both_ref, normed_ref, *rest):
    weights = rest[:-4]
    ordered_ref, ga_ref, partial_ref, natural = rest[-4:]
    ordered_ref[...] = masked_cotangent(view, counts_ref, both_ref, natural)
    grad_attended(view, weights, ordered_ref[...], view.early_rows, ga_ref)
    depth = early_depth(view)
    for block in range(view.early, view.blocks):
        for start, size in chunks(view.in_columns):
            weight = stack_rows(view, weights, block, (start, size), view.early_rows)
            here = pl.ds((block - view.early) * view.in_columns + start, size)
            partial_ref[:, here] = dot(normed_ref[:, :depth], weight, NN)


def main_kernel(view, counts_ref, gain_ref, both_ref, normed_ref, stats_ref, front_ref, *rest):
    weights = rest[:-10]
    out_ref, proj, ga, att, gproj, wide_sum, bias, scores, gprobs, low = rest[-10:]
    middle = weights[:3] if view.early_rows else None
    weights = weights[3:] if view.early_rows else weights
    frames, _, patches, width = both_ref.shape
    groups = patches // SUB
    rows = frames * SUB
    count = counts_ref[0]
    device = view.device()
    in_columns, out_columns = view.in_columns, view.out_columns
    row_starts, row_size = view.row_order()
    block_order = view.block_order()

    def column(block, stride, start=0):
        return pl.multiple_of(block_order[block] * stride + start, 128)

    def real(index):
        return ((index // SUB) ^ device) < count

    live = live_rows(view, counts_ref, rows)
    key = lax.broadcasted_iota(jnp.int32, (rows, 2 * rows), 0)
    query = lax.broadcasted_iota(jnp.int32, (rows, 2 * rows), 1)
    bias[...] = jnp.where((query % SUB == key % SUB) & real(key), 0.0, NEGATIVE)
    lane = lax.broadcasted_iota(jnp.int32, (1, PAIR), 1)
    low_lanes = (lane < DH).astype(jnp.bfloat16)
    high_lanes = (lane >= DH).astype(jnp.bfloat16)

    depth = early_depth(view)
    late_rows = view.rows[len(view.early_rows) :]
    if middle:
        ordered, ga_early, partial = middle
        ga[...] = ga_early[...]
        grad_attended(view, weights, ordered[...], late_rows, ga)
    else:
        ordered = masked_cotangent(view, counts_ref, both_ref, att)
        grad_attended(view, weights, ordered, late_rows, ga)

    for block in range(view.early):
        held = front_ref[:, block * in_columns : (block + 1) * in_columns]
        proj[:, pl.ds(column(block, in_columns), in_columns)] = held
    for block in range(view.early, view.blocks):
        for start, size in chunks(in_columns):
            weight = stack_rows(view, weights, block, (start, size), late_rows)
            value = dot(normed_ref[:, depth:], weight, NN)
            if middle:
                here = pl.ds((block - view.early) * in_columns + start, size)
                value = value + partial[:, here]
            proj[:, pl.ds(column(block, in_columns, start), size)] = value.astype(jnp.bfloat16)

    def apart(block):
        return jnp.concatenate([block * low_lanes, block * high_lanes], axis=0)

    def stacked(block):
        return jnp.concatenate([block[:, :rows], block[:, rows:]], axis=0)

    def lanes(part, pair):
        return pl.ds(pl.multiple_of(part * width + pair * PAIR, PAIR), PAIR)

    chunk = scores.shape[0]
    unroll = min(chunk, 4)

    def each(body):
        @pl.loop(0, chunk // unroll)
        def _(i):
            for inner in range(unroll):
                body(i * unroll + inner)

    for group in range(groups):
        here = pl.ds(group * rows, rows)

        @pl.loop(0, width // (PAIR * chunk))
        def _(part):
            def products(item):
                pair = part * chunk + item
                q_two = apart(proj[here, lanes(0, pair)] * DH ** (-0.5))
                scores[item] = dot(proj[here, lanes(1, pair)], q_two, NT)
                ga_two = apart(ga[here, lanes(0, pair)])
                gprobs[item] = dot(proj[here, lanes(2, pair)], ga_two, NT)

            def softmax(item):
                masked = scores[item] + bias[...]
                expanded = jnp.exp(masked - jnp.max(masked, axis=0, keepdims=True))
                probs = expanded * (1.0 / jnp.sum(expanded, axis=0, keepdims=True))
                low[item, 0] = probs.astype(jnp.bfloat16)
                weighted = probs * gprobs[item]
                delta = jnp.sum(weighted, axis=0, keepdims=True)
                low[item, 1] = (weighted - probs * delta).astype(jnp.bfloat16)

            def results(item):
                pair = part * chunk + item
                probs_low, grad_scores = low[item, 0], low[item, 1]
                q_two = apart(proj[here, lanes(0, pair)] * DH ** (-0.5))
                k_two = apart(proj[here, lanes(1, pair)])
                v_two = apart(proj[here, lanes(2, pair)])
                ga_two = apart(ga[here, lanes(0, pair)])
                att[here, lanes(0, pair)] = dot(stacked(probs_low), v_two, TN).astype(jnp.bfloat16)
                gproj[here, lanes(0, pair)] = (
                    dot(stacked(grad_scores), k_two, TN) * DH ** (-0.5)
                ).astype(jnp.bfloat16)
                gproj[here, lanes(1, pair)] = dot(grad_scores, q_two, NN).astype(jnp.bfloat16)
                gproj[here, lanes(2, pair)] = dot(probs_low, ga_two, NN).astype(jnp.bfloat16)

            each(products)
            each(softmax)
            each(results)

    def store(which, group, value):
        for frame in range(frames):
            out_ref[pl.ds(frame ^ device, 1), which, group * SUB : (group + 1) * SUB, :] = value[
                frame * SUB : (frame + 1) * SUB
            ].reshape(1, SUB, width)

    att_ordered = beside(att, row_starts, row_size)
    for block in range(view.blocks):
        for start, size in chunks(out_columns):
            weight = stack_rows(view, weights, block, (in_columns + start, size))
            wide_sum[:, pl.ds(column(block, out_columns, start), size)] = dot(
                att_ordered, weight, NN
            )

    for group in range(groups):
        here = pl.ds(group * rows, rows)
        wide = load_rows(both_ref, 0, group).astype(jnp.float32)
        store(0, group, (wide + live * wide_sum[here, :]).astype(jnp.bfloat16))

    gproj_ordered = beside(gproj, [column(i, in_columns) for i in range(view.blocks)], in_columns)
    for parts in view.rows:
        weight = stack_columns(view, weights, parts, 0, in_columns)
        put_rows(view, wide_sum, parts, dot(gproj_ordered, weight, NT))

    for group in range(groups):
        here = pl.ds(group * rows, rows)
        grad = wide_sum[here, :] * gain_ref[...]
        scale = stats_ref[here, 1:2]
        hat = (load_rows(both_ref, 0, group).astype(jnp.float32) - stats_ref[here, 0:1]) * scale
        grad_rows = scale * (
            grad
            - jnp.mean(grad, axis=-1, keepdims=True)
            - hat * jnp.mean(grad * hat, axis=-1, keepdims=True)
        )
        cot = load_rows(both_ref, 1, group).astype(jnp.float32)
        store(1, group, (cot + grad_rows).astype(jnp.bfloat16))


def run_front(gain, shape, sources, view):
    frames, _, patches, width = shape
    total = frames * patches
    vmem = pl.BlockSpec(memory_space=pltpu.VMEM)
    return pl.pallas_call(
        functools.partial(front_kernel, view),
        out_shape=(
            jax.ShapeDtypeStruct(shape, jnp.bfloat16),
            jax.ShapeDtypeStruct((total, width), jnp.bfloat16),
            jax.ShapeDtypeStruct((total, 128), jnp.float32),
            jax.ShapeDtypeStruct((total, view.early * view.in_columns), jnp.bfloat16),
        ),
        in_specs=[vmem] * (1 + len(sources)),
        out_specs=(vmem,) * 4,
        scratch_shapes=[pltpu.VMEM((total, width), jnp.bfloat16)],
        compiler_params=pltpu.CompilerParams(vmem_limit_bytes=VMEM_LIMIT),
        cost_estimate=pl.CostEstimate(flops=total, bytes_accessed=total, transcendentals=0),
        name="front",
    )(gain, *sources)


def run_middle(counts, fronted, weights, view):
    both, normed, _, _ = fronted
    total, width = normed.shape
    vmem = pl.BlockSpec(memory_space=pltpu.VMEM)
    columns = (view.blocks - view.early) * view.in_columns
    return pl.pallas_call(
        functools.partial(middle_kernel, view),
        out_shape=(
            jax.ShapeDtypeStruct((total, width), jnp.bfloat16),
            jax.ShapeDtypeStruct((total, width), jnp.bfloat16),
            jax.ShapeDtypeStruct((total, columns), jnp.float32),
        ),
        in_specs=[pl.BlockSpec(memory_space=pltpu.SMEM)] + [vmem] * (2 + len(weights)),
        out_specs=(vmem,) * 3,
        scratch_shapes=[pltpu.VMEM((total, width), jnp.bfloat16)],
        compiler_params=pltpu.CompilerParams(vmem_limit_bytes=VMEM_LIMIT),
        cost_estimate=pl.CostEstimate(flops=total, bytes_accessed=total, transcendentals=0),
        name="middle",
    )(counts, both, normed, *weights)


def run_main(counts, gain, fronted, weights, view):
    both, normed, stats, front = fronted
    frames, _, patches, width = both.shape
    total, rows = frames * patches, frames * SUB
    vmem = pl.BlockSpec(memory_space=pltpu.VMEM)
    smem = pl.BlockSpec(memory_space=pltpu.SMEM)
    chunk = 8 if rows <= 128 else 1
    return pl.pallas_call(
        functools.partial(main_kernel, view),
        out_shape=jax.ShapeDtypeStruct(both.shape, jnp.bfloat16),
        in_specs=[smem] + [vmem] * (5 + len(weights)),
        out_specs=vmem,
        scratch_shapes=[
            pltpu.VMEM((total, 3 * width), jnp.bfloat16),
            pltpu.VMEM((total, width), jnp.bfloat16),
            pltpu.VMEM((total, width), jnp.bfloat16),
            pltpu.VMEM((total, 3 * width), jnp.bfloat16),
            pltpu.VMEM((total, width), jnp.float32),
            pltpu.VMEM((rows, 2 * rows), jnp.float32),
            pltpu.VMEM((chunk, rows, 2 * rows), jnp.float32),
            pltpu.VMEM((chunk, rows, 2 * rows), jnp.float32),
            pltpu.VMEM((chunk, 2, rows, 2 * rows), jnp.bfloat16),
        ],
        compiler_params=pltpu.CompilerParams(
            vmem_limit_bytes=VMEM_LIMIT if rows <= 128 else 2 * VMEM_LIMIT
        ),
        cost_estimate=pl.CostEstimate(
            flops=12 * total * width * width,
            bytes_accessed=8 * width * width + 8 * total * width,
            transcendentals=total * 2048,
        ),
        name="main",
    )(counts, gain, both, normed, stats, front, *weights)


class View:
    def __init__(self, blocks, early, rows, early_rows, in_columns, out_columns, piece, tokens, device, row_order, block_order):
        self.blocks, self.early = blocks, early
        self.rows, self.early_rows = rows, early_rows
        self.in_columns, self.out_columns = in_columns, out_columns
        self.piece, self.tokens, self.device = piece, tokens, device
        self.row_order, self.block_order = row_order, block_order


def swap(array, distance, devices):
    return lax.ppermute(array, "frame", [(f, f ^ distance) for f in range(devices)])


def join_kernel(axis, *refs):
    *sources, target = refs
    start = 0
    for source in sources:
        end = start + source.shape[axis]
        if axis == 0:
            target[start:end, :] = source[...]
        else:
            target[:, start:end] = source[...]
        start = end


def join(axis, *arrays):
    shape = list(arrays[0].shape)
    shape[axis] = sum(array.shape[axis] for array in arrays)
    vmem = pl.BlockSpec(memory_space=pltpu.VMEM)
    return pl.pallas_call(
        functools.partial(join_kernel, axis),
        out_shape=jax.ShapeDtypeStruct(shape, arrays[0].dtype),
        in_specs=[vmem] * len(arrays),
        out_specs=vmem,
        compiler_params=SMALL,
        name="join",
    )(*arrays)


def pack_kernel(patches, share, *refs):
    sources, (joined, own, mine, to_x, to_y), held, fetched, sems = (
        refs[:4], refs[4:9], refs[9], refs[10:14], refs[14]
    )
    copies = [
        pltpu.make_async_copy(source, target, sems.at[i])
        for i, (source, target) in enumerate(zip(sources, fetched))
    ]
    for copy in copies:
        copy.start()
    w_in, w_out, tokens, cot = fetched
    depth = w_in.shape[0]
    half, block = depth // 2, 2 * share
    device = lax.axis_index("frame")
    chip, core = device // 2, device % 2
    full = patches // SUB * SUB
    held[:, full:] = jnp.zeros((2, held.shape[1] - full, held.shape[2]), held.dtype)
    wait(copies)
    joined[:, : w_in.shape[1]] = w_in[...]
    joined[:, w_in.shape[1] :] = w_out[...]
    held[0, :patches] = tokens[0, 0]
    held[1, :patches] = cot[0, 0]

    def put(target, row, owner):
        rows = pl.ds(pl.multiple_of(owner * share, share), share)
        target[row : row + share, :] = held[0, rows, :]
        target[row + share : row + block, :] = held[1, rows, :]

    put(mine, 0, device)
    own[:depth, :] = joined[...]
    put(own, depth, device ^ 1)
    for target, first, last, away, core_by in ((to_x, 0, half, 1, 0), (to_y, half, 0, 2, 1)):
        target[:half, :] = joined[first : first + half, :]
        put(target, half, (chip ^ away) * 2)
        put(target, half + block, (chip ^ away) * 2 + 1)
        target[half + 2 * block : depth + 2 * block, :] = joined[last : last + half, :]
        put(target, depth + 2 * block, (chip ^ 3) * 2 + core_by)


def turn_kernel(half, by_x, by_y, pair_x, pair_y, to_dx, to_dy):
    to_dx[:half, :] = by_y[:half, :]
    to_dx[half:, :] = pair_y[: 2 * half, :]
    to_dy[:half, :] = by_x[half:, :]
    to_dy[half:, :] = pair_x[2 * half :, :]


def gather_in_rounds(
    counts, input_weights, output_weights, tokens, cotangent, gain, share, devices
):
    depth, in_columns = input_weights.shape
    out_columns = output_weights.shape[1]
    _, _, patches, width = tokens.shape
    half, block = depth // 2, 2 * share
    vmem = pl.BlockSpec(memory_space=pltpu.VMEM)

    def rows_of(count):
        return jax.ShapeDtypeStruct((count, width), jnp.bfloat16)

    joined, own, mine, to_x, to_y = pl.pallas_call(
        functools.partial(pack_kernel, patches, share),
        out_shape=tuple(
            map(rows_of, (depth, depth + block, block, depth + 3 * block, depth + 3 * block))
        ),
        in_specs=[pl.BlockSpec(memory_space=pltpu.HBM)] * 4,
        out_specs=(vmem,) * 5,
        scratch_shapes=[pltpu.VMEM((2, devices * share, width), jnp.bfloat16)]
        + [pltpu.VMEM(a.shape, a.dtype) for a in (input_weights, output_weights, tokens, cotangent)]
        + [pltpu.SemaphoreType.DMA((4,))],
        compiler_params=pltpu.CompilerParams(vmem_limit_bytes=PACK_LIMIT),
        name="pack",
    )(input_weights, output_weights, tokens, cotangent)

    def by_clip(array, offset):
        return lax.ppermute(array, "clip", [(c, c ^ offset) for c in range(4)])

    def across(array):
        return [swap(array, 2, devices), swap(array, 4, devices)]

    def other_core(arrays):
        return [swap(array, 1, devices) for array in arrays]

    one, two, three = by_clip(joined, 1), by_clip(joined, 2), by_clip(joined, 3)
    first = [swap(to_x, 2, devices), swap(to_y, 4, devices)]
    tail = half + 2 * block
    first += [swap(first[1][tail:], 2, devices), swap(first[0][tail:], 4, devices)]
    one, first[0], first[1] = lax.optimization_barrier((one, first[0], first[1]))
    second = [one, *across(one)]
    two, three, first[2], first[3] = lax.optimization_barrier((two, three, first[2], first[3]))
    third = [join(0, two, three)]
    second[1], second[2], own, *first = lax.optimization_barrier(
        (second[1], second[2], own, *first)
    )
    first_other = other_core([own, *first])
    ready = [joined, *first, *first_other]
    third += across(third[0])

    def tokens_in(sources, both_ref):
        core = lax.axis_index("frame") % 2
        mine_ref, _, x_ref, y_ref, dx_ref, dy_ref, own2, x2, y2, dx2, dy2 = sources[:11]
        rows = pl.ds(pl.multiple_of(half + core * block, block), block)
        behind = slice(half, half + block)

        def diagonal(by_x, by_y):
            return jnp.where(core == 0, by_y[behind, :], by_x[behind, :])

        found = (
            mine_ref[...], own2[depth : depth + block, :],
            x_ref[rows, :], x2[rows, :], y_ref[rows, :], y2[rows, :],
            diagonal(dx_ref, dy_ref), diagonal(dx2, dy2),
        )
        for distance, value in enumerate(found):
            both_ref[distance] = value.reshape(2, share, width)

    table = [
        [(0, 0, 0, depth, 0)],
        [(0, 2, 0, half, 0), (0, 2, tail, half, half)],
        [(0, 4, 0, half, half), (0, 4, tail, half, 0)],
        [(0, 6, 0, half, 0)],
        [(0, 6, 0, half, half)],
    ]
    others = [[(1, d, 0, depth, 0)] for d in (0, 2, 4)]
    pairs = [[(2, d, 0, depth, 0), (3, d, depth, depth, 0)] for d in (0, 2, 4)]
    pairs += [
        [(1, 6, 0, half, 0), (2, 6, half, depth, 0)],
        [(1, 6, 0, half, half), (3, 6, half, depth, 0)],
    ]
    beyond = [[(1, d, d // 2 * depth, depth, 0) for d in (0, 2, 4)]]
    arrays = []
    for groups in ((table, table), (others, beyond), (pairs, pairs)):
        arrays += [(core, parts) for core in (0, 1) for parts in groups[core]]

    def piece(present):
        def value(refs, offset, distance, first, depth, lanes):
            found = [
                (inside, refs[present.index(ref)][start : start + size, lanes[0] : lanes[0] + lanes[1]])
                for ref, (core, parts) in enumerate(arrays)
                for source, away, start, size, inside in parts
                if (source, away ^ core) == (offset, distance)
            ]
            return jnp.concatenate([held for _, held in sorted(found, key=lambda f: f[0])], axis=0)

        return value

    row_groups = [[(d, 0, depth), (d + 1, 0, depth)] for d in range(0, devices, 2)]

    def view(present):
        return View(
            4,
            1,
            row_groups,
            row_groups[:3],
            in_columns,
            out_columns,
            piece(present),
            tokens_in,
            lambda: lax.axis_index("frame"),
            lambda: ([(lax.axis_index("frame") ^ d) * depth for d in range(devices)], depth),
            lambda: [lax.axis_index("clip") ^ offset for offset in range(4)],
        )

    fronted = run_front(
        gain, (devices, 2, share, width), [mine, *ready[:10]], view([None, *range(10)])
    )
    to_dx, to_dy = pl.pallas_call(
        functools.partial(turn_kernel, half),
        out_shape=(rows_of(depth + half), rows_of(depth + half)),
        in_specs=[vmem] * 4,
        out_specs=(vmem, vmem),
        compiler_params=SMALL,
        name="turn",
    )(second[1], second[2], third[1], third[2])
    third += [swap(to_dx, 2, devices), swap(to_dy, 4, devices)]
    late, fronted = lax.optimization_barrier((second, list(fronted)))
    third_other = other_core(third)
    ready += [*second, swap(join(0, *late), 1, devices)]
    middle = run_middle(
        counts,
        fronted,
        [*ready, *third[:3], *third_other[:3]],
        view([*range(14), 14, 15, 16, 19, 20, 21]),
    )
    weights = [*middle, *ready, *third, *third_other]
    return fronted, weights, view(list(range(24)))


def gather_plainly(
    counts, input_weights, output_weights, tokens, cotangent, gain, share, devices
):
    _, slots, patches, width = tokens.shape
    whole = []
    for weights in (input_weights, output_weights):
        columns = lax.all_gather(weights, "clip", axis=1, tiled=True)
        whole.append(lax.all_gather(columns, "frame", axis=0, tiled=True))

    def by_destination(source):
        padded = jnp.pad(source[0], ((0, 0), (0, devices * share - patches), (0, 0)))
        return padded.reshape(slots, devices, share, width).transpose(1, 0, 2, 3)

    both = jnp.stack([by_destination(tokens), by_destination(cotangent)], axis=2)
    both = lax.all_to_all(both, "frame", split_axis=0, concat_axis=0, tiled=True)
    both = both.reshape(devices * slots, 2, share, width)

    def tokens_in(sources, both_ref):
        both_ref[...] = sources[2][...]

    in_columns, out_columns = whole[0].shape[1], whole[1].shape[1]

    def piece(refs, block, index, first, depth, lanes):
        outer = lanes[0] >= in_columns
        start = lanes[0] - in_columns * outer
        return refs[int(outer)][first : first + depth, start : start + lanes[1]]

    step = math.gcd(width, 256)
    view = View(
        1,
        1,
        [[(0, first, step)] for first in range(0, width, step)],
        [],
        in_columns,
        out_columns,
        piece,
        tokens_in,
        lambda: 0,
        lambda: ([0], width),
        lambda: [0],
    )
    return run_front(gain, both.shape, [*whole, both], view), whole, view


def per_device(clips, devices, tokens, counts, norm_gain, input_weights, output_weights, cotangent):
    _, slots, patches, width = tokens.shape
    share = -(-patches // devices)
    share = -(-share // SUB) * SUB
    depth, in_columns = input_weights.shape
    fits = in_columns % 128 == 0 and output_weights.shape[1] % 128 == 0 and depth % 32 == 0
    small = clips == 4 and devices == 8 and slots == 1 and fits
    gather = gather_in_rounds if small else gather_plainly
    gain = norm_gain.reshape(1, width)
    fronted, weights, view = gather(
        counts, input_weights, output_weights, tokens, cotangent, gain, share, devices
    )
    back = run_main(counts, gain, fronted, weights, view)
    back = back.reshape(devices, slots, 2, share, width)
    back = lax.all_to_all(back, "frame", split_axis=0, concat_axis=0, tiled=True)

    def in_order(which):
        rows = back[:, :, which].transpose(1, 0, 2, 3).reshape(slots, devices * share, width)
        return rows[None, :, :patches]

    return in_order(0), in_order(1)


def solution(mesh):
    in_specs = (
        P("clip", "frame", None, None),
        P("clip"),
        P(),
        P("frame", "clip"),
        P("frame", "clip"),
        P("clip", "frame", None, None),
    )
    out_specs = (P("clip", "frame", None, None), P("clip", "frame", None, None))
    body = functools.partial(per_device, mesh.shape["clip"], mesh.shape["frame"])
    return jax.shard_map(body, mesh=mesh, in_specs=in_specs, out_specs=out_specs, check_vma=False)
```

```python
import functools
import math

import jax
import jax.numpy as jnp
from jax import lax
from jax.experimental import pallas as pl
from jax.experimental.pallas import tpu as pltpu
from jax.sharding import PartitionSpec as P

DH = 64
PAIR = 2 * DH
SUB = 16
EPSILON = 1e-06
NEGATIVE = -1e30
NN = (((1,), (0,)), ((), ()))
NT = (((1,), (1,)), ((), ()))
TN = (((0,), (0,)), ((), ()))
VMEM_LIMIT = 27 * 1024 * 1024
PACK_LIMIT = 58 * 1024 * 1024
SMALL = pltpu.CompilerParams(vmem_limit_bytes=6 * 1024 * 1024)


def dot(a, b, dims):
    return lax.dot_general(a, b, dims, preferred_element_type=jnp.float32)


def wait(copies):
    for copy in copies:
        copy.wait()


def load_rows(ref, which, group):
    frames, _, _, width = ref.shape
    return ref[:, which, group * SUB : (group + 1) * SUB, :].reshape(frames * SUB, width)


def beside(ref, starts, size):
    return jnp.concatenate(
        [ref[:, pl.ds(pl.multiple_of(start, 128), size)] for start in starts], axis=1
    )


def chunks(columns):
    step = math.gcd(columns, 256)
    return [(start, step) for start in range(0, columns, step)]


def stack_rows(view, refs, block, lanes):
    return jnp.concatenate(
        [view.piece(refs, block, *part, lanes) for parts in view.rows for part in parts], axis=0
    )


def stack_columns(view, refs, parts, start, size):
    return jnp.concatenate(
        [
            jnp.concatenate(
                [view.piece(refs, block, *part, (start, size)) for part in parts], axis=0
            )
            for block in range(view.blocks)
        ],
        axis=1,
    )


def front_kernel(view, gain_ref, *refs):
    sources = refs[:-5]
    both_ref, normed_ref, stats_ref, proj_ref, natural = refs[-5:]
    view.tokens(sources, both_ref)
    frames, _, patches, _ = both_ref.shape
    rows = frames * SUB
    for group in range(patches // SUB):
        here = pl.ds(group * rows, rows)
        wide = load_rows(both_ref, 0, group).astype(jnp.float32)
        average = jnp.mean(wide, axis=-1, keepdims=True)
        centred = wide - average
        variance = jnp.mean(centred * centred, axis=-1, keepdims=True)
        scale = lax.rsqrt(variance + EPSILON)
        natural[here, :] = (centred * scale * gain_ref[...]).astype(jnp.bfloat16)
        stats_ref[here, 0:1] = average
        stats_ref[here, 1:2] = scale
    normed_ref[...] = beside(natural, *view.row_order())
    for start, size in chunks(proj_ref.shape[1]):
        weight = stack_rows(view, sources, 0, (start, size))
        proj_ref[:, start : start + size] = dot(normed_ref[...], weight, NN).astype(jnp.bfloat16)


def main_kernel(view, counts_ref, gain_ref, both_ref, normed_ref, stats_ref, front_ref, *rest):
    weights = rest[:-11]
    out_ref, grads, proj, ga, att, gproj, wide_sum, bias, scores, gprobs, low = rest[-11:]
    frames, _, patches, width = both_ref.shape
    groups = patches // SUB
    rows = frames * SUB
    count = counts_ref[0]
    device = view.device()
    in_columns, out_columns = view.in_columns, view.out_columns
    row_starts, row_size = view.row_order()
    block_order = view.block_order()

    def column(block, stride, start=0):
        return pl.multiple_of(block_order[block] * stride + start, 128)

    def put_rows(target, parts, value):
        done = 0
        for index, first, depth in parts:
            start = pl.multiple_of(row_starts[index] + first, 128)
            target[:, pl.ds(start, depth)] = value[:, done : done + depth]
            done += depth

    def real(index):
        return ((index // SUB) ^ device) < count

    live = real(lax.broadcasted_iota(jnp.int32, (rows, 1), 0)).astype(jnp.float32)
    for group in range(groups):
        here = pl.ds(group * rows, rows)
        grads[here, :] = (load_rows(both_ref, 1, group).astype(jnp.float32) * live).astype(
            jnp.bfloat16
        )
    key = lax.broadcasted_iota(jnp.int32, (rows, 2 * rows), 0)
    query = lax.broadcasted_iota(jnp.int32, (rows, 2 * rows), 1)
    bias[...] = jnp.where((query % SUB == key % SUB) & real(key), 0.0, NEGATIVE)
    lane = lax.broadcasted_iota(jnp.int32, (1, PAIR), 1)
    low_lanes = (lane < DH).astype(jnp.bfloat16)
    high_lanes = (lane >= DH).astype(jnp.bfloat16)

    grads_ordered = beside(grads, [column(i, out_columns) for i in range(view.blocks)], out_columns)
    for parts in view.rows:
        weight = stack_columns(view, weights, parts, in_columns, out_columns)
        put_rows(ga, parts, dot(grads_ordered, weight, NT).astype(jnp.bfloat16))

    proj[:, pl.ds(column(0, in_columns), in_columns)] = front_ref[...]
    for block in range(1, view.blocks):
        for start, size in chunks(in_columns):
            weight = stack_rows(view, weights, block, (start, size))
            proj[:, pl.ds(column(block, in_columns, start), size)] = dot(
                normed_ref[...], weight, NN
            ).astype(jnp.bfloat16)

    def apart(block):
        return jnp.concatenate([block * low_lanes, block * high_lanes], axis=0)

    def stacked(block):
        return jnp.concatenate([block[:, :rows], block[:, rows:]], axis=0)

    def lanes(part, pair):
        return pl.ds(pl.multiple_of(part * width + pair * PAIR, PAIR), PAIR)

    chunk = scores.shape[0]
    unroll = min(chunk, 8)

    def each(body):
        @pl.loop(0, chunk // unroll)
        def _(i):
            for inner in range(unroll):
                body(i * unroll + inner)

    for group in range(groups):
        here = pl.ds(group * rows, rows)

        @pl.loop(0, width // (PAIR * chunk))
        def _(part):
            def products(item):
                pair = part * chunk + item
                q_two = apart(proj[here, lanes(0, pair)] * DH ** (-0.5))
                scores[item] = dot(proj[here, lanes(1, pair)], q_two, NT)
                ga_two = apart(ga[here, lanes(0, pair)])
                gprobs[item] = dot(proj[here, lanes(2, pair)], ga_two, NT)

            def softmax(item):
                masked = scores[item] + bias[...]
                expanded = jnp.exp(masked - jnp.max(masked, axis=0, keepdims=True))
                probs = expanded * (1.0 / jnp.sum(expanded, axis=0, keepdims=True))
                low[item, 0] = probs.astype(jnp.bfloat16)
                weighted = probs * gprobs[item]
                delta = jnp.sum(weighted, axis=0, keepdims=True)
                low[item, 1] = (weighted - probs * delta).astype(jnp.bfloat16)

            def results(item):
                pair = part * chunk + item
                probs_low, grad_scores = low[item, 0], low[item, 1]
                q_two = apart(proj[here, lanes(0, pair)] * DH ** (-0.5))
                k_two = apart(proj[here, lanes(1, pair)])
                v_two = apart(proj[here, lanes(2, pair)])
                ga_two = apart(ga[here, lanes(0, pair)])
                att[here, lanes(0, pair)] = dot(stacked(probs_low), v_two, TN).astype(jnp.bfloat16)
                gproj[here, lanes(0, pair)] = (
                    dot(stacked(grad_scores), k_two, TN) * DH ** (-0.5)
                ).astype(jnp.bfloat16)
                gproj[here, lanes(1, pair)] = dot(grad_scores, q_two, NN).astype(jnp.bfloat16)
                gproj[here, lanes(2, pair)] = dot(probs_low, ga_two, NN).astype(jnp.bfloat16)

            each(products)
            each(softmax)
            each(results)

    def store(which, group, value):
        for frame in range(frames):
            out_ref[pl.ds(frame ^ device, 1), which, group * SUB : (group + 1) * SUB, :] = value[
                frame * SUB : (frame + 1) * SUB
            ].reshape(1, SUB, width)

    att_ordered = beside(att, row_starts, row_size)
    for block in range(view.blocks):
        for start, size in chunks(out_columns):
            weight = stack_rows(view, weights, block, (in_columns + start, size))
            wide_sum[:, pl.ds(column(block, out_columns, start), size)] = dot(
                att_ordered, weight, NN
            )

    for group in range(groups):
        here = pl.ds(group * rows, rows)
        wide = load_rows(both_ref, 0, group).astype(jnp.float32)
        store(0, group, (wide + live * wide_sum[here, :]).astype(jnp.bfloat16))

    gproj_ordered = beside(gproj, [column(i, in_columns) for i in range(view.blocks)], in_columns)
    for parts in view.rows:
        weight = stack_columns(view, weights, parts, 0, in_columns)
        put_rows(wide_sum, parts, dot(gproj_ordered, weight, NT))

    for group in range(groups):
        here = pl.ds(group * rows, rows)
        grad = wide_sum[here, :] * gain_ref[...]
        scale = stats_ref[here, 1:2]
        hat = (load_rows(both_ref, 0, group).astype(jnp.float32) - stats_ref[here, 0:1]) * scale
        grad_rows = scale * (
            grad
            - jnp.mean(grad, axis=-1, keepdims=True)
            - hat * jnp.mean(grad * hat, axis=-1, keepdims=True)
        )
        cot = load_rows(both_ref, 1, group).astype(jnp.float32)
        store(1, group, (cot + grad_rows).astype(jnp.bfloat16))


def run_front(gain, shape, sources, view):
    frames, _, patches, width = shape
    total = frames * patches
    vmem = pl.BlockSpec(memory_space=pltpu.VMEM)
    return pl.pallas_call(
        functools.partial(front_kernel, view),
        out_shape=(
            jax.ShapeDtypeStruct(shape, jnp.bfloat16),
            jax.ShapeDtypeStruct((total, width), jnp.bfloat16),
            jax.ShapeDtypeStruct((total, 128), jnp.float32),
            jax.ShapeDtypeStruct((total, view.in_columns), jnp.bfloat16),
        ),
        in_specs=[vmem] * (1 + len(sources)),
        out_specs=(vmem,) * 4,
        scratch_shapes=[pltpu.VMEM((total, width), jnp.bfloat16)],
        compiler_params=pltpu.CompilerParams(vmem_limit_bytes=VMEM_LIMIT),
        cost_estimate=pl.CostEstimate(flops=total, bytes_accessed=total, transcendentals=0),
        name="front",
    )(gain, *sources)


def run_main(counts, gain, fronted, weights, view):
    both, normed, stats, front = fronted
    frames, _, patches, width = both.shape
    total, rows = frames * patches, frames * SUB
    vmem = pl.BlockSpec(memory_space=pltpu.VMEM)
    smem = pl.BlockSpec(memory_space=pltpu.SMEM)
    chunk = 8 if rows <= 128 else 1
    return pl.pallas_call(
        functools.partial(main_kernel, view),
        out_shape=jax.ShapeDtypeStruct(both.shape, jnp.bfloat16),
        in_specs=[smem] + [vmem] * (5 + len(weights)),
        out_specs=vmem,
        scratch_shapes=[
            pltpu.VMEM((total, width), jnp.bfloat16),
            pltpu.VMEM((total, 3 * width), jnp.bfloat16),
            pltpu.VMEM((total, width), jnp.bfloat16),
            pltpu.VMEM((total, width), jnp.bfloat16),
            pltpu.VMEM((total, 3 * width), jnp.bfloat16),
            pltpu.VMEM((total, width), jnp.float32),
            pltpu.VMEM((rows, 2 * rows), jnp.float32),
            pltpu.VMEM((chunk, rows, 2 * rows), jnp.float32),
            pltpu.VMEM((chunk, rows, 2 * rows), jnp.float32),
            pltpu.VMEM((chunk, 2, rows, 2 * rows), jnp.bfloat16),
        ],
        compiler_params=pltpu.CompilerParams(
            vmem_limit_bytes=VMEM_LIMIT if rows <= 128 else 2 * VMEM_LIMIT
        ),
        cost_estimate=pl.CostEstimate(
            flops=12 * total * width * width,
            bytes_accessed=8 * width * width + 8 * total * width,
            transcendentals=total * 2048,
        ),
        name="main",
    )(counts, gain, both, normed, stats, front, *weights)


class View:
    def __init__(self, blocks, rows, in_columns, out_columns, piece, tokens, device, row_order, block_order):
        self.blocks, self.rows = blocks, rows
        self.in_columns, self.out_columns = in_columns, out_columns
        self.piece, self.tokens, self.device = piece, tokens, device
        self.row_order, self.block_order = row_order, block_order


def swap(array, distance, devices):
    return lax.ppermute(array, "frame", [(f, f ^ distance) for f in range(devices)])


def join_kernel(axis, *refs):
    *sources, target = refs
    start = 0
    for source in sources:
        end = start + source.shape[axis]
        if axis == 0:
            target[start:end, :] = source[...]
        else:
            target[:, start:end] = source[...]
        start = end


def join(axis, *arrays):
    shape = list(arrays[0].shape)
    shape[axis] = sum(array.shape[axis] for array in arrays)
    vmem = pl.BlockSpec(memory_space=pltpu.VMEM)
    return pl.pallas_call(
        functools.partial(join_kernel, axis),
        out_shape=jax.ShapeDtypeStruct(shape, arrays[0].dtype),
        in_specs=[vmem] * len(arrays),
        out_specs=vmem,
        compiler_params=SMALL,
        name="join",
    )(*arrays)


def pack_kernel(patches, share, *refs):
    sources, (joined, own, mine, to_x, to_y), held, fetched, sems = (
        refs[:4], refs[4:9], refs[9], refs[10:14], refs[14]
    )
    copies = [
        pltpu.make_async_copy(source, target, sems.at[i])
        for i, (source, target) in enumerate(zip(sources, fetched))
    ]
    for copy in copies:
        copy.start()
    w_in, w_out, tokens, cot = fetched
    depth = w_in.shape[0]
    half, block = depth // 2, 2 * share
    device = lax.axis_index("frame")
    chip, core = device // 2, device % 2
    full = patches // SUB * SUB
    held[:, full:] = jnp.zeros((2, held.shape[1] - full, held.shape[2]), held.dtype)
    wait(copies)
    joined[:, : w_in.shape[1]] = w_in[...]
    joined[:, w_in.shape[1] :] = w_out[...]
    held[0, :patches] = tokens[0, 0]
    held[1, :patches] = cot[0, 0]

    def put(target, row, owner):
        rows = pl.ds(pl.multiple_of(owner * share, share), share)
        target[row : row + share, :] = held[0, rows, :]
        target[row + share : row + block, :] = held[1, rows, :]

    put(mine, 0, device)
    own[:depth, :] = joined[...]
    put(own, depth, device ^ 1)
    for target, first, last, away, core_by in ((to_x, 0, half, 1, 0), (to_y, half, 0, 2, 1)):
        target[:half, :] = joined[first : first + half, :]
        put(target, half, (chip ^ away) * 2)
        put(target, half + block, (chip ^ away) * 2 + 1)
        target[half + 2 * block : depth + 2 * block, :] = joined[last : last + half, :]
        put(target, depth + 2 * block, (chip ^ 3) * 2 + core_by)


def turn_kernel(half, by_x, by_y, pair_x, pair_y, to_dx, to_dy):
    to_dx[:half, :] = by_y[:half, :]
    to_dx[half:, :] = pair_y[: 2 * half, :]
    to_dy[:half, :] = by_x[half:, :]
    to_dy[half:, :] = pair_x[2 * half :, :]


def gather_in_rounds(input_weights, output_weights, tokens, cotangent, gain, share, devices):
    depth, in_columns = input_weights.shape
    out_columns = output_weights.shape[1]
    _, _, patches, width = tokens.shape
    half, block = depth // 2, 2 * share
    vmem = pl.BlockSpec(memory_space=pltpu.VMEM)

    def rows_of(count):
        return jax.ShapeDtypeStruct((count, width), jnp.bfloat16)

    joined, own, mine, to_x, to_y = pl.pallas_call(
        functools.partial(pack_kernel, patches, share),
        out_shape=tuple(
            map(rows_of, (depth, depth + block, block, depth + 3 * block, depth + 3 * block))
        ),
        in_specs=[pl.BlockSpec(memory_space=pltpu.HBM)] * 4,
        out_specs=(vmem,) * 5,
        scratch_shapes=[pltpu.VMEM((2, devices * share, width), jnp.bfloat16)]
        + [pltpu.VMEM(a.shape, a.dtype) for a in (input_weights, output_weights, tokens, cotangent)]
        + [pltpu.SemaphoreType.DMA((4,))],
        compiler_params=pltpu.CompilerParams(vmem_limit_bytes=PACK_LIMIT),
        name="pack",
    )(input_weights, output_weights, tokens, cotangent)

    def by_clip(array, offset):
        return lax.ppermute(array, "clip", [(c, c ^ offset) for c in range(4)])

    def across(array):
        return [swap(array, 2, devices), swap(array, 4, devices)]

    def other_core(arrays):
        return [swap(array, 1, devices) for array in arrays]

    one, two, three = by_clip(joined, 1), by_clip(joined, 2), by_clip(joined, 3)
    first = [swap(to_x, 2, devices), swap(to_y, 4, devices)]
    tail = half + 2 * block
    first += [swap(first[1][tail:], 2, devices), swap(first[0][tail:], 4, devices)]
    one, first[0], first[1] = lax.optimization_barrier((one, first[0], first[1]))
    second = [one, *across(one)]
    two, three, first[2], first[3] = lax.optimization_barrier((two, three, first[2], first[3]))
    third = [join(0, two, three)]
    second[1], second[2], own, *first = lax.optimization_barrier(
        (second[1], second[2], own, *first)
    )
    first_other = other_core([own, *first])
    second_other = other_core(second)
    ready = [joined, *first, *first_other, *second, *second_other]
    third += across(third[0])

    def tokens_in(sources, both_ref):
        core = lax.axis_index("frame") % 2
        mine_ref, _, x_ref, y_ref, dx_ref, dy_ref, own2, x2, y2, dx2, dy2 = sources[:11]
        rows = pl.ds(pl.multiple_of(half + core * block, block), block)
        behind = slice(half, half + block)

        def diagonal(by_x, by_y):
            return jnp.where(core == 0, by_y[behind, :], by_x[behind, :])

        found = (
            mine_ref[...], own2[depth : depth + block, :],
            x_ref[rows, :], x2[rows, :], y_ref[rows, :], y2[rows, :],
            diagonal(dx_ref, dy_ref), diagonal(dx2, dy2),
        )
        for distance, value in enumerate(found):
            both_ref[distance] = value.reshape(2, share, width)

    table = [
        [(0, 0, 0, depth, 0)],
        [(0, 2, 0, half, 0), (0, 2, tail, half, half)],
        [(0, 4, 0, half, half), (0, 4, tail, half, 0)],
        [(0, 6, 0, half, 0)],
        [(0, 6, 0, half, half)],
    ]
    others = [[(1, d, 0, depth, 0)] for d in (0, 2, 4)]
    pairs = [[(2, d, 0, depth, 0), (3, d, depth, depth, 0)] for d in (0, 2, 4)]
    pairs += [
        [(1, 6, 0, half, 0), (2, 6, half, depth, 0)],
        [(1, 6, 0, half, half), (3, 6, half, depth, 0)],
    ]
    arrays = []
    for group in (table, others, pairs):
        arrays += [(core, parts) for core in (0, 1) for parts in group]

    def piece(base):
        def value(refs, offset, distance, first, depth, lanes):
            found = [
                (inside, refs[base + ref][start : start + size, lanes[0] : lanes[0] + lanes[1]])
                for ref, (core, parts) in enumerate(arrays)
                for source, away, start, size, inside in parts
                if (source, away ^ core) == (offset, distance)
            ]
            return jnp.concatenate([held for _, held in sorted(found, key=lambda f: f[0])], axis=0)

        return value

    def view(base):
        return View(
            4,
            [[(d, 0, depth), (d + 1, 0, depth)] for d in range(0, devices, 2)],
            in_columns,
            out_columns,
            piece(base),
            tokens_in,
            lambda: lax.axis_index("frame"),
            lambda: ([(lax.axis_index("frame") ^ d) * depth for d in range(devices)], depth),
            lambda: [lax.axis_index("clip") ^ offset for offset in range(4)],
        )

    fronted = run_front(gain, (devices, 2, share, width), [mine, *ready[:10]], view(1))
    to_dx, to_dy = pl.pallas_call(
        functools.partial(turn_kernel, half),
        out_shape=(rows_of(depth + half), rows_of(depth + half)),
        in_specs=[vmem] * 4,
        out_specs=(vmem, vmem),
        compiler_params=SMALL,
        name="turn",
    )(second[1], second[2], third[1], third[2])
    third += [swap(to_dx, 2, devices), swap(to_dy, 4, devices)]
    third[3], *fronted = lax.optimization_barrier((third[3], *fronted))
    third += other_core(third)
    return fronted, [*ready, *third], view(0)


def gather_plainly(input_weights, output_weights, tokens, cotangent, gain, share, devices):
    _, slots, patches, width = tokens.shape
    whole = []
    for weights in (input_weights, output_weights):
        columns = lax.all_gather(weights, "clip", axis=1, tiled=True)
        whole.append(lax.all_gather(columns, "frame", axis=0, tiled=True))

    def by_destination(source):
        padded = jnp.pad(source[0], ((0, 0), (0, devices * share - patches), (0, 0)))
        return padded.reshape(slots, devices, share, width).transpose(1, 0, 2, 3)

    both = jnp.stack([by_destination(tokens), by_destination(cotangent)], axis=2)
    both = lax.all_to_all(both, "frame", split_axis=0, concat_axis=0, tiled=True)
    both = both.reshape(devices * slots, 2, share, width)

    def tokens_in(sources, both_ref):
        both_ref[...] = sources[2][...]

    in_columns, out_columns = whole[0].shape[1], whole[1].shape[1]

    def piece(refs, block, index, first, depth, lanes):
        outer = lanes[0] >= in_columns
        start = lanes[0] - in_columns * outer
        return refs[int(outer)][first : first + depth, start : start + lanes[1]]

    step = math.gcd(width, 256)
    view = View(
        1,
        [[(0, first, step)] for first in range(0, width, step)],
        in_columns,
        out_columns,
        piece,
        tokens_in,
        lambda: 0,
        lambda: ([0], width),
        lambda: [0],
    )
    return run_front(gain, both.shape, [*whole, both], view), whole, view


def per_device(clips, devices, tokens, counts, norm_gain, input_weights, output_weights, cotangent):
    _, slots, patches, width = tokens.shape
    share = -(-patches // devices)
    share = -(-share // SUB) * SUB
    depth, in_columns = input_weights.shape
    fits = in_columns % 128 == 0 and output_weights.shape[1] % 128 == 0 and depth % 32 == 0
    small = clips == 4 and devices == 8 and slots == 1 and fits
    gather = gather_in_rounds if small else gather_plainly
    gain = norm_gain.reshape(1, width)
    fronted, weights, view = gather(
        input_weights, output_weights, tokens, cotangent, gain, share, devices
    )
    back = run_main(counts, gain, fronted, weights, view)
    back = back.reshape(devices, slots, 2, share, width)
    back = lax.all_to_all(back, "frame", split_axis=0, concat_axis=0, tiled=True)

    def in_order(which):
        rows = back[:, :, which].transpose(1, 0, 2, 3).reshape(slots, devices * share, width)
        return rows[None, :, :patches]

    return in_order(0), in_order(1)


def solution(mesh):
    in_specs = (
        P("clip", "frame", None, None),
        P("clip"),
        P(),
        P("frame", "clip"),
        P("frame", "clip"),
        P("clip", "frame", None, None),
    )
    out_specs = (P("clip", "frame", None, None), P("clip", "frame", None, None))
    body = functools.partial(per_device, mesh.shape["clip"], mesh.shape["frame"])
    return jax.shard_map(body, mesh=mesh, in_specs=in_specs, out_specs=out_specs, check_vma=False)
```
